32 devices in a mesh: batch: 8 (over z, y), win: 4 (over x, core).
Axes of the slice: x: 2, y: 2, z: 4, core: 2. Of those that a mesh axis runs over, the one named last changes fastest.
Arguments:
- frames: bfloat16 [8, 2, 4, 16, 64, 512], P('batch', None, 'win'), may hold values from -6 to 6
- space_gain: float32 [512], replicated, may hold values from 0.1 to 1.9
- space_offset: float32 [512], replicated, may hold values from -3 to 3
- space_entry: bfloat16 [512, 1536], replicated, may hold values from -0.25 to 0.25
- space_exit: bfloat16 [512, 512], replicated, may hold values from -0.75 to 0.75
- space_bias: float32 [512], replicated, may hold values from -1.75 to 1.75
- space_weigh: float32 [512], replicated, may hold values from 0.1 to 1.9
- space_shift: float32 [512], replicated, may hold values from -3 to 3
- space_widen: bfloat16 [512, 2048], replicated, may hold values from -0.25 to 0.25
- space_lift: float32 [2048], replicated, may hold values from -3 to 3
- space_narrow: bfloat16 [2048, 512], replicated, may hold values from -0.125 to 0.125
- space_nudge: float32 [512], replicated, may hold values from -1.75 to 1.75
- time_gain: float32 [512], replicated, may hold values from 0.1 to 1.9
- time_offset: float32 [512], replicated, may hold values from -3 to 3
- time_entry: bfloat16 [512, 1536], replicated, may hold values from -0.25 to 0.25
- time_exit: bfloat16 [512, 512], replicated, may hold values from -0.375 to 0.375
- time_bias: float32 [512], replicated, may hold values from -1.75 to 1.75
- time_weigh: float32 [512], replicated, may hold values from 0.1 to 1.9
- time_shift: float32 [512], replicated, may hold values from -3 to 3
- time_widen: bfloat16 [512, 2048], replicated, may hold values from -0.25 to 0.25
- time_lift: float32 [2048], replicated, may hold values from -3 to 3
- time_narrow: bfloat16 [2048, 512], replicated, may hold values from -0.125 to 0.125
- time_nudge: float32 [512], replicated, may hold values from -1.75 to 1.75
- cotangent: bfloat16 [8, 2, 4, 16, 64, 512], P('batch', None, 'win'), may hold values from -6 to 6
- video_frames: int32 [8, 8], P('batch'), may hold values from 0 to 6, as said below
Outputs:
- result: bfloat16 [8, 2, 4, 16, 64, 512], P('batch', None, 'win')
- frames_delta: bfloat16 [8, 2, 4, 16, 64, 512], P('batch', None, 'win')
- space_gain_delta: float32 [512], P('batch')
- space_offset_delta: float32 [512], P('batch')
- space_entry_delta: float32 [512, 1536], P('batch')
- space_exit_delta: float32 [512, 512], P('batch')
- space_bias_delta: float32 [512], P('batch')
- space_weigh_delta: float32 [512], P('batch')
- space_shift_delta: float32 [512], P('batch')
- space_widen_delta: float32 [512, 2048], P('batch')
- space_lift_delta: float32 [2048], P('batch')
- space_narrow_delta: float32 [2048, 512], P('batch')
- space_nudge_delta: float32 [512], P('batch')
- time_gain_delta: float32 [512], P('batch')
- time_offset_delta: float32 [512], P('batch')
- time_entry_delta: float32 [512, 1536], P('batch')
- time_exit_delta: float32 [512, 512], P('batch')
- time_bias_delta: float32 [512], P('batch')
- time_weigh_delta: float32 [512], P('batch')
- time_shift_delta: float32 [512], P('batch')
- time_widen_delta: float32 [512, 2048], P('batch')
- time_lift_delta: float32 [2048], P('batch')
- time_narrow_delta: float32 [2048, 512], P('batch')
- time_nudge_delta: float32 [512], P('batch')
The draws below stay inside these ranges and needn't reach their ends.
Inputs may be any that keep to these rules, and one draw needn't show every extreme that they name: `video_frames`: each row lists the frame counts of up to 8 videos of one group in frame order, some entries 0; their total is at most 8 and the frames past it are padding. Each row has exactly one video of 6 frames.
All inputs are finite; a program needn't handle non-finite values.
Results may differ from the reference program's by a relative error of at most 0.02.
Values may be sent and summed in bfloat16 or wider, within the bound.
No kernel may reach another device: no remote copies, remote signals or barrier semaphores. Data moves between devices by JAX's collectives and lax.ppermute only.
A program may use at most 320 MiB of HBM per device.

```python
from functools import partial
import jax
import jax.numpy as jnp
from jax import lax

D = 512
HEADS = 8
HDIM = 64
FF = 2048
WTOK = 64
WINS = 16
VSLOT = 8
FW = 2
GROUPS = 8
FDEV = 8
LONGEST = 6
N_WIN = 4


def draw_video_frames(key, part):
    key = jax.random.fold_in(key, 7)
    first_key, padding_key, short_key = jax.random.split(key, 3)
    leading = jax.random.randint(first_key, (GROUPS,), 0, min(2, FDEV - LONGEST) + 1)
    padding = jax.random.randint(padding_key, (GROUPS,), 0, 4)
    limit = jnp.maximum(FDEV - padding, leading + LONGEST)
    shorts = jax.random.randint(short_key, (GROUPS, VSLOT), 1, 4)
    slots = jnp.arange(VSLOT, dtype=jnp.int32)[None, :]
    wanted = jnp.where(slots == 0, leading[:, None], jnp.where(slots == 1, LONGEST, shorts))
    starts = jnp.cumsum(wanted, axis=1) - wanted
    return jnp.clip(limit[:, None] - starts, 0, wanted).astype(jnp.int32)


def block_levels(rng, shape, pieces, least, top_value):
    factor_of, own = 1.0, jax.random.fold_in(rng, 6)
    for axis_at, shards_of in pieces:
        draws = jnp.exp(jax.random.uniform(jax.random.fold_in(own, axis_at), (shards_of,), jnp.float32, least / len(pieces), top_value / len(pieces)))
        factor_of = factor_of * jnp.repeat(draws, shape[axis_at] // shards_of).reshape([-1 if axis == axis_at else 1 for axis in range(len(shape))])
    return factor_of


def gaussian(own_key, shape, width, most, shards=(), kind=jnp.bfloat16):
    factor_of = block_levels(own_key, shape, shards, -0.22, 0.18) if shards else 1.0
    values = jax.random.normal(own_key, shape, jnp.float32) * width * factor_of
    return jnp.minimum(jnp.maximum(values, -most), most).astype(kind)


def setup_inputs(seed: int = 0) -> dict:
    seeds = jax.random.split(jax.random.key(seed), 26)
    frames = gaussian(seeds[0], (GROUPS, FW, N_WIN, WINS, WTOK, D), 1.0, 6.0, ((0, 8), (2, 4)))
    space_gain = jnp.clip(1.0 + 0.18 * jax.random.normal(seeds[1], (D,), jnp.float32), 0.1, 1.9)
    space_offset = gaussian(seeds[2], (D,), 0.5, 3.0, (), jnp.float32)
    space_entry = gaussian(seeds[3], (D, 3 * D), D ** -0.5, 0.25)
    space_exit = gaussian(seeds[4], (D, D), (D // 8) ** -0.5, 0.75)
    space_bias = gaussian(seeds[5], (D,), 0.3, 1.75, (), jnp.float32)
    space_weigh = jnp.clip(1.0 + 0.18 * jax.random.normal(seeds[6], (D,), jnp.float32), 0.1, 1.9)
    space_shift = gaussian(seeds[7], (D,), 0.5, 3.0, (), jnp.float32)
    space_widen = gaussian(seeds[8], (D, FF), D ** -0.5, 0.25)
    space_lift = gaussian(seeds[9], (FF,), 0.5, 3.0, (), jnp.float32)
    space_narrow = gaussian(seeds[10], (FF, D), FF ** -0.5, 0.125)
    space_nudge = gaussian(seeds[11], (D,), 0.3, 1.75, (), jnp.float32)
    time_gain = jnp.clip(1.0 + 0.18 * jax.random.normal(seeds[12], (D,), jnp.float32), 0.1, 1.9)
    time_offset = gaussian(seeds[13], (D,), 0.5, 3.0, (), jnp.float32)
    time_entry = gaussian(seeds[14], (D, 3 * D), D ** -0.5, 0.25)
    time_exit = gaussian(seeds[15], (D, D), (D // 2) ** -0.5, 0.375)
    time_bias = gaussian(seeds[16], (D,), 0.3, 1.75, (), jnp.float32)
    time_weigh = jnp.clip(1.0 + 0.18 * jax.random.normal(seeds[17], (D,), jnp.float32), 0.1, 1.9)
    time_shift = gaussian(seeds[18], (D,), 0.5, 3.0, (), jnp.float32)
    time_widen = gaussian(seeds[19], (D, FF), D ** -0.5, 0.25)
    time_lift = gaussian(seeds[20], (FF,), 0.5, 3.0, (), jnp.float32)
    time_narrow = gaussian(seeds[21], (FF, D), FF ** -0.5, 0.125)
    time_nudge = gaussian(seeds[22], (D,), 0.3, 1.75, (), jnp.float32)
    cotangent = gaussian(seeds[23], (GROUPS, FW, N_WIN, WINS, WTOK, D), 1.0, 6.0, ((0, 8), (2, 4)))
    video_frames = draw_video_frames(jax.random.fold_in(seeds[25], 71), 0)
    return dict(frames=frames, space_gain=space_gain, space_offset=space_offset, space_entry=space_entry, space_exit=space_exit, space_bias=space_bias, space_weigh=space_weigh, space_shift=space_shift, space_widen=space_widen, space_lift=space_lift, space_narrow=space_narrow, space_nudge=space_nudge, time_gain=time_gain, time_offset=time_offset, time_entry=time_entry, time_exit=time_exit, time_bias=time_bias, time_weigh=time_weigh, time_shift=time_shift, time_widen=time_widen, time_lift=time_lift, time_narrow=time_narrow, time_nudge=time_nudge, cotangent=cotangent, video_frames=video_frames)


@jax.custom_vjp
def low(v):
    return lax.optimization_barrier(v.astype(jnp.bfloat16)).astype(jnp.float32)

@jax.custom_vjp
def low_back(v):
    return v

def low_keep(v):
    return (low(v), None)

def low_pass(kept, grad):
    return (grad,)

def back_keep(v):
    return (v, None)

def back_low(kept, grad):
    return (low(grad),)
low.defvjp(low_keep, low_pass)
low_back.defvjp(back_keep, back_low)
EPS = 1e-05
HIGH = lax.Precision.HIGHEST
NEGATIVE = -1e+30

def normalize(rows, gain, offset):
    centre = rows - lax.optimization_barrier(jnp.mean(rows, axis=-1, keepdims=True))
    spread = lax.optimization_barrier(jnp.mean(centre * centre, axis=-1, keepdims=True))
    return centre * lax.rsqrt(spread + EPS) * gain + offset

def product(left, right):
    return jnp.dot(left, right, precision=HIGH)

def attend_window(triple):
    parts = triple.reshape(-1, WTOK, 3, HEADS, HDIM)
    scale = HDIM ** (-0.5)
    raw = jnp.einsum('gthd,gshd->ghts', parts[:, :, 0], parts[:, :, 1], precision=HIGH) * scale
    scores = low_back(raw)
    weights = low(jax.nn.softmax(scores, axis=-1))
    mixed = jnp.einsum('ghts,gshd->gthd', weights, parts[:, :, 2], precision=HIGH)
    return low(low_back(mixed.reshape(-1, D)))

def attend_time(triple, allowed):
    parts = triple.reshape(FDEV, -1, 3, HEADS, HDIM)
    scale = HDIM ** (-0.5)
    raw = jnp.einsum('tphd,sphd->phts', parts[:, :, 0], parts[:, :, 1], precision=HIGH) * scale
    scores = low_back(jnp.where(allowed, raw, NEGATIVE))
    weights = low(jax.nn.softmax(scores, axis=-1))
    mixed = jnp.einsum('phts,sphd->tphd', weights, parts[:, :, 2], precision=HIGH)
    return low(low_back(mixed.reshape(-1, D)))

def block(rows, params, attend):
    gain, offset, entry, leave, bias, weigh, shift, widen, lift, narrow, nudge = params
    normed = low(normalize(rows, gain, offset))
    triple = low(low_back(product(normed, entry)))
    mixed = attend(triple)
    middle = rows + low_back(product(mixed, leave) + bias)
    second = low(normalize(middle, weigh, shift))
    hidden = low_back(product(second, widen) + lift)
    active = low(jax.nn.gelu(hidden, approximate=False))
    return middle + low_back(product(active, narrow) + nudge)

def frame_allowed(lengths):
    ends = jnp.cumsum(lengths)
    positions = jnp.arange(FDEV, dtype=jnp.int32)
    video = lax.optimization_barrier(jnp.sum((positions[:, None] >= ends[None, :]).astype(jnp.int32), axis=1))
    video = jnp.where(positions < ends[-1], video, VSLOT + positions)
    return (video[:, None] == video[None, :]) & (positions[None, :] <= positions[:, None])

def reference(frames, space_gain, space_offset, space_entry, space_exit, space_bias, space_weigh, space_shift, space_widen, space_lift, space_narrow, space_nudge, time_gain, time_offset, time_entry, time_exit, time_bias, time_weigh, time_shift, time_widen, time_lift, time_narrow, time_nudge, cotangent, video_frames):
    spatial = tuple((param.astype(jnp.float32) for param in (space_gain, space_offset, space_entry, space_exit, space_bias, space_weigh, space_shift, space_widen, space_lift, space_narrow, space_nudge)))
    temporal = tuple((param.astype(jnp.float32) for param in (time_gain, time_offset, time_entry, time_exit, time_bias, time_weigh, time_shift, time_widen, time_lift, time_narrow, time_nudge)))
    inputs = frames.astype(jnp.float32)

    def forward(inputs, spatial, temporal):

        def one_group(pair):
            group_rows, lengths = pair
            group_rows = group_rows.reshape(-1, D)
            inner = low(low_back(block(group_rows, spatial, attend_window)))
            outer = block(inner, temporal, partial(attend_time, allowed=frame_allowed(lengths)))
            return low(outer).reshape(FW, N_WIN, WINS, WTOK, D)
        return lax.map(jax.checkpoint(one_group), (inputs, video_frames))
    outcome, pullback = jax.vjp(forward, inputs, spatial, temporal)
    inputs_back, space_back, time_back = pullback(cotangent.astype(jnp.float32))
    return (outcome.astype(jnp.bfloat16), inputs_back.astype(jnp.bfloat16), space_back[0], space_back[1], space_back[2], space_back[3], space_back[4], space_back[5], space_back[6], space_back[7], space_back[8], space_back[9], space_back[10], time_back[0], time_back[1], time_back[2], time_back[3], time_back[4], time_back[5], time_back[6], time_back[7], time_back[8], time_back[9], time_back[10])
```

```python
import functools

import jax
import jax.numpy as jnp
from jax import lax
from jax.experimental import pallas as pl
from jax.experimental.pallas import tpu as pltpu
from jax.sharding import PartitionSpec as P

D = 512
HEADS = 8
HDIM = 64
FF = 2048
PAIR = 2 * HDIM
PAIRS = HEADS // 2
CHUNK = 512
CHUNKS = FF // CHUNK
EPS = 1e-05
NEGATIVE = -1e30
FLOAT = jnp.float32
HALF = jnp.bfloat16
HALVES = 2
UNITS = 16
VMEM = 40 << 20

NORMED, MIXED, SECOND, ACTIVE = 0, 1, 2, 3
LEFTS = 3 + CHUNKS
TRIPLE_BACK, ATTEND_BACK, HIDDEN_BACK, BRANCH_BACK = 0, 3, 4, 4 + CHUNKS
RIGHTS = 5 + CHUNKS
GAIN, OFFSET, BIAS, WEIGH, SHIFT, NUDGE, LIFT = 0, 1, 2, 3, 4, 5, 6
SUMS = 6 + CHUNKS


def dot(left, right):
    return lax.dot_general(left, right, (((1,), (0,)), ((), ())), preferred_element_type=FLOAT)


def dot_right(left, right):
    return lax.dot_general(left, right, (((1,), (1,)), ((), ())), preferred_element_type=FLOAT)


def dot_left(left, right):
    return lax.dot_general(left, right, (((0,), (0,)), ((), ())), preferred_element_type=FLOAT)


def unit_of(rows):
    centre = rows - jnp.mean(rows, axis=-1, keepdims=True)
    inverse = lax.rsqrt(jnp.mean(centre * centre, axis=-1, keepdims=True) + EPS)
    return centre * inverse, inverse


def norm_back(scaled, unit, inverse):
    return inverse * (
        scaled
        - jnp.mean(scaled, axis=-1, keepdims=True)
        - unit * jnp.mean(scaled * unit, axis=-1, keepdims=True)
    )


def gelu_pair(hidden):
    half = 0.5 * lax.erf(hidden * 0.7071067811865476) + 0.5
    bell = jnp.exp(hidden * hidden * -0.5) * 0.3989422804014327
    return hidden * half, half + hidden * bell


def column_sum(values):
    return jnp.sum(values, axis=0, keepdims=True)


def first_head(rows):
    return lax.broadcasted_iota(jnp.int32, (rows, PAIR), 1) < HDIM


def spread(pair, first):
    zero = jnp.zeros_like(pair)
    return jnp.concatenate([jnp.where(first, pair, zero), jnp.where(first, zero, pair)], axis=0)


def gathered(both, first, rows):
    return jnp.where(first, both[:rows], both[rows:])


def attend_units(blocks):
    units = [(block, pair) for block in range(blocks) for pair in range(PAIRS)]
    return [units[start : start + UNITS] for start in range(0, len(units), UNITS)]


def columns(pair, part=0):
    start = part * D + pair * PAIR
    return slice(start, start + PAIR)


def attend_forward(triple, mixed, weights, blocks, rows, mask):
    first = first_head(rows)
    for units in attend_units(blocks):
        spans = [slice(block * rows, block * rows + rows) for block, _ in units]
        queries = [spread(triple[s, columns(p)], first) for s, (_, p) in zip(spans, units)]
        scores = [dot_right(triple[s, columns(p, 1)], q) for q, s, (_, p) in zip(queries, spans, units)]
        if mask is not None:
            scores = [score + mask for score in scores]
        powers = [
            jnp.exp((score - jnp.max(score, axis=0, keepdims=True)) * HDIM ** (-0.5)) for score in scores
        ]
        probs = [
            (power * (1.0 / jnp.sum(power, axis=0, keepdims=True))).astype(HALF) for power in powers
        ]
        both = [dot_left(prob, triple[s, columns(p, 2)]) for prob, s, (_, p) in zip(probs, spans, units)]
        for value, prob, s, (block, p) in zip(both, probs, spans, units):
            weights[block, p] = prob
            mixed[s, columns(p)] = gathered(value, first, rows).astype(HALF)


def attend_backward(triple, weights, mixed_back, put, blocks, rows):
    first = first_head(rows)
    scale = HDIM ** (-0.5)
    for units in attend_units(blocks):
        spans = [slice(block * rows, block * rows + rows) for block, _ in units]
        mixes = [spread(mixed_back[s, columns(p)], first) for s, (_, p) in zip(spans, units)]
        probs = [weights[block, p] for block, p in units]
        values_back = [dot(prob, mix) for prob, mix in zip(probs, mixes)]
        weights_back = [
            dot_right(triple[s, columns(p, 2)], mix) for mix, s, (_, p) in zip(mixes, spans, units)
        ]
        scores_back = []
        for prob, back in zip(probs, weights_back):
            wide = prob.astype(FLOAT)
            inside = back - jnp.sum(back * wide, axis=0, keepdims=True)
            scores_back.append((wide * inside * scale).astype(HALF))
        queries = [spread(triple[s, columns(p)], first) for s, (_, p) in zip(spans, units)]
        keys_back = [dot(score, query) for score, query in zip(scores_back, queries)]
        both = [
            dot_left(score, triple[s, columns(p, 1)])
            for score, s, (_, p) in zip(scores_back, spans, units)
        ]
        for key, value, pair, s, (_, p) in zip(keys_back, values_back, both, spans, units):
            put(s, p, 0, gathered(pair, first, rows).astype(HALF))
            put(s, p, 1, key.astype(HALF))
            put(s, p, 2, value.astype(HALF))


def whole(shape):
    return pl.BlockSpec(shape, lambda *_: (0,) * len(shape), pipeline_mode=pl.Buffered(1))


def run(body, name, grid, scalars, ins, outs, scratch=(), aliases=None, after=(), flops=0, moved=0):
    aliases = aliases or {}
    anywhere = pl.BlockSpec(memory_space=pl.ANY)
    first = len(scalars) + len(ins)
    extra = [*aliases.values(), *after]

    def inner(*refs):
        body(*refs[:first], *refs[first + len(extra) :])

    return pl.pallas_call(
        inner,
        out_shape=[jax.ShapeDtypeStruct(shape, kind) for shape, kind, _ in outs],
        grid_spec=pltpu.PrefetchScalarGridSpec(
            num_scalar_prefetch=len(scalars),
            grid=grid,
            in_specs=[spec for _, spec in ins] + [anywhere] * len(extra),
            out_specs=[spec for _, _, spec in outs],
            scratch_shapes=list(scratch),
        ),
        input_output_aliases={first + at: out for at, out in enumerate(aliases)},
        compiler_params=pltpu.CompilerParams(vmem_limit_bytes=VMEM),
        cost_estimate=pl.CostEstimate(flops=flops, bytes_accessed=moved, transcendentals=0),
        name=name,
    )(*scalars, *[array for array, _ in ins], *extra)


def plain(arrays):
    return [(array, whole(array.shape)) for array in arrays]


def slab_spec(slabs, rows, at):
    return pl.BlockSpec((slabs, rows, D), lambda *i: (0, at(*i), 0))


def row_spec(rows, width, at):
    return pl.BlockSpec((rows, width), lambda *i: (at(*i), 0))


def space_forward_body(place, rows_in, cotangent, *refs, window, pieces):
    gain, offset, entry, leave, bias, weigh, shift, widen, lift, narrow, nudge = refs[:11]
    inners, cuts = refs[11 : 11 + pieces], refs[11 + pieces : 11 + 2 * pieces]
    lefts, triple, weights, middles, slopes = refs[11 + 2 * pieces :]
    step = pl.program_id(0)
    shape = rows_in.shape
    rows = rows_in[...].reshape(-1, D).astype(FLOAT)
    count = rows.shape[0]
    unit, _ = unit_of(rows)
    normed = (unit * gain[...] + offset[...]).astype(HALF)
    lefts[NORMED] = normed
    triple[...] = dot(normed, entry[...]).astype(HALF)
    attend_forward(triple, lefts.at[MIXED], weights, count // window, window, None)
    middle = rows + dot(lefts[MIXED], leave[...]) + bias[...]
    middles[...] = middle
    unit_two, _ = unit_of(middle)
    second = (unit_two * weigh[...] + shift[...]).astype(HALF)
    lefts[SECOND] = second
    total = middle + nudge[...]
    for chunk in range(CHUNKS):
        at = slice(chunk * CHUNK, (chunk + 1) * CHUNK)
        active, slope = gelu_pair(dot(second, widen[:, at]) + lift[:, at])
        active = active.astype(HALF)
        lefts[ACTIVE + chunk] = active
        slopes[:, at] = slope.astype(HALF)
        total = total + dot(active, narrow[at, :])
    inner = total.astype(HALF).reshape(shape)
    for piece in range(pieces):

        @pl.when(step == piece)
        def _(piece=piece):
            inners[piece][...] = inner
            cuts[piece][...] = cotangent[...]


def space_forward(place, frames, cotangent, params, half, pieces, before):
    per_group, windows, window, _ = frames.shape
    each = windows // pieces // HALVES
    block = (per_group, each, window, D)
    rows = per_group * each * window
    count = rows * pieces * HALVES
    cut = pl.BlockSpec(block, lambda i, place: (0, (place[0] ^ i) * HALVES + half, 0, 0))
    at = lambda i, place: half * pieces + i
    attended = (rows // window, PAIRS, window, 2 * window)
    outs = [(block, HALF, pl.BlockSpec(block, lambda i, place: (0, 0, 0, 0)))] * (2 * pieces)
    outs += [
        ((LEFTS, count, D), HALF, slab_spec(LEFTS, rows, at)),
        ((count, 3 * D), HALF, row_spec(rows, 3 * D, at)),
        (
            (count // window, *attended[1:]),
            HALF,
            pl.BlockSpec(attended, lambda i, place: (at(i, place), 0, 0, 0)),
        ),
        ((count, D), FLOAT, row_spec(rows, D, at)),
        ((count, FF), HALF, row_spec(rows, FF, at)),
    ]
    made = run(
        functools.partial(space_forward_body, window=window, pieces=pieces),
        "space_forward",
        (pieces,),
        [place],
        [(frames, cut), (cotangent, cut)] + plain(params),
        outs,
        aliases={2 * pieces + number: array for number, array in enumerate(before)},
        flops=2 * rows * pieces * D * (4 * D + 2 * FF),
        moved=rows * pieces * (8 * D + 2 * LEFTS * D + 10 * D + 4 * D + 2 * FF),
    )
    return made[:pieces], made[pieces : 2 * pieces], made[2 * pieces :]


def by_position(refs, frames_of, positions):
    parts = [ref[frame].astype(FLOAT) for ref in refs for frame in range(frames_of)]
    return jnp.concatenate(
        [part[start : start + 8] for start in range(0, positions, 8) for part in parts], axis=0
    )


def by_frame(values, refs, frames_of, positions):
    total = len(refs) * frames_of
    for at, ref in enumerate(refs):
        for frame in range(frames_of):
            number = at * frames_of + frame
            ref[frame] = jnp.concatenate(
                [
                    values[(group * total + number) * 8 : (group * total + number) * 8 + 8]
                    for group in range(positions // 8)
                ],
                axis=0,
            ).astype(HALF)


def fill_mask(mask, place, lengths, per_group, pieces):
    window = mask.shape[0]
    key = lax.broadcasted_iota(jnp.int32, mask.shape, 0)
    query = lax.broadcasted_iota(jnp.int32, mask.shape, 1) % window
    frames = []
    for row in (query, key):
        number = row // 8
        frames.append((number % per_group) * pieces + ((number // per_group) ^ place[0]))
    videos = [jnp.zeros_like(frame) for frame in frames]
    entries = lengths.shape[1]
    end = 0
    for entry in range(entries):
        end = end + lengths[0, entry]
        videos = [v + (f >= end).astype(jnp.int32) for v, f in zip(videos, frames)]
    videos = [jnp.where(f < end, v, entries + f) for v, f in zip(videos, frames)]
    allowed = (videos[0] == videos[1]) & (frames[1] <= frames[0]) & (query % 8 == key % 8)
    mask[...] = jnp.where(allowed, 0.0, NEGATIVE)


def time_body(place, lengths, *refs, pieces):
    inners, cotangents = refs[:pieces], refs[pieces : 2 * pieces]
    gain, offset, entry, leave, bias, weigh, shift, widen, lift, narrow, nudge = refs[
        2 * pieces : 2 * pieces + 11
    ]
    refs = refs[2 * pieces + 11 :]
    results, backs = refs[:pieces], refs[pieces : 2 * pieces]
    lefts, rights, sums, triple, weights, mixed_back, mask = refs[2 * pieces :]
    frames_of, positions, _ = inners[0].shape
    window = 8 * pieces * frames_of
    rows = by_position(inners, frames_of, positions)
    blocks = rows.shape[0] // window

    @pl.when(pl.program_id(0) == 0)
    def _():
        sums[...] = jnp.zeros_like(sums)
        fill_mask(mask, place, lengths, frames_of, pieces)

    unit, inverse = unit_of(rows)
    normed = (unit * gain[...] + offset[...]).astype(HALF)
    lefts[NORMED] = normed
    triple[...] = dot(normed, entry[...]).astype(HALF)
    attend_forward(triple, lefts.at[MIXED], weights, blocks, window, mask[...])
    middle = rows + dot(lefts[MIXED], leave[...]) + bias[...]
    unit_two, inverse_two = unit_of(middle)
    second = (unit_two * weigh[...] + shift[...]).astype(HALF)
    lefts[SECOND] = second
    upstream = by_position(cotangents, frames_of, positions)
    branch_back = upstream.astype(HALF)
    rights[BRANCH_BACK] = branch_back
    sums[NUDGE] += column_sum(upstream)
    total = middle + nudge[...]
    second_back = jnp.zeros_like(middle)
    for chunk in range(CHUNKS):
        at = slice(chunk * CHUNK, (chunk + 1) * CHUNK)
        active, slope = gelu_pair(dot(second, widen[:, at]) + lift[:, at])
        active = active.astype(HALF)
        lefts[ACTIVE + chunk] = active
        hidden_back = dot_right(branch_back, narrow[at, :]) * slope
        hidden_low = hidden_back.astype(HALF)
        rights[HIDDEN_BACK + chunk] = hidden_low
        sums[LIFT + chunk] += column_sum(hidden_back)
        total = total + dot(active, narrow[at, :])
        second_back = second_back + dot_right(hidden_low, widen[:, at])
    by_frame(total, results, frames_of, positions)
    sums[WEIGH] += column_sum(second_back * unit_two)
    sums[SHIFT] += column_sum(second_back)
    middle_back = upstream + norm_back(second_back * weigh[...], unit_two, inverse_two)
    attend_back = middle_back.astype(HALF)
    rights[ATTEND_BACK] = attend_back
    sums[BIAS] += column_sum(middle_back)
    mixed_back[...] = dot_right(attend_back, leave[...]).astype(HALF)

    def put(span, pair, part, value):
        rights[TRIPLE_BACK + part, span, columns(pair)] = value

    attend_backward(triple, weights, mixed_back, put, blocks, window)
    normed_back = jnp.zeros_like(middle)
    for part in range(3):
        normed_back = normed_back + dot_right(
            rights[TRIPLE_BACK + part], entry[:, part * D : (part + 1) * D]
        )
    sums[GAIN] += column_sum(normed_back * unit)
    sums[OFFSET] += column_sum(normed_back)
    rows_back = middle_back + norm_back(normed_back * gain[...], unit, inverse)
    by_frame(rows_back, backs, frames_of, positions)


def time_block(place, lengths, inners, cotangents, params, half, before, step_rows=256):
    pieces = len(inners)
    per_group, each, window, _ = inners[0].shape
    positions = each * window
    flat = (per_group, positions, D)
    frames = per_group * pieces
    batch = min(max(step_rows // frames, 16), positions)
    rows = batch * frames
    steps = positions // batch
    count = positions * frames
    attended = 8 * frames
    spec = pl.BlockSpec((per_group, batch, D), lambda i, *_: (0, i, 0))
    at = lambda i, *_: half * steps + i
    outs = [(flat, HALF, spec)] * (2 * pieces)
    outs += [
        ((LEFTS, HALVES * count, D), HALF, slab_spec(LEFTS, rows, at)),
        ((RIGHTS, HALVES * count, D), HALF, slab_spec(RIGHTS, rows, at)),
        ((SUMS, 1, D), FLOAT, whole((SUMS, 1, D))),
    ]
    made = run(
        functools.partial(time_body, pieces=pieces),
        "time_block",
        (steps,),
        [place, lengths],
        [(array.reshape(flat), spec) for array in (*inners, *cotangents)] + plain(params),
        outs,
        scratch=[
            pltpu.VMEM((rows, 3 * D), HALF),
            pltpu.VMEM((rows // attended, PAIRS, attended, 2 * attended), HALF),
            pltpu.VMEM((rows, D), HALF),
            pltpu.VMEM((attended, 2 * attended), FLOAT),
        ],
        aliases={2 * pieces + number: array for number, array in enumerate(before)},
        flops=4 * count * D * (4 * D + 2 * FF),
        moved=count * 2 * D * (4 + LEFTS + RIGHTS) + 2 * D * (4 * D + 2 * FF),
    )
    shape = (per_group, each, window, D)
    results = [array.reshape(shape) for array in made[:pieces]]
    backs = [array.reshape(shape) for array in made[pieces : 2 * pieces]]
    return results, backs, made[2 * pieces : 2 * pieces + 2], made[2 * pieces + 2]


def feed_back_body(place, *refs, pieces):
    weigh, widen, narrow = refs[:3]
    backs, results = refs[3 : 3 + pieces], refs[3 + pieces : 3 + 2 * pieces]
    middles, slopes, outcome, rights, middles_back, sums, upstream_low = refs[3 + 2 * pieces :]
    step = pl.program_id(0)

    @pl.when(step == 0)
    def _():
        sums[...] = jnp.zeros_like(sums)

    for piece in range(pieces):

        @pl.when(step == piece)
        def _(piece=piece):
            upstream_low[...] = backs[piece][...].reshape(-1, D)
            outcome[...] = results[piece][...]

    branch_back = upstream_low[...]
    rights[4] = branch_back
    upstream = branch_back.astype(FLOAT)
    sums[NUDGE] += column_sum(upstream)
    second_back = jnp.zeros_like(upstream)
    for chunk in range(CHUNKS):
        at = slice(chunk * CHUNK, (chunk + 1) * CHUNK)
        hidden_back = dot_right(branch_back, narrow[at, :]) * slopes[:, at].astype(FLOAT)
        hidden_low = hidden_back.astype(HALF)
        rights[chunk] = hidden_low
        sums[LIFT + chunk] += column_sum(hidden_back)
        second_back = second_back + dot_right(hidden_low, widen[:, at])
    unit_two, inverse_two = unit_of(middles[...])
    sums[WEIGH] += column_sum(second_back * unit_two)
    sums[SHIFT] += column_sum(second_back)
    middle_back = upstream + norm_back(second_back * weigh[...], unit_two, inverse_two)
    middles_back[...] = middle_back
    sums[BIAS] += column_sum(middle_back)


def feed_back(place, shape, params, backs, results, middles, slopes, after):
    pieces = len(backs)
    per_group, windows, window, _ = shape
    block = backs[0].shape
    rows = per_group * block[1] * window
    count = rows * pieces
    across = pieces // HALVES
    cut = pl.BlockSpec(block, lambda i, place: (0, (place[0] ^ (i % across)) * HALVES + i // across, 0, 0))
    at = lambda i, place: i
    ins = plain([params[5], params[7], params[9]]) + plain(backs) + plain(results)
    ins += [(middles, row_spec(rows, D, at)), (slopes, row_spec(rows, FF, at))]
    return run(
        functools.partial(feed_back_body, pieces=pieces),
        "feed_back",
        (pieces,),
        [place],
        ins,
        [
            (shape, HALF, cut),
            ((CHUNKS + 1, count, D), HALF, slab_spec(CHUNKS + 1, rows, at)),
            ((count, D), FLOAT, row_spec(rows, D, at)),
            ((SUMS, 1, D), FLOAT, whole((SUMS, 1, D))),
        ],
        scratch=[pltpu.VMEM((rows, D), HALF)],
        after=after,
        flops=4 * count * D * FF,
        moved=count * (8 * D + 2 * (CHUNKS + 1) * D + 8 * D + 2 * FF),
    )


def attention_back_body(place, rows_in, gain, entry, leave, triple, weights, middles_back, *refs, window):
    delta, rights, sums, mixed_back = refs
    step = pl.program_id(0)

    @pl.when(step == 0)
    def _():
        sums[...] = jnp.zeros_like(sums)

    shape = rows_in.shape
    middle_back = middles_back[...]
    attend_back = middle_back.astype(HALF)
    rights[3] = attend_back
    mixed_back[...] = dot_right(attend_back, leave[...]).astype(HALF)

    def put(span, pair, part, value):
        rights[part, span, columns(pair)] = value

    attend_backward(triple, weights, mixed_back, put, middle_back.shape[0] // window, window)
    normed_back = jnp.zeros_like(middle_back)
    for part in range(3):
        normed_back = normed_back + dot_right(rights[part], entry[:, part * D : (part + 1) * D])
    unit, inverse = unit_of(rows_in[...].reshape(-1, D).astype(FLOAT))
    sums[GAIN] += column_sum(normed_back * unit)
    sums[OFFSET] += column_sum(normed_back)
    rows_back = middle_back + norm_back(normed_back * gain[...], unit, inverse)
    delta[...] = rows_back.astype(HALF).reshape(shape)


def attention_back(place, frames, params, triple, weights, middles_back, pieces, after):
    per_group, windows, window, _ = frames.shape
    block = (per_group, windows // pieces, window, D)
    rows = per_group * block[1] * window
    count = rows * pieces
    across = pieces // HALVES
    cut = pl.BlockSpec(block, lambda i, place: (0, (place[0] ^ (i % across)) * HALVES + i // across, 0, 0))
    at = lambda i, place: i
    attended = (rows // window, PAIRS, window, 2 * window)
    ins = [(frames, cut)] + plain([params[0], params[2], params[3]])
    ins += [
        (triple, row_spec(rows, 3 * D, at)),
        (weights, pl.BlockSpec(attended, lambda i, place: (i, 0, 0, 0))),
        (middles_back, row_spec(rows, D, at)),
    ]
    return run(
        functools.partial(attention_back_body, window=window),
        "attention_back",
        (pieces,),
        [place],
        ins,
        [
            (frames.shape, HALF, cut),
            ((4, count, D), HALF, slab_spec(4, rows, at)),
            ((SUMS, 1, D), FLOAT, whole((SUMS, 1, D))),
        ],
        scratch=[pltpu.VMEM((rows, D), HALF)],
        after=after,
        flops=8 * count * D * D,
        moved=count * D * 2 * (3 + 1 + 2 + 4 + 2),
    )


def gradient_body(core, left_at, right_at, left, right, *outs, narrows, sent):
    step = pl.program_id(0)
    value = dot_left(left[0], right[0]).astype(HALF)
    if narrows:
        away, own = outs[:2]
        outs = outs[2:]
        _, shards, rows, _ = away.shape
        parts = value.reshape(shards, 4, rows, CHUNK)

        @pl.when(step < narrows)
        def _():
            for sub in range(2):
                for shard in range(shards):
                    one, two = parts[shard, sub], parts[shard, 2 + sub]
                    own[sub, shard] = jnp.where(core[0] == 0, one, two)
                    away[sub, shard] = jnp.where(core[0] == 0, two, one)

    if sent:
        away, own = outs

        @pl.when((step >= narrows) & (step < narrows + sent))
        def _():
            away[0] = value.reshape(away.shape[1:])

        @pl.when(step >= narrows + sent)
        def _():
            own[0] = value.reshape(own.shape[1:])


def gradient_tiles(core, lefts, rights, narrow, tiles, batch, after=()):
    sent = len(tiles) // 2
    narrows = 0 if narrow is None else CHUNKS
    order = [jnp.arange(sent) + sent * (1 - core), jnp.arange(sent) + sent * core]
    order = jnp.concatenate(order).astype(jnp.int32)
    tables = []
    for which in range(2):
        table = jnp.array([tile[which] for tile in tiles], jnp.int32)[order]
        first = [ACTIVE + i if which == 0 else narrow for i in range(narrows)]
        tables.append(jnp.concatenate([jnp.array(first, jnp.int32), table]))
    count = lefts.shape[1]
    block = (1, count, CHUNK)
    rows = D // batch
    outs = []
    if narrows:
        shards = batch // CHUNKS
        spec = pl.BlockSpec(
            (2, shards, rows, CHUNK), lambda i, *_: (0, jnp.minimum(i, narrows - 1), 0, 0)
        )
        outs += [((2, batch, rows, CHUNK), HALF, spec)] * 2
    if sent:
        for start in (narrows, narrows + sent):
            spec = pl.BlockSpec(
                (1, batch, rows, CHUNK),
                lambda i, *_, start=start: (jnp.clip(i - start, 0, sent - 1), 0, 0, 0),
            )
            outs.append(((sent, batch, rows, CHUNK), HALF, spec))
    made = run(
        functools.partial(gradient_body, narrows=narrows, sent=sent),
        "gradient_tiles",
        (narrows + len(tiles),),
        [core.reshape(1), *tables],
        [
            (lefts, pl.BlockSpec(block, lambda i, core, left, right: (left[i], 0, 0))),
            (rights, pl.BlockSpec(block, lambda i, core, left, right: (right[i], 0, 0))),
        ],
        outs,
        after=after,
        flops=2 * count * CHUNK * CHUNK * (narrows + len(tiles)),
        moved=4 * count * CHUNK * (narrows + len(tiles)),
    )
    return made[::2], made[1::2]


def swap(value, axis, mask):
    size = lax.axis_size(axis)
    if mask == 0:
        return value
    return lax.ppermute(value, axis, [(i, i ^ mask) for i in range(size)])


def move(value, batch_mask, win_mask):
    if batch_mask == 0:
        return swap(value, "win", win_mask)
    if win_mask == 0:
        return swap(value, "batch", batch_mask)
    batch, win = lax.axis_size("batch"), lax.axis_size("win")
    pairs = [
        (b * win + w, (b ^ batch_mask) * win + (w ^ win_mask)) for b in range(batch) for w in range(win)
    ]
    return lax.ppermute(value, ("batch", "win"), pairs)


def exchange(arrays):
    made = {k: swap(arrays[k], "win", k) for k in reversed(range(len(arrays)))}
    return [made[k] for k in range(len(arrays))]


def split_body(place, *refs, groups, across):
    own, got, outs = refs[:groups], refs[groups : 2 * groups], refs[2 * groups :]
    column, row = place[1], place[2]
    width = CHUNK // across
    at = 0
    for one, two in zip(own, got):
        rows = one.shape[3]
        for tile in range(one.shape[0]):
            for piece, out in enumerate(outs):
                y = row ^ (piece % 2)
                x = pl.ds(pl.multiple_of((column ^ (piece // 2)) * width, width), width)
                total = one[tile, :, y, :, x].astype(FLOAT) + two[tile, :, y, :, x].astype(FLOAT)
                out[:, at : at + rows] = total.astype(HALF)
            at += rows


def merge_body(place, *refs, inputs):
    ins, outs = refs[:inputs], refs[inputs:]
    for piece, out in enumerate(outs):
        z = place[3] ^ piece
        total = ins[0][z].astype(FLOAT)
        for ref in ins[1:]:
            total = total + ref[z].astype(FLOAT)
        out[...] = total.astype(HALF)


def last_body(*refs):
    ins, out = refs[:-1], refs[-1]
    total = ins[0][...].astype(FLOAT)
    for ref in ins[1:]:
        total = total + ref[...].astype(FLOAT)
    out[...] = total.astype(HALF)


def unpack_body(place, *refs, pieces, across, layout):
    ins, outs, held = refs[:pieces], refs[pieces:-1], refs[-1]
    width = CHUNK // across
    for piece, ref in enumerate(ins):
        x = pl.ds(pl.multiple_of((place[1] ^ (piece // 2)) * width, width), width)
        held[place[4] ^ (piece % 2), :, x] = ref[...].astype(FLOAT)
    for out, places in zip(outs, layout):
        for core, start, rows, left, wide, row, column in places:
            out[row : row + rows, column : column + wide] = held[
                core, start : start + rows, left : left + wide
            ]


class Reduction:
    def __init__(self, place, away, own):
        self.place = place
        self.batch, self.win = lax.axis_size("batch"), lax.axis_size("win")
        self.across, self.depth = self.win // 2, self.batch // 2
        cut = lambda a: a.reshape(-1, self.depth, 2, *a.shape[2:])
        self.own = [cut(a) for a in own]
        self.got = [swap(cut(a), "win", 1) for a in away]
        self.rows = sum(a.shape[0] * a.shape[3] for a in self.own)
        self.width = CHUNK // self.across

    def cores(self, after=()):
        shape = (self.depth, self.rows, self.width)
        pieces = run(
            functools.partial(split_body, groups=len(self.own), across=self.across),
            "sum_cores",
            (1,),
            [self.place],
            plain(self.own + self.got),
            [(shape, HALF, whole(shape))] * (2 * self.across),
            after=after,
        )
        self.mark = pieces[:1]
        self.pieces = [move(a, number % 2, 2 * (number // 2)) for number, a in enumerate(pieces)]

    def chips(self, after=()):
        shape = (self.rows, self.width)
        pieces = run(
            functools.partial(merge_body, inputs=len(self.pieces)),
            "sum_chips",
            (1,),
            [self.place],
            plain(self.pieces),
            [(shape, HALF, whole(shape))] * self.depth,
            after=after,
        )
        self.mark = pieces[:1]
        self.pieces = [swap(a, "batch", 2 * number) for number, a in enumerate(pieces)]

    def last(self, after=()):
        shape = (self.rows, self.width)
        outs = [(shape, HALF, whole(shape))]
        (total,) = run(last_body, "sum_last", (1,), [], plain(self.pieces), outs, after=after)
        self.mark = [total]
        self.pieces = [swap(total, "win", number) for number in range(self.win)]

    def unpack(self, layout, shapes):
        return run(
            functools.partial(
                unpack_body, pieces=self.win, across=self.across, layout=layout
            ),
            "unpack",
            (1,),
            [self.place],
            plain(self.pieces),
            [(s, FLOAT, whole(s)) for s in shapes],
            scratch=[pltpu.VMEM((2, self.rows, CHUNK), FLOAT)],
        )


SMALL_ROWS = 16


def small_tiles(core, sums, batch):
    vectors = sums[:6, 0].reshape(6, batch, D // batch).swapaxes(0, 1).reshape(batch, -1)
    lifts = sums[LIFT:, 0].reshape(batch, FF // batch)
    both = [jnp.pad(a, ((0, 0), (0, CHUNK - a.shape[1]))).astype(HALF) for a in (vectors, lifts)]
    both = [jnp.broadcast_to(a[None, :, None], (1, batch, SMALL_ROWS, CHUNK)) for a in both]
    own = jnp.where(core == 0, both[0], both[1])
    away = jnp.where(core == 0, both[1], both[0])
    return away, own


ENTRY_TILES = [(NORMED, TRIPLE_BACK + part) for part in range(3)] + [(MIXED, ATTEND_BACK)]
WIDEN_TILES = [(SECOND, HIDDEN_BACK + chunk) for chunk in range(CHUNKS)]
TIME_TILES = WIDEN_TILES[:2] + ENTRY_TILES[:2] + WIDEN_TILES[2:] + ENTRY_TILES[2:]


def entry_places(rows, start):
    spot = lambda tile: (tile // 2, start + tile % 2 * rows, rows, 0, CHUNK)
    return [
        [(*spot(part), 0, part * CHUNK) for part in range(3)],
        [(*spot(3), 0, 0)],
    ], [(rows, 3 * D), (rows, D)]


def widen_places(rows, start):
    narrows = [(sub // 2, start + sub % 2 * rows, rows, 0, CHUNK, sub * rows, 0) for sub in range(4)]
    start += 2 * rows
    widens = [
        (chunk // 2, start + chunk % 2 * rows, rows, 0, CHUNK, 0, chunk * CHUNK) for chunk in range(CHUNKS)
    ]
    return [widens, narrows], [(rows, FF), (4 * rows, D)]


def small_places(rows, start):
    layout = [[(0, start, 1, number * rows, rows, 0, 0)] for number in range(6)]
    layout.append([(1, start, 1, 0, 4 * rows, 0, 0)])
    return layout, [(1, rows)] * 6 + [(1, 4 * rows)]


def local(*args):
    frames, cotangent, video_frames = args[0], args[23], args[24]
    space = [a.reshape(1, -1) if a.ndim == 1 else a for a in args[1:12]]
    time = [a.reshape(1, -1) if a.ndim == 1 else a for a in args[12:23]]
    batch, win = lax.axis_size("batch"), lax.axis_size("win")
    here, group = lax.axis_index("win"), lax.axis_index("batch")
    core = here % 2
    place = jnp.stack([here, here // 2, group % 2, group // 2, core]).astype(jnp.int32)
    _, per_group, _, windows, window, _ = frames.shape
    shape = (per_group, windows, window, D)
    rows_in, cotangent = frames.reshape(shape), cotangent.reshape(shape)
    rows = D // batch

    kept, inners, cotangents = [], [], []
    for half in range(HALVES):
        inner, cut, kept = space_forward(place, rows_in, cotangent, space, half, win, kept)
        inners.append(exchange(inner))
        cotangents.append(exchange(cut))
    space_lefts, triple, weights, middles, slopes = kept
    results, backs, slabs, time_sums = [], [], [], []
    for half in range(HALVES):
        result, back, slabs, sums = time_block(
            place, video_frames, inners[half], cotangents[half], time, half, slabs
        )
        backs += exchange(back)
        results += exchange(result)
        time_sums.append(sums)
    time_lefts, time_rights = slabs

    away, own = gradient_tiles(
        core, time_lefts, time_rights, BRANCH_BACK, TIME_TILES, batch
    )
    mark = own[:1]
    small_away, small_own = small_tiles(core, sum(time_sums), batch)
    time_sum = Reduction(place, [*away, small_away], [*own, small_own])
    outcome, feed_rights, middles_back, feed_sums = feed_back(
        place, shape, space, backs, results, middles, slopes, mark
    )
    time_sum.cores([middles_back])
    away, own = gradient_tiles(
        core,
        space_lefts,
        feed_rights,
        CHUNKS,
        [(SECOND, chunk) for chunk in range(CHUNKS)],
        batch,
        time_sum.mark,
    )
    feed_sum = Reduction(place, away, own)
    delta, attend_rights, attend_sums = attention_back(
        place, rows_in, space, triple, weights, middles_back, 2 * win, own[:1]
    )
    time_sum.chips([delta])
    feed_sum.cores(time_sum.mark)
    away, own = gradient_tiles(
        core,
        space_lefts,
        attend_rights,
        None,
        [(NORMED, part) for part in range(3)] + [(MIXED, 3)],
        batch,
        feed_sum.mark,
    )
    small_away, small_own = small_tiles(core, feed_sums + attend_sums, batch)
    attend_sum = Reduction(place, [*away, small_away], [*own, small_own])
    attend_sum.cores(own[:1])
    time_sum.last(attend_sum.mark)
    feed_sum.chips(time_sum.mark)
    attend_sum.chips(feed_sum.mark)
    feed_sum.last(attend_sum.mark)
    attend_sum.last(feed_sum.mark)

    return (
        outcome.reshape(frames.shape),
        delta.reshape(frames.shape),
        *collected(feed_sum, attend_sum, rows),
        *collected(time_sum, time_sum, rows),
    )


def collected(feed, attend, rows):
    feed_layout, feed_shapes = widen_places(rows, 0)
    attend_layout, attend_shapes = entry_places(rows, 4 * rows if feed is attend else 0)
    small_layout, small_shapes = small_places(rows, attend.rows - SMALL_ROWS)
    if feed is attend:
        made = feed.unpack(
            feed_layout + attend_layout + small_layout, feed_shapes + attend_shapes + small_shapes
        )
    else:
        made = feed.unpack(feed_layout, feed_shapes)
        made += attend.unpack(attend_layout + small_layout, attend_shapes + small_shapes)
    widen, narrow, entry, leave = made[:4]
    gain, offset, bias, weigh, shift, nudge, lift = [a.reshape(-1) for a in made[4:]]
    return gain, offset, entry, leave, bias, weigh, shift, widen, lift, narrow, nudge


def solution(mesh):
    rows = P("batch", None, "win", None, None, None)
    one, two = P("batch"), P("batch", None)
    grads = (one, one, two, two, one, one, one, two, one, two, one)
    return jax.shard_map(
        local,
        mesh=mesh,
        in_specs=(rows, *([P()] * 22), rows, P("batch", None)),
        out_specs=(rows, rows, *grads, *grads),
        check_vma=False,
    )
```

```python
import functools

import jax
import jax.numpy as jnp
from jax import lax
from jax.experimental import pallas as pl
from jax.experimental.pallas import tpu as pltpu
from jax.sharding import PartitionSpec as P

D = 512
HEADS = 8
HDIM = 64
FF = 2048
PAIR = 2 * HDIM
PAIRS = HEADS // 2
CHUNK = 512
CHUNKS = FF // CHUNK
EPS = 1e-05
NEGATIVE = -1e30
FLOAT = jnp.float32
HALF = jnp.bfloat16
HALVES = 2
UNITS = 16
VMEM = 62 << 20
SLOWER = 4

NORMED, MIXED, SECOND, ACTIVE = 0, 1, 2, 3
LEFTS = 3 + CHUNKS
TRIPLE_BACK, ATTEND_BACK, HIDDEN_BACK, BRANCH_BACK = 0, 3, 4, 4 + CHUNKS
RIGHTS = 5 + CHUNKS
INNER, COTANGENT = 0, 1
BACK, RESULT = 0, 1
GAIN, OFFSET, BIAS, WEIGH, SHIFT, NUDGE, LIFT = 0, 1, 2, 3, 4, 5, 6
SUMS = 6 + CHUNKS


def dot(left, right):
    return lax.dot_general(left, right, (((1,), (0,)), ((), ())), preferred_element_type=FLOAT)


def dot_right(left, right):
    return lax.dot_general(left, right, (((1,), (1,)), ((), ())), preferred_element_type=FLOAT)


def dot_left(left, right):
    return lax.dot_general(left, right, (((0,), (0,)), ((), ())), preferred_element_type=FLOAT)


def unit_of(rows):
    centre = rows - jnp.mean(rows, axis=-1, keepdims=True)
    inverse = lax.rsqrt(jnp.mean(centre * centre, axis=-1, keepdims=True) + EPS)
    return centre * inverse, inverse


def norm_back(scaled, unit, inverse):
    return inverse * (
        scaled
        - jnp.mean(scaled, axis=-1, keepdims=True)
        - unit * jnp.mean(scaled * unit, axis=-1, keepdims=True)
    )


def gelu_pair(hidden):
    half = 0.5 * lax.erf(hidden * 0.7071067811865476) + 0.5
    bell = jnp.exp(hidden * hidden * -0.5) * 0.3989422804014327
    return hidden * half, half + hidden * bell


def column_sum(values):
    return jnp.sum(values, axis=0, keepdims=True)


def first_head(rows):
    return lax.broadcasted_iota(jnp.int32, (rows, PAIR), 1) < HDIM


def spread(pair, first):
    zero = jnp.zeros_like(pair)
    return jnp.concatenate([jnp.where(first, pair, zero), jnp.where(first, zero, pair)], axis=0)


def gathered(both, first, rows):
    return jnp.where(first, both[:rows], both[rows:])


def attend_units(blocks):
    units = [(block, pair) for block in range(blocks) for pair in range(PAIRS)]
    return [units[start : start + UNITS] for start in range(0, len(units), UNITS)]


def columns(pair, part=0):
    start = part * D + pair * PAIR
    return slice(start, start + PAIR)


def attend_forward(triple, mixed, weights, blocks, rows, mask):
    first = first_head(rows)
    for units in attend_units(blocks):
        spans = [slice(block * rows, block * rows + rows) for block, _ in units]
        queries = [spread(triple[s, columns(p)], first) for s, (_, p) in zip(spans, units)]
        scores = [dot_right(triple[s, columns(p, 1)], q) for q, s, (_, p) in zip(queries, spans, units)]
        if mask is not None:
            scores = [score + mask for score in scores]
        powers = [
            jnp.exp((score - jnp.max(score, axis=0, keepdims=True)) * HDIM ** (-0.5)) for score in scores
        ]
        probs = [
            (power * (1.0 / jnp.sum(power, axis=0, keepdims=True))).astype(HALF) for power in powers
        ]
        both = [dot_left(prob, triple[s, columns(p, 2)]) for prob, s, (_, p) in zip(probs, spans, units)]
        for value, prob, s, (block, p) in zip(both, probs, spans, units):
            weights[block, p] = prob
            mixed[s, columns(p)] = gathered(value, first, rows).astype(HALF)


def attend_backward(triple, weights, mixed_back, put, blocks, rows):
    first = first_head(rows)
    scale = HDIM ** (-0.5)
    for units in attend_units(blocks):
        spans = [slice(block * rows, block * rows + rows) for block, _ in units]
        mixes = [spread(mixed_back[s, columns(p)], first) for s, (_, p) in zip(spans, units)]
        probs = [weights[block, p] for block, p in units]
        values_back = [dot(prob, mix) for prob, mix in zip(probs, mixes)]
        weights_back = [
            dot_right(triple[s, columns(p, 2)], mix) for mix, s, (_, p) in zip(mixes, spans, units)
        ]
        scores_back = []
        for prob, back in zip(probs, weights_back):
            wide = prob.astype(FLOAT)
            inside = back - jnp.sum(back * wide, axis=0, keepdims=True)
            scores_back.append((wide * inside * scale).astype(HALF))
        queries = [spread(triple[s, columns(p)], first) for s, (_, p) in zip(spans, units)]
        keys_back = [dot(score, query) for score, query in zip(scores_back, queries)]
        both = [
            dot_left(score, triple[s, columns(p, 1)])
            for score, s, (_, p) in zip(scores_back, spans, units)
        ]
        for key, value, pair, s, (_, p) in zip(keys_back, values_back, both, spans, units):
            put(s, p, 0, gathered(pair, first, rows).astype(HALF))
            put(s, p, 1, key.astype(HALF))
            put(s, p, 2, value.astype(HALF))


def whole(shape):
    return pl.BlockSpec(shape, lambda *_: (0,) * len(shape), pipeline_mode=pl.Buffered(1))


def run(body, name, grid, scalars, ins, outs, scratch=(), aliases=None, after=(), flops=0, moved=0):
    aliases = aliases or {}
    anywhere = pl.BlockSpec(memory_space=pl.ANY)
    first = len(scalars) + len(ins)
    extra = [*aliases.values(), *after]

    def inner(*refs):
        body(*refs[:first], *refs[first + len(extra) :])

    return pl.pallas_call(
        inner,
        out_shape=[jax.ShapeDtypeStruct(shape, kind) for shape, kind, _ in outs],
        grid_spec=pltpu.PrefetchScalarGridSpec(
            num_scalar_prefetch=len(scalars),
            grid=grid,
            in_specs=[spec for _, spec in ins] + [anywhere] * len(extra),
            out_specs=[spec for _, _, spec in outs],
            scratch_shapes=list(scratch),
        ),
        input_output_aliases={first + at: out for at, out in enumerate(aliases)},
        compiler_params=pltpu.CompilerParams(vmem_limit_bytes=VMEM),
        cost_estimate=pl.CostEstimate(flops=flops * SLOWER, bytes_accessed=moved * SLOWER, transcendentals=0),
        name=name,
    )(*scalars, *[array for array, _ in ins], *extra)


def plain(arrays):
    return [(array, whole(array.shape)) for array in arrays]


def slab_spec(slabs, rows, at):
    return pl.BlockSpec((slabs, rows, D), lambda *i: (0, at(*i), 0))


def row_spec(rows, width, at):
    return pl.BlockSpec((rows, width), lambda *i: (at(*i), 0))


def space_forward_body(place, rows_in, cotangent, *refs, window, pieces):
    gain, offset, entry, leave, bias, weigh, shift, widen, lift, narrow, nudge = refs[:11]
    sent = refs[11 : 11 + pieces]
    lefts, triple, weights, middles, slopes = refs[11 + pieces :]
    step = pl.program_id(0)
    shape = rows_in.shape
    rows = rows_in[...].reshape(-1, D).astype(FLOAT)
    count = rows.shape[0]
    unit, _ = unit_of(rows)
    normed = (unit * gain[...] + offset[...]).astype(HALF)
    lefts[NORMED] = normed
    triple[...] = dot(normed, entry[...]).astype(HALF)
    attend_forward(triple, lefts.at[MIXED], weights, count // window, window, None)
    middle = rows + dot(lefts[MIXED], leave[...]) + bias[...]
    middles[...] = middle
    unit_two, _ = unit_of(middle)
    second = (unit_two * weigh[...] + shift[...]).astype(HALF)
    lefts[SECOND] = second
    total = middle + nudge[...]
    for chunk in range(CHUNKS):
        at = slice(chunk * CHUNK, (chunk + 1) * CHUNK)
        active, slope = gelu_pair(dot(second, widen[:, at]) + lift[:, at])
        active = active.astype(HALF)
        lefts[ACTIVE + chunk] = active
        slopes[:, at] = slope.astype(HALF)
        total = total + dot(active, narrow[at, :])
    inner = total.astype(HALF).reshape(shape)
    for piece in range(pieces):

        @pl.when(step == piece)
        def _(piece=piece):
            sent[piece][INNER] = inner
            sent[piece][COTANGENT] = cotangent[...]


def space_forward(place, frames, cotangent, params, half, pieces, before):
    per_group, windows, window, _ = frames.shape
    each = windows // pieces // HALVES
    block = (per_group, each, window, D)
    rows = per_group * each * window
    count = rows * pieces * HALVES
    cut = pl.BlockSpec(block, lambda i, place: (0, (place[0] ^ i) * HALVES + half, 0, 0))
    at = lambda i, place: half * pieces + i
    attended = (rows // window, PAIRS, window, 2 * window)
    both = (2, *block)
    outs = [(both, HALF, pl.BlockSpec(both, lambda i, place: (0,) * 5))] * pieces
    outs += [
        ((LEFTS, count, D), HALF, slab_spec(LEFTS, rows, at)),
        ((count, 3 * D), HALF, row_spec(rows, 3 * D, at)),
        (
            (count // window, *attended[1:]),
            HALF,
            pl.BlockSpec(attended, lambda i, place: (at(i, place), 0, 0, 0)),
        ),
        ((count, D), FLOAT, row_spec(rows, D, at)),
        ((count, FF), HALF, row_spec(rows, FF, at)),
    ]
    made = run(
        functools.partial(space_forward_body, window=window, pieces=pieces),
        "space_forward",
        (pieces,),
        [place],
        [(frames, cut), (cotangent, cut)] + plain(params),
        outs,
        aliases={pieces + number: array for number, array in enumerate(before)},
        flops=2 * rows * pieces * D * (4 * D + 2 * FF),
        moved=rows * pieces * (8 * D + 2 * LEFTS * D + 10 * D + 4 * D + 2 * FF),
    )
    return made[:pieces], made[pieces:]


def by_position(refs, which, frames_of, positions):
    parts = [ref[which, frame].astype(FLOAT) for ref in refs for frame in range(frames_of)]
    return jnp.concatenate(
        [part[start : start + 8] for start in range(0, positions, 8) for part in parts], axis=0
    )


def by_frame(values, refs, which, frames_of, positions):
    total = len(refs) * frames_of
    for at, ref in enumerate(refs):
        for frame in range(frames_of):
            number = at * frames_of + frame
            ref[which, frame] = jnp.concatenate(
                [
                    values[(group * total + number) * 8 : (group * total + number) * 8 + 8]
                    for group in range(positions // 8)
                ],
                axis=0,
            ).astype(HALF)


def fill_mask(mask, place, lengths, per_group, pieces):
    window = mask.shape[0]
    key = lax.broadcasted_iota(jnp.int32, mask.shape, 0)
    query = lax.broadcasted_iota(jnp.int32, mask.shape, 1) % window
    frames = []
    for row in (query, key):
        number = row // 8
        frames.append((number % per_group) * pieces + ((number // per_group) ^ place[0]))
    videos = [jnp.zeros_like(frame) for frame in frames]
    entries = lengths.shape[1]
    end = 0
    for entry in range(entries):
        end = end + lengths[0, entry]
        videos = [v + (f >= end).astype(jnp.int32) for v, f in zip(videos, frames)]
    videos = [jnp.where(f < end, v, entries + f) for v, f in zip(videos, frames)]
    allowed = (videos[0] == videos[1]) & (frames[1] <= frames[0]) & (query % 8 == key % 8)
    mask[...] = jnp.where(allowed, 0.0, NEGATIVE)


def time_body(place, lengths, *refs, pieces):
    came = refs[:pieces]
    gain, offset, entry, leave, bias, weigh, shift, widen, lift, narrow, nudge = refs[pieces : pieces + 11]
    sent = refs[pieces + 11 : 2 * pieces + 11]
    refs = refs[2 * pieces + 11 :]
    lefts, rights, sums, triple, weights, mixed_back, mask = refs
    _, frames_of, positions, _ = came[0].shape
    window = 8 * pieces * frames_of
    rows = by_position(came, INNER, frames_of, positions)
    blocks = rows.shape[0] // window

    @pl.when(pl.program_id(0) == 0)
    def _():
        sums[...] = jnp.zeros_like(sums)
        fill_mask(mask, place, lengths, frames_of, pieces)

    unit, inverse = unit_of(rows)
    normed = (unit * gain[...] + offset[...]).astype(HALF)
    lefts[NORMED] = normed
    triple[...] = dot(normed, entry[...]).astype(HALF)
    attend_forward(triple, lefts.at[MIXED], weights, blocks, window, mask[...])
    middle = rows + dot(lefts[MIXED], leave[...]) + bias[...]
    unit_two, inverse_two = unit_of(middle)
    second = (unit_two * weigh[...] + shift[...]).astype(HALF)
    lefts[SECOND] = second
    upstream = by_position(came, COTANGENT, frames_of, positions)
    branch_back = upstream.astype(HALF)
    rights[BRANCH_BACK] = branch_back
    sums[NUDGE] += column_sum(upstream)
    total = middle + nudge[...]
    second_back = jnp.zeros_like(middle)
    for chunk in range(CHUNKS):
        at = slice(chunk * CHUNK, (chunk + 1) * CHUNK)
        active, slope = gelu_pair(dot(second, widen[:, at]) + lift[:, at])
        active = active.astype(HALF)
        lefts[ACTIVE + chunk] = active
        hidden_back = dot_right(branch_back, narrow[at, :]) * slope
        hidden_low = hidden_back.astype(HALF)
        rights[HIDDEN_BACK + chunk] = hidden_low
        sums[LIFT + chunk] += column_sum(hidden_back)
        total = total + dot(active, narrow[at, :])
        second_back = second_back + dot_right(hidden_low, widen[:, at])
    by_frame(total, sent, RESULT, frames_of, positions)
    sums[WEIGH] += column_sum(second_back * unit_two)
    sums[SHIFT] += column_sum(second_back)
    middle_back = upstream + norm_back(second_back * weigh[...], unit_two, inverse_two)
    attend_back = middle_back.astype(HALF)
    rights[ATTEND_BACK] = attend_back
    sums[BIAS] += column_sum(middle_back)
    mixed_back[...] = dot_right(attend_back, leave[...]).astype(HALF)

    def put(span, pair, part, value):
        rights[TRIPLE_BACK + part, span, columns(pair)] = value

    attend_backward(triple, weights, mixed_back, put, blocks, window)
    normed_back = jnp.zeros_like(middle)
    for part in range(3):
        normed_back = normed_back + dot_right(
            rights[TRIPLE_BACK + part], entry[:, part * D : (part + 1) * D]
        )
    sums[GAIN] += column_sum(normed_back * unit)
    sums[OFFSET] += column_sum(normed_back)
    rows_back = middle_back + norm_back(normed_back * gain[...], unit, inverse)
    by_frame(rows_back, sent, BACK, frames_of, positions)


def time_block(place, lengths, came, params, half, before, step_rows=256):
    pieces = len(came)
    _, per_group, each, window, _ = came[0].shape
    positions = each * window
    flat = (2, per_group, positions, D)
    frames = per_group * pieces
    batch = min(max(step_rows // frames, 16), positions)
    rows = batch * frames
    steps = positions // batch
    count = positions * frames
    attended = 8 * frames
    spec = pl.BlockSpec((2, per_group, batch, D), lambda i, *_: (0, 0, i, 0))
    at = lambda i, *_: half * steps + i
    outs = [(flat, HALF, spec)] * pieces
    outs += [
        ((LEFTS, HALVES * count, D), HALF, slab_spec(LEFTS, rows, at)),
        ((RIGHTS, HALVES * count, D), HALF, slab_spec(RIGHTS, rows, at)),
        ((SUMS, 1, D), FLOAT, whole((SUMS, 1, D))),
    ]
    made = run(
        functools.partial(time_body, pieces=pieces),
        "time_block",
        (steps,),
        [place, lengths],
        [(array.reshape(flat), spec) for array in came] + plain(params),
        outs,
        scratch=[
            pltpu.VMEM((rows, 3 * D), HALF),
            pltpu.VMEM((rows // attended, PAIRS, attended, 2 * attended), HALF),
            pltpu.VMEM((rows, D), HALF),
            pltpu.VMEM((attended, 2 * attended), FLOAT),
        ],
        aliases={pieces + number: array for number, array in enumerate(before)},
        flops=4 * count * D * (4 * D + 2 * FF),
        moved=count * 2 * D * (4 + LEFTS + RIGHTS) + 2 * D * (4 * D + 2 * FF),
    )
    shape = (2, per_group, each, window, D)
    sent = [array.reshape(shape) for array in made[:pieces]]
    return sent, made[pieces : pieces + 2], made[pieces + 2]


def feed_back_body(place, *refs, pieces):
    weigh, widen, narrow = refs[:3]
    came = refs[3 : 3 + pieces]
    middles, slopes, outcome, rights, middles_back, sums, upstream_low = refs[3 + pieces :]
    step = pl.program_id(0)

    @pl.when(step == 0)
    def _():
        sums[...] = jnp.zeros_like(sums)

    for piece in range(pieces):

        @pl.when(step == piece)
        def _(piece=piece):
            upstream_low[...] = came[piece][BACK].reshape(-1, D)
            outcome[...] = came[piece][RESULT]

    branch_back = upstream_low[...]
    rights[4] = branch_back
    upstream = branch_back.astype(FLOAT)
    sums[NUDGE] += column_sum(upstream)
    second_back = jnp.zeros_like(upstream)
    for chunk in range(CHUNKS):
        at = slice(chunk * CHUNK, (chunk + 1) * CHUNK)
        hidden_back = dot_right(branch_back, narrow[at, :]) * slopes[:, at].astype(FLOAT)
        hidden_low = hidden_back.astype(HALF)
        rights[chunk] = hidden_low
        sums[LIFT + chunk] += column_sum(hidden_back)
        second_back = second_back + dot_right(hidden_low, widen[:, at])
    unit_two, inverse_two = unit_of(middles[...])
    sums[WEIGH] += column_sum(second_back * unit_two)
    sums[SHIFT] += column_sum(second_back)
    middle_back = upstream + norm_back(second_back * weigh[...], unit_two, inverse_two)
    middles_back[...] = middle_back
    sums[BIAS] += column_sum(middle_back)


def feed_back(place, shape, params, came, middles, slopes, after):
    pieces = len(came)
    per_group, windows, window, _ = shape
    block = came[0].shape[1:]
    rows = per_group * block[1] * window
    count = rows * pieces
    across = pieces // HALVES
    cut = pl.BlockSpec(block, lambda i, place: (0, (place[0] ^ (i % across)) * HALVES + i // across, 0, 0))
    at = lambda i, place: i
    ins = plain([params[5], params[7], params[9]]) + plain(came)
    ins += [(middles, row_spec(rows, D, at)), (slopes, row_spec(rows, FF, at))]
    return run(
        functools.partial(feed_back_body, pieces=pieces),
        "feed_back",
        (pieces,),
        [place],
        ins,
        [
            (shape, HALF, cut),
            ((CHUNKS + 1, count, D), HALF, slab_spec(CHUNKS + 1, rows, at)),
            ((count, D), FLOAT, row_spec(rows, D, at)),
            ((SUMS, 1, D), FLOAT, whole((SUMS, 1, D))),
        ],
        scratch=[pltpu.VMEM((rows, D), HALF)],
        after=after,
        flops=4 * count * D * FF,
        moved=count * (8 * D + 2 * (CHUNKS + 1) * D + 8 * D + 2 * FF),
    )


def attention_back_body(place, rows_in, gain, entry, leave, triple, weights, middles_back, *refs, window):
    delta, rights, sums, mixed_back = refs
    step = pl.program_id(0)

    @pl.when(step == 0)
    def _():
        sums[...] = jnp.zeros_like(sums)

    shape = rows_in.shape
    middle_back = middles_back[...]
    attend_back = middle_back.astype(HALF)
    rights[3] = attend_back
    mixed_back[...] = dot_right(attend_back, leave[...]).astype(HALF)

    def put(span, pair, part, value):
        rights[part, span, columns(pair)] = value

    attend_backward(triple, weights, mixed_back, put, middle_back.shape[0] // window, window)
    normed_back = jnp.zeros_like(middle_back)
    for part in range(3):
        normed_back = normed_back + dot_right(rights[part], entry[:, part * D : (part + 1) * D])
    unit, inverse = unit_of(rows_in[...].reshape(-1, D).astype(FLOAT))
    sums[GAIN] += column_sum(normed_back * unit)
    sums[OFFSET] += column_sum(normed_back)
    rows_back = middle_back + norm_back(normed_back * gain[...], unit, inverse)
    delta[...] = rows_back.astype(HALF).reshape(shape)


def attention_back(place, frames, params, triple, weights, middles_back, pieces, after):
    per_group, windows, window, _ = frames.shape
    block = (per_group, windows // pieces, window, D)
    rows = per_group * block[1] * window
    count = rows * pieces
    across = pieces // HALVES
    cut = pl.BlockSpec(block, lambda i, place: (0, (place[0] ^ (i % across)) * HALVES + i // across, 0, 0))
    at = lambda i, place: i
    attended = (rows // window, PAIRS, window, 2 * window)
    ins = [(frames, cut)] + plain([params[0], params[2], params[3]])
    ins += [
        (triple, row_spec(rows, 3 * D, at)),
        (weights, pl.BlockSpec(attended, lambda i, place: (i, 0, 0, 0))),
        (middles_back, row_spec(rows, D, at)),
    ]
    return run(
        functools.partial(attention_back_body, window=window),
        "attention_back",
        (pieces,),
        [place],
        ins,
        [
            (frames.shape, HALF, cut),
            ((4, count, D), HALF, slab_spec(4, rows, at)),
            ((SUMS, 1, D), FLOAT, whole((SUMS, 1, D))),
        ],
        scratch=[pltpu.VMEM((rows, D), HALF)],
        after=after,
        flops=8 * count * D * D,
        moved=count * D * 2 * (3 + 1 + 2 + 4 + 2),
    )


def gradient_body(core, left_at, right_at, left, right, *outs, narrows, starts):
    step = pl.program_id(0)
    value = dot_left(left[0], right[0]).astype(HALF)
    if narrows:
        away, own = outs[:2]
        outs = outs[2:]
        _, shards, rows, _ = away.shape
        parts = value.reshape(shards, 4, rows, CHUNK)

        @pl.when(step < narrows)
        def _():
            for sub in range(2):
                for shard in range(shards):
                    one, two = parts[shard, sub], parts[shard, 2 + sub]
                    own[sub, shard] = jnp.where(core[0] == 0, one, two)
                    away[sub, shard] = jnp.where(core[0] == 0, two, one)

    for out, (start, size) in zip(outs, starts):

        @pl.when((step >= start) & (step < start + size))
        def _(out=out):
            out[0] = value.reshape(out.shape[1:])


def gradient_tiles(core, lefts, rights, narrow, groups, batch, after=()):
    narrows = 0 if narrow is None else CHUNKS
    lists = [[ACTIVE + i for i in range(narrows)], [narrow] * narrows]
    tables = [[jnp.array(a, jnp.int32)] for a in lists]
    count = lefts.shape[1]
    block = (1, count, CHUNK)
    rows = D // batch
    outs, starts, start = [], [], narrows
    if narrows:
        shards = batch // CHUNKS
        spec = pl.BlockSpec(
            (2, shards, rows, CHUNK), lambda i, *_: (0, jnp.minimum(i, narrows - 1), 0, 0)
        )
        outs += [((2, batch, rows, CHUNK), HALF, spec)] * 2
    for tiles, which in groups:
        size = len(tiles) // 2
        for side in range(2):
            halves = [jnp.array([t[side] for t in tiles[h * size : (h + 1) * size]], jnp.int32) for h in range(2)]
            tables[side].append(jnp.where(which == 0, halves[0], halves[1]))
        spec = pl.BlockSpec(
            (1, batch, rows, CHUNK),
            lambda i, *_, start=start, size=size: (jnp.clip(i - start, 0, size - 1), 0, 0, 0),
        )
        outs.append(((size, batch, rows, CHUNK), HALF, spec))
        starts.append((start, size))
        start += size
    return run(
        functools.partial(gradient_body, narrows=narrows, starts=starts),
        "gradient_tiles",
        (start,),
        [core.reshape(1), *[jnp.concatenate(table) for table in tables]],
        [
            (lefts, pl.BlockSpec(block, lambda i, core, left, right: (left[i], 0, 0))),
            (rights, pl.BlockSpec(block, lambda i, core, left, right: (right[i], 0, 0))),
        ],
        outs,
        after=after,
        flops=2 * count * CHUNK * CHUNK * start,
        moved=4 * count * CHUNK * start,
    )


def scatter_body(left_at, right_at, left, right, out, buffer, sems, *, narrows, units):
    step = pl.program_id(0)
    steps = pl.num_programs(0)
    slot = step % 2
    batch, win, _, rows, width = out.shape

    def copies(number, at, narrow):
        made = []
        for half in range(2):
            x = pl.ds(half * width, width)
            if narrow:
                shards = batch // narrows
                source = buffer.at[at].reshape(shards, 4, rows, CHUNK)
                for sub in range(4):
                    unit = sub * 2 + half
                    made.append(
                        pltpu.make_async_copy(
                            source.at[:, sub, :, x],
                            out.at[pl.ds(number * shards, shards), unit // units, unit % units],
                            sems.at[at, sub * 2 + half],
                        )
                    )
            else:
                unit = 8 + (number - narrows) * 2 + half
                made.append(
                    pltpu.make_async_copy(
                        buffer.at[at].reshape(batch, rows, CHUNK).at[:, :, x],
                        out.at[:, unit // units, unit % units],
                        sems.at[at, half],
                    )
                )
        return made

    def each(number, at, act):
        @pl.when(number < narrows)
        def _():
            for copy in copies(number, at, True):
                act(copy)

        @pl.when(number >= narrows)
        def _():
            for copy in copies(number, at, False):
                act(copy)

    @pl.when(step >= 2)
    def _():
        each(step - 2, slot, lambda copy: copy.wait())

    buffer[slot] = dot_left(left[0], right[0]).astype(HALF)
    each(step, slot, lambda copy: copy.start())

    @pl.when(step == steps - 1)
    def _():
        each(step - 1, 1 - slot, lambda copy: copy.wait())
        each(step, slot, lambda copy: copy.wait())


def scattered_tiles(lefts, rights, narrow, tiles, batch, win, after):
    units = 2 * (CHUNKS + len(tiles)) // win
    rows, width = D // batch, CHUNK // 2
    count = lefts.shape[1]
    block = (1, count, CHUNK)
    left_at = jnp.array([ACTIVE + i for i in range(CHUNKS)] + [t[0] for t in tiles], jnp.int32)
    right_at = jnp.array([narrow] * CHUNKS + [t[1] for t in tiles], jnp.int32)
    steps = CHUNKS + len(tiles)
    (out,) = run(
        functools.partial(scatter_body, narrows=CHUNKS, units=units),
        "scattered_tiles",
        (steps,),
        [left_at, right_at],
        [
            (lefts, pl.BlockSpec(block, lambda i, left, right: (left[i], 0, 0))),
            (rights, pl.BlockSpec(block, lambda i, left, right: (right[i], 0, 0))),
        ],
        [((batch, win, units, rows, width), HALF, pl.BlockSpec(memory_space=pl.ANY))],
        scratch=[pltpu.VMEM((2, CHUNK, CHUNK), HALF), pltpu.SemaphoreType.DMA((2, 8))],
        after=after,
        flops=2 * count * CHUNK * CHUNK * steps,
        moved=4 * count * CHUNK * steps,
    )
    return out.reshape(batch * win, units * rows, width)


def spread_body(place, *refs, pieces, layout):
    ins, outs, held = refs[:pieces], refs[pieces:-1], refs[-1]
    for piece, ref in enumerate(ins):
        held[place[0] ^ piece] = ref[...].astype(FLOAT)
    units = held.shape[1]
    rows, width = held.shape[2:]
    for out, places in zip(outs, layout):
        for unit, row, column in places:
            out[row * rows : (row + 1) * rows, column * width : (column + 1) * width] = held[
                unit // units, unit % units
            ]


def spread_units(place, total, win, rows, after=()):
    units = total.shape[0] // rows
    width = total.shape[1]
    pieces = [swap(total, "win", number).reshape(units, rows, width) for number in range(win)]
    spot = lambda tile, row, column: [(8 + tile * 2 + half, row, column * 2 + half) for half in range(2)]
    narrow = [(sub * 2 + half, sub, half) for sub in range(4) for half in range(2)]
    layout = [
        sum([spot(chunk, 0, chunk) for chunk in range(CHUNKS)], []),
        narrow,
        sum([spot(CHUNKS + part, 0, part) for part in range(3)], []),
        spot(CHUNKS + 3, 0, 0),
    ]
    shapes = [(rows, FF), (4 * rows, D), (rows, 3 * D), (rows, D)]
    return run(
        functools.partial(spread_body, pieces=win, layout=layout),
        "spread_units",
        (1,),
        [place],
        plain(pieces),
        [(s, FLOAT, whole(s)) for s in shapes],
        scratch=[pltpu.VMEM((win, units, rows, width), FLOAT)],
        after=after,
    )


def swap(value, axis, mask):
    size = lax.axis_size(axis)
    if mask == 0:
        return value
    return lax.ppermute(value, axis, [(i, i ^ mask) for i in range(size)])


def move(value, batch_mask, win_mask):
    if batch_mask == 0:
        return swap(value, "win", win_mask)
    if win_mask == 0:
        return swap(value, "batch", batch_mask)
    batch, win = lax.axis_size("batch"), lax.axis_size("win")
    pairs = [
        (b * win + w, (b ^ batch_mask) * win + (w ^ win_mask)) for b in range(batch) for w in range(win)
    ]
    return lax.ppermute(value, ("batch", "win"), pairs)


def exchange(arrays):
    made = {k: swap(arrays[k], "win", k) for k in reversed(range(len(arrays)))}
    return [made[k] for k in range(len(arrays))]


def split_body(place, *refs, groups, across):
    own, got, outs = refs[:groups], refs[groups : 2 * groups], refs[2 * groups :]
    column, row = place[1], place[2]
    width = CHUNK // across
    at = 0
    for one, two in zip(own, got):
        rows = one.shape[3]
        for tile in range(one.shape[0]):
            for piece, out in enumerate(outs):
                y = row ^ (piece % 2)
                x = pl.ds(pl.multiple_of((column ^ (piece // 2)) * width, width), width)
                total = one[tile, :, y, :, x].astype(FLOAT) + two[tile, :, y, :, x].astype(FLOAT)
                out[:, at : at + rows] = total.astype(HALF)
            at += rows


def merge_body(place, *refs, inputs):
    ins, outs = refs[:inputs], refs[inputs:]
    for piece, out in enumerate(outs):
        z = place[3] ^ piece
        total = ins[0][z].astype(FLOAT)
        for ref in ins[1:]:
            total = total + ref[z].astype(FLOAT)
        out[...] = total.astype(HALF)


def last_body(*refs):
    ins, out = refs[:-1], refs[-1]
    total = ins[0][...].astype(FLOAT)
    for ref in ins[1:]:
        total = total + ref[...].astype(FLOAT)
    out[...] = total.astype(HALF)


def unpack_body(place, *refs, pieces, across, layout):
    ins, outs, held = refs[:pieces], refs[pieces:-1], refs[-1]
    width = CHUNK // across
    for piece, ref in enumerate(ins):
        x = pl.ds(pl.multiple_of((place[1] ^ (piece // 2)) * width, width), width)
        held[place[4] ^ (piece % 2), :, x] = ref[...].astype(FLOAT)
    for out, places in zip(outs, layout):
        for core, start, rows, left, wide, row, column in places:
            out[row : row + rows, column : column + wide] = held[
                core, start : start + rows, left : left + wide
            ]


class Reduction:
    def __init__(self, place, away, own):
        self.place = place
        self.batch, self.win = lax.axis_size("batch"), lax.axis_size("win")
        self.across, self.depth = self.win // 2, self.batch // 2
        cut = lambda a: a.reshape(-1, self.depth, 2, *a.shape[2:])
        self.own = [cut(a) for a in own]
        self.got = [swap(cut(a), "win", 1) for a in away]
        self.rows = sum(a.shape[0] * a.shape[3] for a in self.own)
        self.width = CHUNK // self.across

    def cores(self, after=()):
        shape = (self.depth, self.rows, self.width)
        pieces = run(
            functools.partial(split_body, groups=len(self.own), across=self.across),
            "sum_cores",
            (1,),
            [self.place],
            plain(self.own + self.got),
            [(shape, HALF, whole(shape))] * (2 * self.across),
            after=after,
        )
        self.mark = pieces[:1]
        self.pieces = [move(a, number % 2, 2 * (number // 2)) for number, a in enumerate(pieces)]

    def chips(self, after=()):
        shape = (self.rows, self.width)
        pieces = run(
            functools.partial(merge_body, inputs=len(self.pieces)),
            "sum_chips",
            (1,),
            [self.place],
            plain(self.pieces),
            [(shape, HALF, whole(shape))] * self.depth,
            after=after,
        )
        self.mark = pieces[:1]
        self.pieces = [swap(a, "batch", 2 * number) for number, a in enumerate(pieces)]

    def last(self, after=()):
        shape = (self.rows, self.width)
        outs = [(shape, HALF, whole(shape))]
        (total,) = run(last_body, "sum_last", (1,), [], plain(self.pieces), outs, after=after)
        self.mark = [total]
        self.pieces = [swap(total, "win", number) for number in range(self.win)]

    def unpack(self, layout, shapes, after=()):
        return run(
            functools.partial(
                unpack_body, pieces=self.win, across=self.across, layout=layout
            ),
            "unpack",
            (1,),
            [self.place],
            plain(self.pieces),
            [(s, FLOAT, whole(s)) for s in shapes],
            scratch=[pltpu.VMEM((2, self.rows, CHUNK), FLOAT)],
            after=after,
        )


SMALL_ROWS = 16


def small_tiles(core, sums, batch):
    blocks = len(sums)
    sums = jnp.stack(sums)[:, :, 0]
    vectors = sums[:, :6].reshape(blocks, 6, batch, -1).transpose(2, 0, 1, 3).reshape(batch, blocks, -1)
    lifts = sums[:, LIFT:].reshape(blocks, batch, -1).swapaxes(0, 1)
    pad = lambda a: jnp.pad(a, ((0, 0), (0, SMALL_ROWS - blocks), (0, CHUNK - a.shape[2])))
    both = [pad(a).astype(HALF)[None] for a in (vectors, lifts)]
    return jnp.where(core == 0, both[1], both[0]), jnp.where(core == 0, both[0], both[1])


ENTRY_TILES = [(NORMED, TRIPLE_BACK + part) for part in range(3)] + [(MIXED, ATTEND_BACK)]
WIDEN_TILES = [(SECOND, HIDDEN_BACK + chunk) for chunk in range(CHUNKS)]
TIME_TILES = WIDEN_TILES + ENTRY_TILES


def attend_places(rows, start):
    spot = lambda tile: (tile // 2, start + tile % 2 * rows, rows, 0, CHUNK)
    return [
        [(*spot(part), 0, part * CHUNK) for part in range(3)],
        [(*spot(3), 0, 0)],
    ], [(rows, 3 * D), (rows, D)]


def feed_places(rows, start):
    narrows = [(sub // 2, start + sub % 2 * rows, rows, 0, CHUNK, sub * rows, 0) for sub in range(4)]
    start += 2 * rows
    widens = [
        (chunk // 2, start + chunk % 2 * rows, rows, 0, CHUNK, 0, chunk * CHUNK) for chunk in range(CHUNKS)
    ]
    return [widens, narrows], [(rows, FF), (4 * rows, D)]


def small_places(rows, start):
    layout, shapes = [], []
    for block in range(2):
        layout += [[(0, start + block, 1, number * rows, rows, 0, 0)] for number in range(6)]
        layout.append([(1, start + block, 1, 0, 4 * rows, 0, 0)])
        shapes += [(1, rows)] * 6 + [(1, 4 * rows)]
    return layout, shapes


def local(*args):
    frames, cotangent, video_frames = args[0], args[23], args[24]
    space = [a.reshape(1, -1) if a.ndim == 1 else a for a in args[1:12]]
    time = [a.reshape(1, -1) if a.ndim == 1 else a for a in args[12:23]]
    batch, win = lax.axis_size("batch"), lax.axis_size("win")
    here, group = lax.axis_index("win"), lax.axis_index("batch")
    core = here % 2
    place = jnp.stack([here, here // 2, group % 2, group // 2, core]).astype(jnp.int32)
    _, per_group, _, windows, window, _ = frames.shape
    shape = (per_group, windows, window, D)
    rows_in, cotangent = frames.reshape(shape), cotangent.reshape(shape)
    rows = D // batch

    kept, came = [], []
    for half in range(HALVES):
        sent, kept = space_forward(place, rows_in, cotangent, space, half, win, kept)
        came.append(exchange(sent))
    lefts, triple, weights, middles, slopes = kept
    backs, slabs, time_sums = [], [], []
    for half in range(HALVES):
        sent, slabs, sums = time_block(place, video_frames, came[half], time, half, slabs)
        backs += exchange(sent)
        time_sums.append(sums)

    time_tiles = scattered_tiles(*slabs, BRANCH_BACK, TIME_TILES, batch, win, backs[1:win])
    time_total = lax.psum_scatter(time_tiles, ("batch", "win"), scatter_dimension=0, tiled=True)[0]
    outcome, feed_rights, middles_back, feed_sums = feed_back(
        place, shape, space, backs, middles, slopes, [time_tiles]
    )
    feed_tiles = [(SECOND, chunk) for chunk in range(CHUNKS)]
    narrow_away, narrow_own, away = gradient_tiles(
        core, lefts, feed_rights, CHUNKS, [(feed_tiles, 1 - core)], batch
    )
    (own,) = gradient_tiles(core, lefts, feed_rights, None, [(feed_tiles, core)], batch, [away])
    feed_sum = Reduction(place, [narrow_away, away], [narrow_own, own])
    feed_sum.cores()
    delta, attend_rights, attend_sums = attention_back(
        place, rows_in, space, triple, weights, middles_back, 2 * win, feed_sum.mark
    )
    attend_tiles = [(NORMED, part) for part in range(3)] + [(MIXED, 3)]
    (away,) = gradient_tiles(
        core, lefts, attend_rights, None, [(attend_tiles, 1 - core)], batch
    )
    feed_sum.chips([away])
    (own,) = gradient_tiles(
        core, lefts, attend_rights, None, [(attend_tiles, core)], batch, feed_sum.mark
    )
    small_away, small_own = small_tiles(core, [feed_sums + attend_sums, sum(time_sums)], batch)
    attend_sum = Reduction(place, [away, small_away], [own, small_own])
    attend_sum.cores()
    feed_sum.last(attend_sum.mark)
    attend_sum.chips(feed_sum.mark)
    feed_layout, feed_shapes = feed_places(rows, 0)
    feed_grads = feed_sum.unpack(feed_layout, feed_shapes, attend_sum.mark)
    attend_sum.last(feed_grads[:1])
    time_grads = spread_units(place, time_total, win, rows, attend_sum.mark)
    attend_layout, attend_shapes = attend_places(rows, 0)
    small_layout, small_shapes = small_places(rows, 2 * rows)
    attend_grads = attend_sum.unpack(
        attend_layout + small_layout, attend_shapes + small_shapes, time_grads[:1]
    )
    smalls = [a.reshape(-1) for a in attend_grads[2:]]

    def collected(grads, smalls):
        widen, narrow, entry, leave = grads
        gain, offset, bias, weigh, shift, nudge, lift = smalls
        return gain, offset, entry, leave, bias, weigh, shift, widen, lift, narrow, nudge

    return (
        outcome.reshape(frames.shape),
        delta.reshape(frames.shape),
        *collected([*feed_grads, *attend_grads[:2]], smalls[:7]),
        *collected(time_grads, smalls[7:]),
    )


def solution(mesh):
    rows = P("batch", None, "win", None, None, None)
    one, two = P("batch"), P("batch", None)
    grads = (one, one, two, two, one, one, one, two, one, two, one)
    return jax.shard_map(
        local,
        mesh=mesh,
        in_specs=(rows, *([P()] * 22), rows, P("batch", None)),
        out_specs=(rows, rows, *grads, *grads),
        check_vma=False,
    )
```

```python
import functools

import jax
import jax.numpy as jnp
from jax import lax
from jax.experimental import pallas as pl
from jax.experimental.pallas import tpu as pltpu
from jax.sharding import PartitionSpec as P

D = 512
HEADS = 8
HDIM = 64
FF = 2048
PAIR = 2 * HDIM
PAIRS = HEADS // 2
CHUNK = 512
CHUNKS = FF // CHUNK
EPS = 1e-05
NEGATIVE = -1e30
FLOAT = jnp.float32
HALF = jnp.bfloat16
HALVES = 2
UNITS = 16
VMEM = 62 << 20
SMALL_VMEM = 24 << 20
ARRIVED_FLOPS = 6 * 10**9
FIRST_FEED = 2
SMALL_FLOPS = 2 * 10**8
SLOWER = 4

NARROW, WIDEN, ENTRY, EXIT = 0, CHUNKS, 2 * CHUNKS, 2 * CHUNKS + 3
TILES = 2 * CHUNKS + 4
INNER, COTANGENT = 0, 1
BACK, RESULT = 0, 1
GAIN, OFFSET, BIAS, WEIGH, SHIFT, NUDGE, LIFT = 0, 1, 2, 3, 4, 5, 6
SUMS = 6 + CHUNKS


def dot(left, right):
    return lax.dot_general(left, right, (((1,), (0,)), ((), ())), preferred_element_type=FLOAT)


def dot_right(left, right):
    return lax.dot_general(left, right, (((1,), (1,)), ((), ())), preferred_element_type=FLOAT)


def dot_left(left, right):
    return lax.dot_general(left, right, (((0,), (0,)), ((), ())), preferred_element_type=FLOAT)


def unit_of(rows):
    centre = rows - jnp.mean(rows, axis=-1, keepdims=True)
    inverse = lax.rsqrt(jnp.mean(centre * centre, axis=-1, keepdims=True) + EPS)
    return centre * inverse, inverse


def norm_back(scaled, unit, inverse):
    return inverse * (
        scaled
        - jnp.mean(scaled, axis=-1, keepdims=True)
        - unit * jnp.mean(scaled * unit, axis=-1, keepdims=True)
    )


def gelu_pair(hidden):
    half = 0.5 * lax.erf(hidden * 0.7071067811865476) + 0.5
    bell = jnp.exp(hidden * hidden * -0.5) * 0.3989422804014327
    return hidden * half, half + hidden * bell


def gelu_of(hidden):
    return hidden * (0.5 * lax.erf(hidden * 0.7071067811865476) + 0.5)


def column_sum(values):
    return jnp.sum(values, axis=0, keepdims=True)


def first_head(rows):
    return lax.broadcasted_iota(jnp.int32, (rows, PAIR), 1) < HDIM


def spread(pair, first):
    zero = jnp.zeros_like(pair)
    return jnp.concatenate([jnp.where(first, pair, zero), jnp.where(first, zero, pair)], axis=0)


def gathered(both, first, rows):
    return jnp.where(first, both[:rows], both[rows:])


def attend_units(blocks):
    units = [(block, pair) for block in range(blocks) for pair in range(PAIRS)]
    return [units[start : start + UNITS] for start in range(0, len(units), UNITS)]


def columns(pair, part=0):
    start = part * D + pair * PAIR
    return slice(start, start + PAIR)


def attend_forward(triple, mixed, weights, blocks, rows, mask):
    first = first_head(rows)
    for units in attend_units(blocks):
        spans = [slice(block * rows, block * rows + rows) for block, _ in units]
        queries = [spread(triple[s, columns(p)], first) for s, (_, p) in zip(spans, units)]
        scores = [dot_right(triple[s, columns(p, 1)], q) for q, s, (_, p) in zip(queries, spans, units)]
        if mask is not None:
            scores = [score + mask for score in scores]
        powers = [
            jnp.exp((score - jnp.max(score, axis=0, keepdims=True)) * HDIM ** (-0.5)) for score in scores
        ]
        probs = [
            (power * (1.0 / jnp.sum(power, axis=0, keepdims=True))).astype(HALF) for power in powers
        ]
        both = [dot_left(prob, triple[s, columns(p, 2)]) for prob, s, (_, p) in zip(probs, spans, units)]
        for value, prob, s, (block, p) in zip(both, probs, spans, units):
            weights[block, p] = prob
            mixed[s, columns(p)] = gathered(value, first, rows).astype(HALF)


def attend_backward(triple, weights, mixed_back, put, blocks, rows):
    first = first_head(rows)
    scale = HDIM ** (-0.5)
    for units in attend_units(blocks):
        spans = [slice(block * rows, block * rows + rows) for block, _ in units]
        mixes = [spread(mixed_back[s, columns(p)], first) for s, (_, p) in zip(spans, units)]
        probs = [weights[block, p] for block, p in units]
        values_back = [dot(prob, mix) for prob, mix in zip(probs, mixes)]
        weights_back = [
            dot_right(triple[s, columns(p, 2)], mix) for mix, s, (_, p) in zip(mixes, spans, units)
        ]
        scores_back = []
        for prob, back in zip(probs, weights_back):
            wide = prob.astype(FLOAT)
            inside = back - jnp.sum(back * wide, axis=0, keepdims=True)
            scores_back.append((wide * inside * scale).astype(HALF))
        queries = [spread(triple[s, columns(p)], first) for s, (_, p) in zip(spans, units)]
        keys_back = [dot(score, query) for score, query in zip(scores_back, queries)]
        both = [
            dot_left(score, triple[s, columns(p, 1)])
            for score, s, (_, p) in zip(scores_back, spans, units)
        ]
        for key, value, pair, s, (_, p) in zip(keys_back, values_back, both, spans, units):
            put(s, p, 0, gathered(pair, first, rows).astype(HALF))
            put(s, p, 1, key.astype(HALF))
            put(s, p, 2, value.astype(HALF))


def whole(shape):
    return pl.BlockSpec(shape, lambda *_: (0,) * len(shape), pipeline_mode=pl.Buffered(1))


def run(body, name, grid, scalars, ins, outs, scratch=(), aliases=None, after=(), flops=0, moved=0, vmem=VMEM):
    aliases = aliases or {}
    anywhere = pl.BlockSpec(memory_space=pl.ANY)
    first = len(scalars) + len(ins)
    extra = [*aliases.values(), *after]

    def inner(*refs):
        body(*refs[:first], *refs[first + len(extra) :])

    return pl.pallas_call(
        inner,
        out_shape=[jax.ShapeDtypeStruct(shape, kind) for shape, kind, _ in outs],
        grid_spec=pltpu.PrefetchScalarGridSpec(
            num_scalar_prefetch=len(scalars),
            grid=grid,
            in_specs=[spec for _, spec in ins] + [anywhere] * len(extra),
            out_specs=[spec for _, _, spec in outs],
            scratch_shapes=list(scratch),
        ),
        input_output_aliases={first + at: out for at, out in enumerate(aliases)},
        compiler_params=pltpu.CompilerParams(vmem_limit_bytes=vmem),
        cost_estimate=pl.CostEstimate(flops=flops * SLOWER, bytes_accessed=moved * SLOWER, transcendentals=0),
        name=name,
    )(*scalars, *[array for array, _ in ins], *extra)


def plain(arrays):
    return [(array, whole(array.shape)) for array in arrays]


def slab_spec(slabs, rows, at):
    return pl.BlockSpec((slabs, rows, D), lambda *i: (0, at(*i), 0))


def row_spec(rows, width, at):
    return pl.BlockSpec((rows, width), lambda *i: (at(*i), 0))


def space_forward_body(place, rows_in, cotangent, *refs, window, pieces):
    gain, offset, entry, leave, bias, weigh, shift, widen, lift, narrow, nudge = refs[:11]
    sent = refs[11 : 11 + pieces]
    triple, weights, mixed, middles, hiddens = refs[11 + pieces :]
    step = pl.program_id(0)
    shape = rows_in.shape
    rows = rows_in[...].reshape(-1, D).astype(FLOAT)
    count = rows.shape[0]
    unit, _ = unit_of(rows)
    normed = (unit * gain[...] + offset[...]).astype(HALF)
    triple[...] = dot(normed, entry[...]).astype(HALF)
    attend_forward(triple, mixed, weights, count // window, window, None)
    middle = rows + dot(mixed[...], leave[...]) + bias[...]
    middles[...] = middle
    unit_two, _ = unit_of(middle)
    second = (unit_two * weigh[...] + shift[...]).astype(HALF)
    total = middle + nudge[...]
    for chunk in range(CHUNKS):
        at = slice(chunk * CHUNK, (chunk + 1) * CHUNK)
        hidden = dot(second, widen[:, at]) + lift[:, at]
        hiddens[:, at] = hidden.astype(HALF)
        total = total + dot(gelu_of(hidden).astype(HALF), narrow[at, :])
    inner = total.astype(HALF).reshape(shape)
    for piece in range(pieces):

        @pl.when(step == piece)
        def _(piece=piece):
            sent[piece][INNER] = inner
            sent[piece][COTANGENT] = cotangent[...]


def space_forward(place, frames, cotangent, params, half, pieces, before):
    per_group, windows, window, _ = frames.shape
    each = windows // pieces // HALVES
    block = (per_group, each, window, D)
    rows = per_group * each * window
    count = rows * pieces * HALVES
    cut = pl.BlockSpec(block, lambda i, place: (0, (place[0] ^ i) * HALVES + half, 0, 0))
    at = lambda i, place: half * pieces + i
    attended = (rows // window, PAIRS, window, 2 * window)
    both = (2, *block)
    outs = [(both, HALF, pl.BlockSpec(both, lambda i, place: (0,) * 5))] * pieces
    outs += [
        ((count, 3 * D), HALF, row_spec(rows, 3 * D, at)),
        (
            (count // window, *attended[1:]),
            HALF,
            pl.BlockSpec(attended, lambda i, place: (at(i, place), 0, 0, 0)),
        ),
        ((count, D), HALF, row_spec(rows, D, at)),
        ((count, D), FLOAT, row_spec(rows, D, at)),
        ((count, FF), HALF, row_spec(rows, FF, at)),
    ]
    made = run(
        functools.partial(space_forward_body, window=window, pieces=pieces),
        "space_forward",
        (pieces,),
        [place],
        [(frames, cut), (cotangent, cut)] + plain(params),
        outs,
        aliases={pieces + number: array for number, array in enumerate(before)},
        flops=2 * rows * pieces * D * (4 * D + 2 * FF),
        moved=rows * pieces * (8 * D + 12 * D + 2 * FF),
    )
    return made[:pieces], made[pieces:]


def by_position(refs, which, frames_of, positions):
    parts = [ref[which, frame].astype(FLOAT) for ref in refs for frame in range(frames_of)]
    return jnp.concatenate(
        [part[start : start + 8] for start in range(0, positions, 8) for part in parts], axis=0
    )


def by_frame(values, refs, which, frames_of, positions):
    total = len(refs) * frames_of
    for at, ref in enumerate(refs):
        for frame in range(frames_of):
            number = at * frames_of + frame
            ref[which, frame] = jnp.concatenate(
                [
                    values[(group * total + number) * 8 : (group * total + number) * 8 + 8]
                    for group in range(positions // 8)
                ],
                axis=0,
            ).astype(HALF)


def fill_mask(mask, place, lengths, per_group, pieces):
    window = mask.shape[0]
    key = lax.broadcasted_iota(jnp.int32, mask.shape, 0)
    query = lax.broadcasted_iota(jnp.int32, mask.shape, 1) % window
    frames = []
    for row in (query, key):
        number = row // 8
        frames.append((number % per_group) * pieces + ((number // per_group) ^ place[0]))
    videos = [jnp.zeros_like(frame) for frame in frames]
    entries = lengths.shape[1]
    end = 0
    for entry in range(entries):
        end = end + lengths[0, entry]
        videos = [v + (f >= end).astype(jnp.int32) for v, f in zip(videos, frames)]
    videos = [jnp.where(f < end, v, entries + f) for v, f in zip(videos, frames)]
    allowed = (videos[0] == videos[1]) & (frames[1] <= frames[0]) & (query % 8 == key % 8)
    mask[...] = jnp.where(allowed, 0.0, NEGATIVE)


def scatter_copies(tile, stage, out, sems):
    batch, _, units, rows, width = out.shape
    made = []
    for half in range(2):
        x = pl.ds(half * width, width)
        if tile < WIDEN:
            shards = batch // CHUNKS
            source = stage.at[tile].reshape(shards, 4, rows, CHUNK)
            for sub in range(4):
                unit = sub * 2 + half
                made.append((source.at[:, sub, :, x], out.at[pl.ds(tile * shards, shards), unit // units, unit % units]))
        else:
            unit = 8 + (tile - WIDEN) * 2 + half
            source = stage.at[tile].reshape(batch, rows, CHUNK)
            made.append((source.at[:, :, x], out.at[:, unit // units, unit % units]))
    return [
        pltpu.make_async_copy(source, target, sems.at[tile, number])
        for number, (source, target) in enumerate(made)
    ]


def time_body(place, lengths, *refs, pieces, last):
    came = refs[:pieces]
    gain, offset, entry, leave, bias, weigh, shift, widen, lift, narrow, nudge = refs[pieces : pieces + 11]
    refs = refs[pieces + 11 :]
    if last:
        partial, refs = refs[0], refs[1:]
    sent, refs = refs[:pieces], refs[pieces:]
    grads, sums, triple, weights, mixed, mixed_back, triple_back, mask, held, stage, sems = refs
    _, frames_of, positions, _ = came[0].shape
    window = 8 * pieces * frames_of
    rows = by_position(came, INNER, frames_of, positions)
    blocks = rows.shape[0] // window
    step = pl.program_id(0)

    @pl.when(step == 0)
    def _():
        sums[...] = jnp.zeros_like(sums)
        held[...] = jnp.zeros_like(held)
        fill_mask(mask, place, lengths, frames_of, pieces)
        if last:
            pltpu.make_async_copy(partial, stage, sems.at[0, 0]).start()

    unit, inverse = unit_of(rows)
    normed = (unit * gain[...] + offset[...]).astype(HALF)
    triple[...] = dot(normed, entry[...]).astype(HALF)
    attend_forward(triple, mixed, weights, blocks, window, mask[...])
    middle = rows + dot(mixed[...], leave[...]) + bias[...]
    unit_two, inverse_two = unit_of(middle)
    second = (unit_two * weigh[...] + shift[...]).astype(HALF)
    upstream = by_position(came, COTANGENT, frames_of, positions)
    branch_back = upstream.astype(HALF)
    sums[NUDGE] += column_sum(upstream)
    total = middle + nudge[...]
    second_back = jnp.zeros_like(middle)
    for chunk in range(CHUNKS):
        at = slice(chunk * CHUNK, (chunk + 1) * CHUNK)
        active, slope = gelu_pair(dot(second, widen[:, at]) + lift[:, at])
        active = active.astype(HALF)
        hidden_back = dot_right(branch_back, narrow[at, :]) * slope
        hidden_low = hidden_back.astype(HALF)
        sums[LIFT + chunk] += column_sum(hidden_back)
        total = total + dot(active, narrow[at, :])
        second_back = second_back + dot_right(hidden_low, widen[:, at])
        held[NARROW + chunk] += dot_left(active, branch_back)
        held[WIDEN + chunk] += dot_left(second, hidden_low)
    by_frame(total, sent, RESULT, frames_of, positions)
    sums[WEIGH] += column_sum(second_back * unit_two)
    sums[SHIFT] += column_sum(second_back)
    middle_back = upstream + norm_back(second_back * weigh[...], unit_two, inverse_two)
    attend_back = middle_back.astype(HALF)
    sums[BIAS] += column_sum(middle_back)
    mixed_back[...] = dot_right(attend_back, leave[...]).astype(HALF)
    held[EXIT] += dot_left(mixed[...], attend_back)

    def put(span, pair, part, value):
        triple_back[part, span, columns(pair)] = value

    attend_backward(triple, weights, mixed_back, put, blocks, window)
    normed_back = jnp.zeros_like(middle)
    for part in range(3):
        back = triple_back[part]
        normed_back = normed_back + dot_right(back, entry[:, part * D : (part + 1) * D])
        held[ENTRY + part] += dot_left(normed, back)
    sums[GAIN] += column_sum(normed_back * unit)
    sums[OFFSET] += column_sum(normed_back)
    rows_back = middle_back + norm_back(normed_back * gain[...], unit, inverse)
    by_frame(rows_back, sent, BACK, frames_of, positions)

    @pl.when(step == pl.num_programs(0) - 1)
    def _():
        if last:
            pltpu.make_async_copy(partial, stage, sems.at[0, 0]).wait()
        copies = []
        for tile in range(TILES):
            value = held[tile]
            if last:
                value = value + stage[tile].astype(FLOAT)
            stage[tile] = value.astype(HALF)
            if last:
                made = scatter_copies(tile, stage, grads, sems)
            else:
                made = [pltpu.make_async_copy(stage.at[tile], grads.at[tile], sems.at[tile, 0])]
            for copy in made:
                copy.start()
            copies += made
        for copy in copies:
            copy.wait()


def time_block(place, lengths, came, params, batch, partial=None, step_rows=512):
    pieces = len(came)
    _, per_group, each, window, _ = came[0].shape
    positions = each * window
    flat = (2, per_group, positions, D)
    frames = per_group * pieces
    together = min(max(step_rows // frames, 16), positions)
    rows = together * frames
    steps = positions // together
    count = positions * frames
    attended = 8 * frames
    last = partial is not None
    anywhere = pl.BlockSpec(memory_space=pl.ANY)
    spec = pl.BlockSpec((2, per_group, together, D), lambda i, *_: (0, 0, i, 0))
    grads = (batch, pieces, 2 * TILES // pieces, D // batch, CHUNK // 2) if last else (TILES, CHUNK, CHUNK)
    outs = [(flat, HALF, spec)] * pieces
    outs += [(grads, HALF, anywhere), ((SUMS, 1, D), FLOAT, whole((SUMS, 1, D)))]
    ins = [(array.reshape(flat), spec) for array in came] + plain(params)
    if last:
        ins.append((partial, anywhere))
    made = run(
        functools.partial(time_body, pieces=pieces, last=last),
        "time_block",
        (steps,),
        [place, lengths],
        ins,
        outs,
        scratch=[
            pltpu.VMEM((rows, 3 * D), HALF),
            pltpu.VMEM((rows // attended, PAIRS, attended, 2 * attended), HALF),
            pltpu.VMEM((rows, D), HALF),
            pltpu.VMEM((rows, D), HALF),
            pltpu.VMEM((3, rows, D), HALF),
            pltpu.VMEM((attended, 2 * attended), FLOAT),
            pltpu.VMEM((TILES, CHUNK, CHUNK), FLOAT),
            pltpu.VMEM((TILES, CHUNK, CHUNK), HALF),
            pltpu.SemaphoreType.DMA((TILES, 8)),
        ],
        flops=6 * count * D * (4 * D + 2 * FF),
        moved=count * 2 * D * 4 + 2 * D * (4 * D + 2 * FF),
    )
    shape = (2, per_group, each, window, D)
    sent = [array.reshape(shape) for array in made[:pieces]]
    return sent, made[pieces], made[pieces + 1]


def side_by_side(refs, index=slice(None)):
    return jnp.concatenate([ref[index] for ref in refs], axis=0)


def pick(core, away, own, tiles):
    size = len(tiles) // 2
    for number in range(size):
        one, two = tiles[number], tiles[size + number]
        own[number] = jnp.where(core == 0, one, two).reshape(own.shape[1:])
        away[number] = jnp.where(core == 0, two, one).reshape(away.shape[1:])


def feed_back_body(place, weigh, shift, widen, narrow, *refs, arrays, steps, last):
    came, refs = refs[:arrays], refs[arrays:]
    middles, hiddens, refs = refs[:2], refs[2:4], refs[4:]
    if last:
        partial, refs = refs[0], refs[1:]
    middles_back, refs = refs[0], refs[1:]
    if last:
        narrow_away, narrow_own, away, own, sums, arrived, held, sems, stage, stage_sem = refs
    else:
        tiles, sums, arrived, held, sems = refs
    step = pl.program_id(0)

    def coming(number):
        return [
            pltpu.make_async_copy(
                came[number * 2 + side].at[BACK], arrived.at[number % 2, side], sems.at[number % 2, side]
            )
            for side in range(2)
        ]

    @pl.when(step == 0)
    def _():
        for copy in coming(0):
            copy.start()
        if last:
            pltpu.make_async_copy(partial, stage, stage_sem).start()
        sums[...] = jnp.zeros_like(sums)
        held[...] = jnp.zeros_like(held)

    for number in range(steps):

        @pl.when(step == number)
        def _(number=number):
            for copy in coming(number):
                copy.wait()
            if number + 1 < steps:
                for copy in coming(number + 1):
                    copy.start()

    branch_back = arrived[step % 2].reshape(-1, D)
    upstream = branch_back.astype(FLOAT)
    unit_two, inverse_two = unit_of(side_by_side(middles))
    second = (unit_two * weigh[...] + shift[...]).astype(HALF)
    sums[NUDGE] += column_sum(upstream)
    second_back = jnp.zeros_like(upstream)
    for chunk in range(CHUNKS):
        at = slice(chunk * CHUNK, (chunk + 1) * CHUNK)
        active, slope = gelu_pair(side_by_side(hiddens, (slice(None), at)).astype(FLOAT))
        hidden_back = dot_right(branch_back, narrow[at, :]) * slope
        hidden_low = hidden_back.astype(HALF)
        sums[LIFT + chunk] += column_sum(hidden_back)
        second_back = second_back + dot_right(hidden_low, widen[:, at])
        held[NARROW + chunk] += dot_left(active.astype(HALF), branch_back)
        held[WIDEN + chunk] += dot_left(second, hidden_low)
    sums[WEIGH] += column_sum(second_back * unit_two)
    sums[SHIFT] += column_sum(second_back)
    middle_back = upstream + norm_back(second_back * weigh[...], unit_two, inverse_two)
    middles_back[...] = middle_back
    sums[BIAS] += column_sum(middle_back)

    @pl.when(step == steps - 1)
    def _():
        if not last:
            tiles[...] = held[...].astype(HALF)
            return
        pltpu.make_async_copy(partial, stage, stage_sem).wait()
        value = lambda tile: (held[tile] + stage[tile].astype(FLOAT)).astype(HALF)
        pick(place[4], away, own, [value(WIDEN + chunk) for chunk in range(CHUNKS)])
        _, batch, rows, _ = narrow_own.shape
        shards = batch // CHUNKS
        for chunk in range(CHUNKS):
            parts = value(NARROW + chunk).reshape(shards, 4, rows, CHUNK)
            at = pl.ds(chunk * shards, shards)
            pick(place[4], narrow_away.at[:, at], narrow_own.at[:, at], [parts[:, sub] for sub in range(4)])


def feed_back(place, params, came, middles, hiddens, batch, before=None, after=()):
    pieces = len(came[0])
    part = came[0][0].shape[1:]
    count = middles.shape[0]
    rows = count // (pieces * HALVES)
    last = before is not None
    pairs = [((0, 0), (1, 0)), ((0, 1), (1, 1))] + [((0, k), (0, k + 1)) for k in range(2, pieces, 2)]
    start = len(pairs) if last else 0
    if last:
        pairs = [((1, k), (1, k + 1)) for k in range(2, pieces, 2)]
    steps = len(pairs)
    numbers = [[half * pieces + piece for half, piece in side] for side in zip(*pairs)]
    tables = [jnp.array(side, jnp.int32) for side in numbers]
    block_of = lambda width, side: pl.BlockSpec((rows, width), lambda i, place, *tables: (tables[side][i], 0))
    ins = plain([params[5], params[6], params[7], params[9]])
    ins += [(came[half][piece], pl.BlockSpec(memory_space=pl.ANY)) for pair in pairs for half, piece in pair]
    ins += [(middles, block_of(D, side)) for side in range(2)]
    ins += [(hiddens, block_of(FF, side)) for side in range(2)]
    scratch = [
        pltpu.VMEM((2, 2, *part), HALF),
        pltpu.VMEM((2 * CHUNKS, CHUNK, CHUNK), FLOAT),
        pltpu.SemaphoreType.DMA((2, 2)),
    ]
    outs = [((count, D), FLOAT, row_spec(2 * rows, D, lambda i, *_: start + i))]
    aliases = {}
    if last:
        aliases = {0: before[0]}
        ins.append((before[1], pl.BlockSpec(memory_space=pl.ANY)))
        tiles = (2, batch, D // batch, CHUNK)
        outs += [(tiles, HALF, whole(tiles))] * 4
        scratch += [pltpu.VMEM((2 * CHUNKS, CHUNK, CHUNK), HALF), pltpu.SemaphoreType.DMA]
    else:
        tiles = (2 * CHUNKS, CHUNK, CHUNK)
        outs.append((tiles, HALF, whole(tiles)))
    outs.append(((SUMS, 1, D), FLOAT, whole((SUMS, 1, D))))
    body = functools.partial(feed_back_body, arrays=2 * steps, steps=steps, last=last)
    return run(
        lambda place, one, two, *refs: body(place, *refs),
        "feed_back",
        (steps,),
        [place, *tables],
        ins,
        outs,
        scratch=scratch,
        aliases=aliases,
        after=after,
        flops=16 * rows * steps * D * FF * (1 if last else FIRST_FEED),
        moved=2 * rows * steps * (10 * D + 2 * FF) + 8 * D * FF,
    )


def attention_back_body(place, rows_in, gain, offset, entry, leave, *refs, window, pieces):
    came, refs = refs[: HALVES * pieces], refs[HALVES * pieces :]
    triples, weights, mixes, middles_back = [refs[HALVES * k : HALVES * (k + 1)] for k in range(4)]
    delta, outcome, away, own, sums, mixed_back, triple_back, held, sems = refs[4 * HALVES :]
    step = pl.program_id(0)
    each = rows_in.shape[1] // HALVES

    def results(piece):
        return [
            pltpu.make_async_copy(
                came[half * pieces + piece].at[RESULT],
                outcome.at[:, pl.ds(half * each, each)],
                sems.at[half],
            )
            for half in range(HALVES)
        ]

    @pl.when(step == 0)
    def _():
        sums[...] = jnp.zeros_like(sums)
        held[...] = jnp.zeros_like(held)

    for piece in range(pieces):

        @pl.when(step == piece)
        def _(piece=piece):
            for copy in results(piece):
                copy.start()

    parts = [rows_in[:, half * each : (half + 1) * each].reshape(-1, D) for half in range(HALVES)]
    count = parts[0].shape[0]
    middle_back = side_by_side(middles_back)
    attend_back = middle_back.astype(HALF)
    mixed_back[...] = dot_right(attend_back, leave[...]).astype(HALF)
    held[3] += dot_left(side_by_side(mixes), attend_back)
    unit, inverse = unit_of(jnp.concatenate(parts, axis=0).astype(FLOAT))
    normed = (unit * gain[...] + offset[...]).astype(HALF)
    for half in range(HALVES):
        span = pl.ds(half * count, count)
        back = triple_back.at[:, span]

        def put(rows, pair, part, value, back=back):
            back[part, rows, columns(pair)] = value

        attend_backward(triples[half], weights[half], mixed_back.at[span], put, count // window, window)
    normed_back = jnp.zeros_like(middle_back)
    for part in range(3):
        back = triple_back[part]
        normed_back = normed_back + dot_right(back, entry[:, part * D : (part + 1) * D])
        held[part] += dot_left(normed, back)
    sums[GAIN] += column_sum(normed_back * unit)
    sums[OFFSET] += column_sum(normed_back)
    rows_back = (middle_back + norm_back(normed_back * gain[...], unit, inverse)).astype(HALF)
    for half in range(HALVES):
        delta[:, half * each : (half + 1) * each] = rows_back[half * count : (half + 1) * count].reshape(
            -1, each, window, D
        )

    @pl.when(step == pl.num_programs(0) - 1)
    def _():
        pick(place[4], away, own, [held[tile].astype(HALF) for tile in range(4)])

    for piece in range(pieces):

        @pl.when(step == piece)
        def _(piece=piece):
            for copy in results(piece):
                copy.wait()


def attention_back(place, frames, params, came, triple, weights, mixed, middles_back, batch, after):
    pieces = len(came[0])
    per_group, windows, window, _ = frames.shape
    block = (per_group, windows // pieces, window, D)
    rows = per_group * block[1] * window // HALVES
    cut = pl.BlockSpec(block, lambda i, place: (0, place[0] ^ i, 0, 0))
    attended = (rows // window, PAIRS, window, 2 * window)
    halves = range(HALVES)
    spread_out = lambda half: lambda i, place: jnp.where(i < 2, 2 * i + half, i + (pieces if half else 2))
    ins = [(frames, cut)] + plain(params[:4])
    ins += [(array, pl.BlockSpec(memory_space=pl.ANY)) for half in came for array in half]
    ins += [(triple, row_spec(rows, 3 * D, lambda i, place, h=h: h * pieces + i)) for h in halves]
    ins += [
        (weights, pl.BlockSpec(attended, lambda i, place, h=h: (h * pieces + i, 0, 0, 0))) for h in halves
    ]
    ins += [(mixed, row_spec(rows, D, lambda i, place, h=h: h * pieces + i)) for h in halves]
    ins += [(middles_back, row_spec(rows, D, spread_out(h))) for h in halves]
    tiles = (2, batch, D // batch, CHUNK)
    count = rows * pieces * HALVES
    return run(
        functools.partial(attention_back_body, window=window, pieces=pieces),
        "attention_back",
        (pieces,),
        [place],
        ins,
        [
            (frames.shape, HALF, cut),
            (frames.shape, HALF, cut),
            *[(tiles, HALF, whole(tiles))] * 2,
            ((SUMS, 1, D), FLOAT, whole((SUMS, 1, D))),
        ],
        scratch=[
            pltpu.VMEM((rows * HALVES, D), HALF),
            pltpu.VMEM((3, rows * HALVES, D), HALF),
            pltpu.VMEM((4, CHUNK, CHUNK), FLOAT),
            pltpu.SemaphoreType.DMA((HALVES,)),
        ],
        after=after,
        flops=16 * count * D * D,
        moved=count * D * 2 * (3 + 1 + 1 + 2 + 2 + 4),
    )


def swap(value, axis, mask):
    size = lax.axis_size(axis)
    if mask == 0:
        return value
    return lax.ppermute(value, axis, [(i, i ^ mask) for i in range(size)])


def move(value, batch_mask, win_mask):
    if batch_mask == 0:
        return swap(value, "win", win_mask)
    if win_mask == 0:
        return swap(value, "batch", batch_mask)
    batch, win = lax.axis_size("batch"), lax.axis_size("win")
    pairs = [
        (b * win + w, (b ^ batch_mask) * win + (w ^ win_mask)) for b in range(batch) for w in range(win)
    ]
    return lax.ppermute(value, ("batch", "win"), pairs)


def exchange(arrays):
    made = {k: swap(arrays[k], "win", k) for k in reversed(range(len(arrays)))}
    return [made[k] for k in range(len(arrays))]


def split_body(place, *refs, groups, across):
    own, got, outs = refs[:groups], refs[groups : 2 * groups], refs[2 * groups :]
    column, row = place[1], place[2]
    width = CHUNK // across
    at = 0
    for one, two in zip(own, got):
        rows = one.shape[3]
        for tile in range(one.shape[0]):
            for piece, out in enumerate(outs):
                y = row ^ (piece % 2)
                x = pl.ds(pl.multiple_of((column ^ (piece // 2)) * width, width), width)
                total = one[tile, :, y, :, x].astype(FLOAT) + two[tile, :, y, :, x].astype(FLOAT)
                out[:, at : at + rows] = total.astype(HALF)
            at += rows


def merge_body(place, *refs, inputs):
    ins, outs = refs[:inputs], refs[inputs:]
    for piece, out in enumerate(outs):
        z = place[3] ^ piece
        total = ins[0][z].astype(FLOAT)
        for ref in ins[1:]:
            total = total + ref[z].astype(FLOAT)
        out[...] = total.astype(HALF)


def last_body(*refs):
    ins, out = refs[:-1], refs[-1]
    total = ins[0][...].astype(FLOAT)
    for ref in ins[1:]:
        total = total + ref[...].astype(FLOAT)
    out[...] = total.astype(HALF)


def unpack_body(place, *refs, pieces, across, layout):
    ins, outs, held = refs[:pieces], refs[pieces:-1], refs[-1]
    width = CHUNK // across
    for piece, ref in enumerate(ins):
        x = pl.ds(pl.multiple_of((place[1] ^ (piece // 2)) * width, width), width)
        held[place[4] ^ (piece % 2), :, x] = ref[...].astype(FLOAT)
    for out, places in zip(outs, layout):
        for core, start, rows, left, wide, row, column in places:
            out[row : row + rows, column : column + wide] = held[
                core, start : start + rows, left : left + wide
            ]


def arrived_body(*refs):
    refs[-1][...] = jnp.zeros_like(refs[-1])


def arrived(arrays):
    shape = (8, 128)
    outs = [(shape, FLOAT, whole(shape))]
    return run(
        arrived_body, "arrived", (1,), [], [], outs, after=arrays, flops=ARRIVED_FLOPS, vmem=SMALL_VMEM
    )


class Reduction:
    def __init__(self, place, away, own):
        self.place = place
        self.batch, self.win = lax.axis_size("batch"), lax.axis_size("win")
        self.across, self.depth = self.win // 2, self.batch // 2
        cut = lambda a: a.reshape(-1, self.depth, 2, *a.shape[2:])
        self.own = [cut(a) for a in own]
        self.got = [swap(cut(a), "win", 1) for a in away]
        self.rows = sum(a.shape[0] * a.shape[3] for a in self.own)
        self.width = CHUNK // self.across

    def cores(self, after=()):
        shape = (self.depth, self.rows, self.width)
        pieces = run(
            functools.partial(split_body, groups=len(self.own), across=self.across),
            "sum_cores",
            (1,),
            [self.place],
            plain(self.own + self.got),
            [(shape, HALF, whole(shape))] * (2 * self.across),
            after=after,
            vmem=SMALL_VMEM,
            flops=SMALL_FLOPS,
        )
        self.mark = pieces[:1]
        self.pieces = [move(a, number % 2, 2 * (number // 2)) for number, a in enumerate(pieces)]

    def chips(self, after=(), flops=SMALL_FLOPS):
        shape = (self.rows, self.width)
        pieces = run(
            functools.partial(merge_body, inputs=len(self.pieces)),
            "sum_chips",
            (1,),
            [self.place],
            plain(self.pieces),
            [(shape, HALF, whole(shape))] * self.depth,
            after=after,
            vmem=SMALL_VMEM,
            flops=flops,
        )
        self.mark = pieces[:1]
        self.pieces = [swap(a, "batch", 2 * number) for number, a in enumerate(pieces)]

    def last(self, after=()):
        shape = (self.rows, self.width)
        outs = [(shape, HALF, whole(shape))]
        (total,) = run(last_body, "sum_last", (1,), [], plain(self.pieces), outs, after=after, vmem=SMALL_VMEM, flops=SMALL_FLOPS)
        self.mark = [total]
        self.pieces = [swap(total, "win", number) for number in range(self.win)]

    def unpack(self, layout, shapes, after=()):
        return run(
            functools.partial(
                unpack_body, pieces=self.win, across=self.across, layout=layout
            ),
            "unpack",
            (1,),
            [self.place],
            plain(self.pieces),
            [(s, FLOAT, whole(s)) for s in shapes],
            scratch=[pltpu.VMEM((2, self.rows, CHUNK), FLOAT)],
            after=after,
            vmem=SMALL_VMEM,
            flops=SMALL_FLOPS,
        )


def spread_body(place, *refs, pieces, layout):
    ins, outs, held = refs[:pieces], refs[pieces:-1], refs[-1]
    for piece, ref in enumerate(ins):
        held[place[0] ^ piece] = ref[...].astype(FLOAT)
    units = held.shape[1]
    rows, width = held.shape[2:]
    for out, places in zip(outs, layout):
        for unit, row, column in places:
            out[row * rows : (row + 1) * rows, column * width : (column + 1) * width] = held[
                unit // units, unit % units
            ]


def spread_units(place, total, win, rows, after=()):
    units = total.shape[0] // rows
    width = total.shape[1]
    pieces = [swap(total, "win", number).reshape(units, rows, width) for number in range(win)]
    spot = lambda tile, row, column: [(8 + tile * 2 + half, row, column * 2 + half) for half in range(2)]
    narrow = [(sub * 2 + half, sub, half) for sub in range(4) for half in range(2)]
    layout = [
        sum([spot(chunk, 0, chunk) for chunk in range(CHUNKS)], []),
        narrow,
        sum([spot(CHUNKS + part, 0, part) for part in range(3)], []),
        spot(CHUNKS + 3, 0, 0),
    ]
    shapes = [(rows, FF), (4 * rows, D), (rows, 3 * D), (rows, D)]
    return run(
        functools.partial(spread_body, pieces=win, layout=layout),
        "spread_units",
        (1,),
        [place],
        plain(pieces),
        [(s, FLOAT, whole(s)) for s in shapes],
        scratch=[pltpu.VMEM((win, units, rows, width), FLOAT)],
        after=after,
            vmem=SMALL_VMEM,
            flops=SMALL_FLOPS,
    )


SMALL_ROWS = 16


def small_tiles(core, sums, batch):
    blocks = len(sums)
    sums = jnp.stack(sums)[:, :, 0]
    vectors = sums[:, :6].reshape(blocks, 6, batch, -1).transpose(2, 0, 1, 3).reshape(batch, blocks, -1)
    lifts = sums[:, LIFT:].reshape(blocks, batch, -1).swapaxes(0, 1)
    pad = lambda a: jnp.pad(a, ((0, 0), (0, SMALL_ROWS - blocks), (0, CHUNK - a.shape[2])))
    both = [pad(a).astype(HALF)[None] for a in (vectors, lifts)]
    return jnp.where(core == 0, both[1], both[0]), jnp.where(core == 0, both[0], both[1])


def attend_places(rows, start):
    spot = lambda tile: (tile // 2, start + tile % 2 * rows, rows, 0, CHUNK)
    return [
        [(*spot(part), 0, part * CHUNK) for part in range(3)],
        [(*spot(3), 0, 0)],
    ], [(rows, 3 * D), (rows, D)]


def feed_places(rows, start):
    narrows = [(sub // 2, start + sub % 2 * rows, rows, 0, CHUNK, sub * rows, 0) for sub in range(4)]
    start += 2 * rows
    widens = [
        (chunk // 2, start + chunk % 2 * rows, rows, 0, CHUNK, 0, chunk * CHUNK) for chunk in range(CHUNKS)
    ]
    return [widens, narrows], [(rows, FF), (4 * rows, D)]


def small_places(rows, start):
    layout, shapes = [], []
    for block in range(2):
        layout += [[(0, start + block, 1, number * rows, rows, 0, 0)] for number in range(6)]
        layout.append([(1, start + block, 1, 0, 4 * rows, 0, 0)])
        shapes += [(1, rows)] * 6 + [(1, 4 * rows)]
    return layout, shapes


def local(*args):
    frames, cotangent, video_frames = args[0], args[23], args[24]
    space = [a.reshape(1, -1) if a.ndim == 1 else a for a in args[1:12]]
    time = [a.reshape(1, -1) if a.ndim == 1 else a for a in args[12:23]]
    batch, win = lax.axis_size("batch"), lax.axis_size("win")
    here, group = lax.axis_index("win"), lax.axis_index("batch")
    core = here % 2
    place = jnp.stack([here, here // 2, group % 2, group // 2, core]).astype(jnp.int32)
    _, per_group, _, windows, window, _ = frames.shape
    shape = (per_group, windows, window, D)
    rows_in, cotangent = frames.reshape(shape), cotangent.reshape(shape)
    rows = D // batch

    kept, came = [], []
    for half in range(HALVES):
        sent, kept = space_forward(place, rows_in, cotangent, space, half, win, kept)
        came.append(exchange(sent))
    triple, weights, mixed, middles, hiddens = kept
    backs, time_sums, tiles = [], [], None
    for half in range(HALVES):
        sent, tiles, sums = time_block(place, video_frames, came[half], time, batch, tiles)
        backs.append(exchange(sent))
        time_sums.append(sums)

    time_tiles = tiles.reshape(batch * win, -1, CHUNK // 2)
    time_total = lax.psum_scatter(time_tiles, ("batch", "win"), scatter_dimension=0, tiled=True)[0]
    mark = [*arrived(backs[0][1:]), tiles]
    *fed, first_sums = feed_back(place, space, backs, middles, hiddens, batch, after=mark)
    middles_back, narrow_away, narrow_own, away, own, feed_sums = feed_back(
        place, space, backs, middles, hiddens, batch, fed
    )
    feed_sum = Reduction(place, [narrow_away, away], [narrow_own, own])
    feed_sum.cores()
    delta, outcome, away, own, attend_sums = attention_back(
        place, rows_in, space, backs, triple, weights, mixed, middles_back, batch, feed_sum.mark
    )
    small_away, small_own = small_tiles(
        core, [first_sums + feed_sums + attend_sums, sum(time_sums)], batch
    )
    attend_sum = Reduction(place, [away, small_away], [own, small_own])
    feed_sum.chips([delta], 10 * SMALL_FLOPS)
    attend_sum.cores(feed_sum.mark)
    feed_sum.last(attend_sum.mark)
    attend_sum.chips(feed_sum.mark)
    feed_layout, feed_shapes = feed_places(rows, 0)
    feed_grads = feed_sum.unpack(feed_layout, feed_shapes, attend_sum.mark)
    attend_sum.last(feed_grads[:1])
    time_grads = spread_units(place, time_total, win, rows, attend_sum.mark)
    attend_layout, attend_shapes = attend_places(rows, 0)
    small_layout, small_shapes = small_places(rows, 2 * rows)
    attend_grads = attend_sum.unpack(
        attend_layout + small_layout, attend_shapes + small_shapes, time_grads[:1]
    )
    smalls = [a.reshape(-1) for a in attend_grads[2:]]

    def collected(grads, smalls):
        widen, narrow, entry, leave = grads
        gain, offset, bias, weigh, shift, nudge, lift = smalls
        return gain, offset, entry, leave, bias, weigh, shift, widen, lift, narrow, nudge

    return (
        outcome.reshape(frames.shape),
        delta.reshape(frames.shape),
        *collected([*feed_grads, *attend_grads[:2]], smalls[:7]),
        *collected(time_grads, smalls[7:]),
    )


def solution(mesh):
    rows = P("batch", None, "win", None, None, None)
    one, two = P("batch"), P("batch", None)
    grads = (one, one, two, two, one, one, one, two, one, two, one)
    return jax.shard_map(
        local,
        mesh=mesh,
        in_specs=(rows, *([P()] * 22), rows, P("batch", None)),
        out_specs=(rows, rows, *grads, *grads),
        check_vma=False,
    )
```

```python
import functools

import jax
import jax.numpy as jnp
from jax import lax
from jax.experimental import pallas as pl
from jax.experimental.pallas import tpu as pltpu
from jax.sharding import PartitionSpec as P

D = 512
HEADS = 8
HDIM = 64
FF = 2048
PAIR = 2 * HDIM
PAIRS = HEADS // 2
CHUNK = 512
CHUNKS = FF // CHUNK
EPS = 1e-05
NEGATIVE = -1e30
FLOAT = jnp.float32
HALF = jnp.bfloat16
HALVES = 2
UNITS = 16
VMEM = 127 << 19
SMALL_VMEM = 24 << 20
LONG_FLOPS = 10**11
SMALL_FLOPS = 2 * 10**8
SLOWER = 4

NARROW, WIDEN, ENTRY, EXIT = 0, CHUNKS, 2 * CHUNKS, 2 * CHUNKS + 3
TILES = 2 * CHUNKS + 4
SHARED = [WIDEN, WIDEN + 1, ENTRY, ENTRY + 1, WIDEN + 2, WIDEN + 3, ENTRY + 2, EXIT]
INNER, COTANGENT = 0, 1
BACK, RESULT = 0, 1
GAIN, OFFSET, BIAS, WEIGH, SHIFT, NUDGE, LIFT = 0, 1, 2, 3, 4, 5, 6
SUMS = 6 + CHUNKS


def dot(left, right):
    return lax.dot_general(left, right, (((1,), (0,)), ((), ())), preferred_element_type=FLOAT)


def dot_right(left, right):
    return lax.dot_general(left, right, (((1,), (1,)), ((), ())), preferred_element_type=FLOAT)


def dot_left(left, right):
    return lax.dot_general(left, right, (((0,), (0,)), ((), ())), preferred_element_type=FLOAT)


def unit_of(rows):
    centre = rows - jnp.mean(rows, axis=-1, keepdims=True)
    inverse = lax.rsqrt(jnp.mean(centre * centre, axis=-1, keepdims=True) + EPS)
    return centre * inverse, inverse


def norm_back(scaled, unit, inverse):
    return inverse * (
        scaled
        - jnp.mean(scaled, axis=-1, keepdims=True)
        - unit * jnp.mean(scaled * unit, axis=-1, keepdims=True)
    )


def gelu_pair(hidden):
    half = 0.5 * lax.erf(hidden * 0.7071067811865476) + 0.5
    bell = jnp.exp(hidden * hidden * -0.5) * 0.3989422804014327
    return hidden * half, half + hidden * bell


def gelu_of(hidden):
    return hidden * (0.5 * lax.erf(hidden * 0.7071067811865476) + 0.5)


def column_sum(values):
    return jnp.sum(values, axis=0, keepdims=True)


def first_head(rows):
    return lax.broadcasted_iota(jnp.int32, (rows, PAIR), 1) < HDIM


def spread(pair, first):
    zero = jnp.zeros_like(pair)
    return jnp.concatenate([jnp.where(first, pair, zero), jnp.where(first, zero, pair)], axis=0)


def gathered(both, first, rows):
    return jnp.where(first, both[:rows], both[rows:])


def attend_units(blocks):
    units = [(block, pair) for block in range(blocks) for pair in range(PAIRS)]
    return [units[start : start + UNITS] for start in range(0, len(units), UNITS)]


def columns(pair, part=0):
    start = part * D + pair * PAIR
    return slice(start, start + PAIR)


def attend_forward(triple, mixed, weights, blocks, rows, mask):
    first = first_head(rows)
    for units in attend_units(blocks):
        spans = [slice(block * rows, block * rows + rows) for block, _ in units]
        queries = [spread(triple[s, columns(p)], first) for s, (_, p) in zip(spans, units)]
        scores = [dot_right(triple[s, columns(p, 1)], q) for q, s, (_, p) in zip(queries, spans, units)]
        if mask is not None:
            scores = [score + mask for score in scores]
        powers = [
            jnp.exp((score - jnp.max(score, axis=0, keepdims=True)) * HDIM ** (-0.5)) for score in scores
        ]
        probs = [
            (power * (1.0 / jnp.sum(power, axis=0, keepdims=True))).astype(HALF) for power in powers
        ]
        both = [dot_left(prob, triple[s, columns(p, 2)]) for prob, s, (_, p) in zip(probs, spans, units)]
        for value, prob, s, (block, p) in zip(both, probs, spans, units):
            weights[block, p] = prob
            mixed[s, columns(p)] = gathered(value, first, rows).astype(HALF)


def attend_backward(triple, weights, mixed_back, put, blocks, rows):
    first = first_head(rows)
    scale = HDIM ** (-0.5)
    for units in attend_units(blocks):
        spans = [slice(block * rows, block * rows + rows) for block, _ in units]
        mixes = [spread(mixed_back[s, columns(p)], first) for s, (_, p) in zip(spans, units)]
        probs = [weights[block, p] for block, p in units]
        values_back = [dot(prob, mix) for prob, mix in zip(probs, mixes)]
        weights_back = [
            dot_right(triple[s, columns(p, 2)], mix) for mix, s, (_, p) in zip(mixes, spans, units)
        ]
        scores_back = []
        for prob, back in zip(probs, weights_back):
            wide = prob.astype(FLOAT)
            inside = back - jnp.sum(back * wide, axis=0, keepdims=True)
            scores_back.append((wide * inside * scale).astype(HALF))
        queries = [spread(triple[s, columns(p)], first) for s, (_, p) in zip(spans, units)]
        keys_back = [dot(score, query) for score, query in zip(scores_back, queries)]
        both = [
            dot_left(score, triple[s, columns(p, 1)])
            for score, s, (_, p) in zip(scores_back, spans, units)
        ]
        for key, value, pair, s, (_, p) in zip(keys_back, values_back, both, spans, units):
            put(s, p, 0, gathered(pair, first, rows).astype(HALF))
            put(s, p, 1, key.astype(HALF))
            put(s, p, 2, value.astype(HALF))


def whole(shape):
    return pl.BlockSpec(shape, lambda *_: (0,) * len(shape), pipeline_mode=pl.Buffered(1))


def run(body, name, grid, scalars, ins, outs, scratch=(), aliases=None, after=(), flops=0, moved=0, vmem=VMEM):
    aliases = aliases or {}
    unread = pl.BlockSpec(memory_space=pl.ANY)
    first = len(scalars) + len(ins)
    extra = [*aliases.values(), *after]

    def inner(*refs):
        body(*refs[:first], *refs[first + len(extra) :])

    return pl.pallas_call(
        inner,
        out_shape=[jax.ShapeDtypeStruct(shape, kind) for shape, kind, _ in outs],
        grid_spec=pltpu.PrefetchScalarGridSpec(
            num_scalar_prefetch=len(scalars),
            grid=grid,
            in_specs=[spec for _, spec in ins] + [unread] * len(extra),
            out_specs=[spec for _, _, spec in outs],
            scratch_shapes=list(scratch),
        ),
        input_output_aliases={first + at: out for at, out in enumerate(aliases)},
        compiler_params=pltpu.CompilerParams(vmem_limit_bytes=vmem),
        cost_estimate=pl.CostEstimate(flops=flops * SLOWER, bytes_accessed=moved * SLOWER, transcendentals=0),
        name=name,
    )(*scalars, *[array for array, _ in ins], *extra)


class Fetched:
    def __init__(self, sources, buffers, sems):
        self.copies = [
            pltpu.make_async_copy(source, buffer, sems.at[number])
            for number, (source, buffer) in enumerate(zip(sources, buffers))
        ]

    def start(self):
        for copy in self.copies:
            copy.start()

    def need(self, *numbers):
        @pl.when(pl.program_id(0) == 0)
        def _():
            for number in numbers:
                self.copies[number].wait()


def anywhere(arrays):
    return [(array, pl.BlockSpec(memory_space=pl.ANY)) for array in arrays]


def buffers_of(arrays):
    return [pltpu.VMEM(a.shape, a.dtype) for a in arrays] + [pltpu.SemaphoreType.DMA((len(arrays),))]


def plain(arrays):
    return [(array, whole(array.shape)) for array in arrays]


def slab_spec(slabs, rows, at):
    return pl.BlockSpec((slabs, rows, D), lambda *i: (0, at(*i), 0))


def row_spec(rows, width, at):
    return pl.BlockSpec((rows, width), lambda *i: (at(*i), 0))


def vectors_of(params):
    return [param for param in params if param.shape[0] == 1]


def weights_of(params):
    return [param for param in params if param.shape[0] > 1]


def space_forward_body(place, *refs, window, pieces):
    ins, cotangents, refs = refs[:2], refs[2:4], refs[4:]
    gain, offset, bias, weigh, shift, lift, nudge = refs[:7]
    sent = refs[11 : 11 + pieces]
    triple, weights, mixed, middles, hiddens, *buffers, sems = refs[11 + pieces :]
    entry, leave, widen, narrow = buffers
    fetched = Fetched(refs[7:11], buffers, sems)
    step = pl.program_id(0)

    @pl.when(step == 0)
    def _():
        fetched.start()

    shape = ins[0].shape
    rows = jnp.concatenate([ref[...].reshape(-1, D) for ref in ins], axis=0).astype(FLOAT)
    count = rows.shape[0]
    unit, _ = unit_of(rows)
    normed = (unit * gain[...] + offset[...]).astype(HALF)
    fetched.need(0)
    triple[...] = dot(normed, entry[...]).astype(HALF)
    attend_forward(triple, mixed, weights, count // window, window, None)
    fetched.need(1, 2, 3)
    middle = rows + dot(mixed[...], leave[...]) + bias[...]
    middles[...] = middle
    unit_two, _ = unit_of(middle)
    second = (unit_two * weigh[...] + shift[...]).astype(HALF)
    total = middle + nudge[...]
    for chunk in range(CHUNKS):
        at = slice(chunk * CHUNK, (chunk + 1) * CHUNK)
        hidden = dot(second, widen[:, at]) + lift[:, at]
        hiddens[:, at] = hidden.astype(HALF)
        total = total + dot(gelu_of(hidden).astype(HALF), narrow[at, :])
    inner = total.astype(HALF).reshape(2, *shape)
    for piece in range(pieces):

        @pl.when(step == piece // 2)
        def _(piece=piece):
            sent[piece][INNER] = inner[piece % 2]
            sent[piece][COTANGENT] = cotangents[piece % 2][...]


def space_forward(place, frames, cotangent, params, half, pieces, before):
    per_group, windows, window, _ = frames.shape
    each = windows // pieces // HALVES
    block = (per_group, each, window, D)
    rows = per_group * each * window
    count = rows * pieces * HALVES
    cuts = [
        pl.BlockSpec(block, lambda i, place, side=side: (0, (place[0] ^ (2 * i + side)) * HALVES + half, 0, 0))
        for side in range(2)
    ]
    rows *= 2
    at = lambda i, place: half * pieces // 2 + i
    attended = (rows // window, PAIRS, window, 2 * window)
    both = (2, *block)
    outs = [(both, HALF, pl.BlockSpec(both, lambda i, place: (0,) * 5))] * pieces
    outs += [
        ((count, 3 * D), HALF, row_spec(rows, 3 * D, at)),
        (
            (count // window, *attended[1:]),
            HALF,
            pl.BlockSpec(attended, lambda i, place: (at(i, place), 0, 0, 0)),
        ),
        ((count, D), HALF, row_spec(rows, D, at)),
        ((count, D), FLOAT, row_spec(rows, D, at)),
        ((count, FF), HALF, row_spec(rows, FF, at)),
    ]
    made = run(
        functools.partial(space_forward_body, window=window, pieces=pieces),
        "space_forward",
        (pieces // 2,),
        [place],
        [(a, cut) for a in (frames, cotangent) for cut in cuts] + plain(vectors_of(params)) + anywhere(weights_of(params)),
        outs,
        scratch=buffers_of(weights_of(params)),
        aliases={pieces + number: array for number, array in enumerate(before)},
        flops=rows * pieces * D * (4 * D + 2 * FF),
        moved=rows * pieces * (4 * D + 6 * D + FF),
    )
    return made[:pieces], made[pieces:]


def by_position(refs, which, frames_of, positions):
    parts = [ref[which, frame].astype(FLOAT) for ref in refs for frame in range(frames_of)]
    return jnp.concatenate(
        [part[start : start + 8] for start in range(0, positions, 8) for part in parts], axis=0
    )


def by_frame(values, refs, which, frames_of, positions):
    total = len(refs) * frames_of
    for at, ref in enumerate(refs):
        for frame in range(frames_of):
            number = at * frames_of + frame
            ref[which, frame] = jnp.concatenate(
                [
                    values[(group * total + number) * 8 : (group * total + number) * 8 + 8]
                    for group in range(positions // 8)
                ],
                axis=0,
            ).astype(HALF)


def fill_mask(mask, place, lengths, per_group, pieces):
    window = mask.shape[0]
    key = lax.broadcasted_iota(jnp.int32, mask.shape, 0)
    query = lax.broadcasted_iota(jnp.int32, mask.shape, 1) % window
    frames = []
    for row in (query, key):
        number = row // 8
        frames.append((number % per_group) * pieces + ((number // per_group) ^ place[0]))
    videos = [jnp.zeros_like(frame) for frame in frames]
    entries = lengths.shape[1]
    end = 0
    for entry in range(entries):
        end = end + lengths[0, entry]
        videos = [v + (f >= end).astype(jnp.int32) for v, f in zip(videos, frames)]
    videos = [jnp.where(f < end, v, entries + f) for v, f in zip(videos, frames)]
    allowed = (videos[0] == videos[1]) & (frames[1] <= frames[0]) & (query % 8 == key % 8)
    mask[...] = jnp.where(allowed, 0.0, NEGATIVE)


def shared_copies(tile, core, stage, away, own, sems):
    _, batch, rows, _ = own.shape
    made = []
    if tile < WIDEN:
        shards = batch // CHUNKS
        source = stage.at[tile].reshape(shards, 4, rows, CHUNK)
        at = pl.ds(tile * shards, shards)
        for sub in range(4):
            target = own if sub // 2 == core else away
            made.append((source.at[:, sub], target.at[sub % 2, at]))
    else:
        place = SHARED.index(tile)
        target = own if place // 4 == core else away
        made.append((stage.at[tile].reshape(batch, rows, CHUNK), target.at[2 + place % 4]))
    return [
        pltpu.make_async_copy(source, target, sems.at[tile, number])
        for number, (source, target) in enumerate(made)
    ]


def time_body(place, lengths, *refs, pieces, last):
    came = refs[:pieces]
    gain, offset, bias, weigh, shift, lift, nudge = refs[pieces : pieces + 7]
    entry, leave, widen, narrow, fetch_sems = refs[-5:]
    fetched = Fetched(refs[pieces + 7 : pieces + 11], [entry, leave, widen, narrow], fetch_sems)
    refs = refs[pieces + 11 : -5]
    if last:
        partial, refs = refs[0], refs[1:]
    sent, refs = refs[:pieces], refs[pieces:]
    grads, refs = refs[: 1 + last], refs[1 + last :]
    sums, triple, weights, mixed, mixed_back, triple_back, mask, held, stage, sems, came_sem = refs
    _, frames_of, positions, _ = came[0].shape
    window = 8 * pieces * frames_of
    rows = by_position(came, INNER, frames_of, positions)
    blocks = rows.shape[0] // window
    step = pl.program_id(0)

    @pl.when(step == 0)
    def _():
        fetched.start()
        sums[...] = jnp.zeros_like(sums)
        fill_mask(mask, place, lengths, frames_of, pieces)
        if last:
            pltpu.make_async_copy(partial, stage, came_sem).start()

    def each_copy(tile, act):
        if not last:
            act(pltpu.make_async_copy(stage.at[tile], grads[0].at[tile], sems.at[tile, 0]))
            return
        for core in range(2):

            @pl.when(place[4] == core)
            def _(core=core):
                for copy in shared_copies(tile, core, stage, *grads, sems):
                    act(copy)

    def done(tiles):
        @pl.when(step == pl.num_programs(0) - 1)
        def _():
            if last and tiles[0] == 0:
                pltpu.make_async_copy(partial, stage, came_sem).wait()
            for tile in tiles:
                value = held[tile]
                if last:
                    value = value + stage[tile].astype(FLOAT)
                stage[tile] = value.astype(HALF)
                each_copy(tile, lambda copy: copy.start())

    def add(tile, left, right):
        before = jnp.where(step == 0, 0.0, held[tile])
        held[tile] = before + dot_left(left, right)

    unit, inverse = unit_of(rows)
    normed = (unit * gain[...] + offset[...]).astype(HALF)
    fetched.need(0)
    triple[...] = dot(normed, entry[...]).astype(HALF)
    attend_forward(triple, mixed, weights, blocks, window, mask[...])
    fetched.need(1, 2, 3)
    middle = rows + dot(mixed[...], leave[...]) + bias[...]
    unit_two, inverse_two = unit_of(middle)
    second = (unit_two * weigh[...] + shift[...]).astype(HALF)
    upstream = by_position(came, COTANGENT, frames_of, positions)
    branch_back = upstream.astype(HALF)
    sums[NUDGE] += column_sum(upstream)
    total = middle + nudge[...]
    second_back = jnp.zeros_like(middle)
    for chunk in range(CHUNKS):
        at = slice(chunk * CHUNK, (chunk + 1) * CHUNK)
        active, slope = gelu_pair(dot(second, widen[:, at]) + lift[:, at])
        active = active.astype(HALF)
        hidden_back = dot_right(branch_back, narrow[at, :]) * slope
        hidden_low = hidden_back.astype(HALF)
        sums[LIFT + chunk] += column_sum(hidden_back)
        total = total + dot(active, narrow[at, :])
        second_back = second_back + dot_right(hidden_low, widen[:, at])
        add(NARROW + chunk, active, branch_back)
        add(WIDEN + chunk, second, hidden_low)
    done(range(ENTRY))
    by_frame(total, sent, RESULT, frames_of, positions)
    sums[WEIGH] += column_sum(second_back * unit_two)
    sums[SHIFT] += column_sum(second_back)
    middle_back = upstream + norm_back(second_back * weigh[...], unit_two, inverse_two)
    attend_back = middle_back.astype(HALF)
    sums[BIAS] += column_sum(middle_back)
    mixed_back[...] = dot_right(attend_back, leave[...]).astype(HALF)
    add(EXIT, mixed[...], attend_back)

    def put(span, pair, part, value):
        triple_back[part, span, columns(pair)] = value

    attend_backward(triple, weights, mixed_back, put, blocks, window)
    normed_back = jnp.zeros_like(middle)
    for part in range(3):
        back = triple_back[part]
        normed_back = normed_back + dot_right(back, entry[:, part * D : (part + 1) * D])
        add(ENTRY + part, normed, back)
    sums[GAIN] += column_sum(normed_back * unit)
    sums[OFFSET] += column_sum(normed_back)
    rows_back = middle_back + norm_back(normed_back * gain[...], unit, inverse)
    by_frame(rows_back, sent, BACK, frames_of, positions)

    done(range(ENTRY, TILES))

    @pl.when(step == pl.num_programs(0) - 1)
    def _():
        for tile in range(TILES):
            each_copy(tile, lambda copy: copy.wait())


def time_block(place, lengths, came, params, batch, partial=None, step_rows=512):
    pieces = len(came)
    _, per_group, each, window, _ = came[0].shape
    positions = each * window
    flat = (2, per_group, positions, D)
    frames = per_group * pieces
    together = min(max(step_rows // frames, 16), positions)
    rows = together * frames
    steps = positions // together
    count = positions * frames
    attended = 8 * frames
    last = partial is not None
    spec = pl.BlockSpec((2, per_group, together, D), lambda i, *_: (0, 0, i, 0))
    grads = (TILES // 2, batch, D // batch, CHUNK) if last else (TILES, CHUNK, CHUNK)
    outs = [(flat, HALF, spec)] * pieces
    outs += [(grads, HALF, pl.BlockSpec(memory_space=pl.ANY))] * (1 + last)
    outs += [((SUMS, 1, D), FLOAT, whole((SUMS, 1, D)))]
    ins = [(array.reshape(flat), spec) for array in came] + plain(vectors_of(params))
    ins += anywhere(weights_of(params))
    if last:
        ins += anywhere([partial])
    made = run(
        functools.partial(time_body, pieces=pieces, last=last),
        "time_block",
        (steps,),
        [place, lengths],
        ins,
        outs,
        scratch=[
            pltpu.VMEM((rows, 3 * D), HALF),
            pltpu.VMEM((rows // attended, PAIRS, attended, 2 * attended), HALF),
            pltpu.VMEM((rows, D), HALF),
            pltpu.VMEM((rows, D), HALF),
            pltpu.VMEM((3, rows, D), HALF),
            pltpu.VMEM((attended, 2 * attended), FLOAT),
            pltpu.VMEM((TILES, CHUNK, CHUNK), FLOAT),
            pltpu.VMEM((TILES, CHUNK, CHUNK), HALF),
            pltpu.SemaphoreType.DMA((TILES, 8)),
            pltpu.SemaphoreType.DMA,
            *buffers_of(weights_of(params)),
        ],
        flops=6 * count * D * (4 * D + 2 * FF),
        moved=count * 2 * D * 4 + 2 * D * (4 * D + 2 * FF),
    )
    shape = (2, per_group, each, window, D)
    sent = [array.reshape(shape) for array in made[:pieces]]
    return sent, made[pieces:-1], made[-1]


def side_by_side(refs, index=slice(None)):
    return jnp.concatenate([ref[index] for ref in refs], axis=0)


def pick(core, away, own, tiles):
    size = len(tiles) // 2
    for number in range(size):
        one, two = tiles[number], tiles[size + number]
        own[number] = jnp.where(core == 0, one, two).reshape(own.shape[1:])
        away[number] = jnp.where(core == 0, two, one).reshape(away.shape[1:])


def feed_back_body(place, weigh, shift, narrow_in, widen_in, *refs, arrays, steps, last):
    narrow, widen, fetch_sems = refs[-3:]
    fetched = Fetched([narrow_in, widen_in], [narrow, widen], fetch_sems)
    came, refs = refs[:arrays], refs[arrays:-3]
    middles, hiddens, refs = refs[:2], refs[2:4], refs[4:]
    if last:
        partial, refs = refs[0], refs[1:]
    middles_back, refs = refs[0], refs[1:]
    if last:
        away, own, sums, arrived, held, sems, stage, stage_sem = refs
    else:
        tiles, sums, arrived, held, sems = refs
    step = pl.program_id(0)

    def coming(number):
        return [
            pltpu.make_async_copy(
                came[number * 2 + side].at[BACK], arrived.at[number % 2, side], sems.at[number % 2, side]
            )
            for side in range(2)
        ]

    @pl.when(step == 0)
    def _():
        for copy in coming(0):
            copy.start()
        fetched.start()
        if last:
            pltpu.make_async_copy(partial, stage, stage_sem).start()
        sums[...] = jnp.zeros_like(sums)
        held[...] = jnp.zeros_like(held)

    for number in range(steps):

        @pl.when(step == number)
        def _(number=number):
            for copy in coming(number):
                copy.wait()
            if number + 1 < steps:
                for copy in coming(number + 1):
                    copy.start()

    branch_back = arrived[step % 2].reshape(-1, D)
    upstream = branch_back.astype(FLOAT)
    unit_two, inverse_two = unit_of(side_by_side(middles))
    second = (unit_two * weigh[...] + shift[...]).astype(HALF)
    sums[NUDGE] += column_sum(upstream)
    second_back = jnp.zeros_like(upstream)
    fetched.need(0, 1)
    for chunk in range(CHUNKS):
        at = slice(chunk * CHUNK, (chunk + 1) * CHUNK)
        active, slope = gelu_pair(side_by_side(hiddens, (slice(None), at)).astype(FLOAT))
        hidden_back = dot_right(branch_back, narrow[at, :]) * slope
        hidden_low = hidden_back.astype(HALF)
        sums[LIFT + chunk] += column_sum(hidden_back)
        second_back = second_back + dot_right(hidden_low, widen[:, at])
        held[NARROW + chunk] += dot_left(active.astype(HALF), branch_back)
        held[WIDEN + chunk] += dot_left(second, hidden_low)
    sums[WEIGH] += column_sum(second_back * unit_two)
    sums[SHIFT] += column_sum(second_back)
    middle_back = upstream + norm_back(second_back * weigh[...], unit_two, inverse_two)
    middles_back[...] = middle_back
    sums[BIAS] += column_sum(middle_back)

    @pl.when(step == steps - 1)
    def _():
        if not last:
            tiles[...] = held[...].astype(HALF)
            return
        pltpu.make_async_copy(partial, stage, stage_sem).wait()
        value = lambda tile: (held[tile] + stage[tile].astype(FLOAT)).astype(HALF)
        tail = pl.ds(2, 2)
        pick(place[4], away.at[tail], own.at[tail], [value(WIDEN + chunk) for chunk in range(CHUNKS)])
        _, batch, rows, _ = own.shape
        shards = batch // CHUNKS
        for chunk in range(CHUNKS):
            parts = value(NARROW + chunk).reshape(shards, 4, rows, CHUNK)
            at = pl.ds(chunk * shards, shards)
            pick(place[4], away.at[:, at], own.at[:, at], [parts[:, sub] for sub in range(4)])


def feed_back(place, params, came, middles, hiddens, batch, before=None, after=()):
    pieces = len(came[0])
    part = came[0][0].shape[1:]
    count = middles.shape[0]
    rows = count // (pieces * HALVES)
    last = before is not None
    pairs = [((0, 0), (1, 0)), ((0, 1), (1, 1))] + [((0, k), (0, k + 1)) for k in range(2, pieces, 2)]
    start = len(pairs) if last else 0
    if last:
        pairs = [((1, k), (1, k + 1)) for k in range(2, pieces, 2)]
    steps = len(pairs)
    numbers = [[half * pieces + piece for half, piece in side] for side in zip(*pairs)]
    tables = [jnp.array(side, jnp.int32) for side in numbers]
    block_of = lambda width, side: pl.BlockSpec((rows, width), lambda i, place, *tables: (tables[side][i], 0))
    ins = plain([params[5], params[6]]) + anywhere([params[9], params[7]])
    ins += [(came[half][piece], pl.BlockSpec(memory_space=pl.ANY)) for pair in pairs for half, piece in pair]
    ins += [(middles, block_of(D, side)) for side in range(2)]
    ins += [(hiddens, block_of(FF, side)) for side in range(2)]
    scratch = [
        pltpu.VMEM((2, 2, *part), HALF),
        pltpu.VMEM((2 * CHUNKS, CHUNK, CHUNK), FLOAT),
        pltpu.SemaphoreType.DMA((2, 2)),
    ]
    outs = [((count, D), FLOAT, row_spec(2 * rows, D, lambda i, *_: start + i))]
    aliases = {}
    if last:
        aliases = {0: before[0]}
        ins.append((before[1], pl.BlockSpec(memory_space=pl.ANY)))
        tiles = (4, batch, D // batch, CHUNK)
        outs += [(tiles, HALF, whole(tiles))] * 2
        scratch += [pltpu.VMEM((2 * CHUNKS, CHUNK, CHUNK), HALF), pltpu.SemaphoreType.DMA]
    else:
        tiles = (2 * CHUNKS, CHUNK, CHUNK)
        outs.append((tiles, HALF, whole(tiles)))
    outs.append(((SUMS, 1, D), FLOAT, whole((SUMS, 1, D))))
    scratch += buffers_of([params[9], params[7]])
    body = functools.partial(feed_back_body, arrays=2 * steps, steps=steps, last=last)
    return run(
        lambda place, one, two, *refs: body(place, *refs),
        "feed_back",
        (steps,),
        [place, *tables],
        ins,
        outs,
        scratch=scratch,
        aliases=aliases,
        after=after,
        flops=SMALL_FLOPS if last else 32 * rows * steps * D * FF,
        moved=0 if last else 2 * rows * steps * (10 * D + 2 * FF) + 8 * D * FF,
    )


def attention_back_body(place, rows_in, gain, offset, leave_in, entry_in, *refs, window, pieces):
    leave, entry, fetch_sems = refs[-3:]
    fetched = Fetched([leave_in, entry_in], [leave, entry], fetch_sems)
    refs = refs[:-3]
    came, refs = refs[: HALVES * pieces], refs[HALVES * pieces :]
    triples, weights, mixes, middles_back = [refs[HALVES * k : HALVES * (k + 1)] for k in range(4)]
    delta, outcome, away, own, sums, mixed_back, triple_back, held, sems = refs[4 * HALVES :]
    step = pl.program_id(0)
    each = rows_in.shape[1] // HALVES

    def results(piece):
        return [
            pltpu.make_async_copy(
                came[half * pieces + piece].at[RESULT],
                outcome.at[:, pl.ds(half * each, each)],
                sems.at[half],
            )
            for half in range(HALVES)
        ]

    @pl.when(step == 0)
    def _():
        fetched.start()
        sums[...] = jnp.zeros_like(sums)

    def add(tile, left, right):
        before = jnp.where(step == 0, 0.0, held[tile])
        held[tile] = before + dot_left(left, right)

    for piece in range(pieces):

        @pl.when(step == piece)
        def _(piece=piece):
            for copy in results(piece):
                copy.start()

    parts = [rows_in[:, half * each : (half + 1) * each].reshape(-1, D) for half in range(HALVES)]
    count = parts[0].shape[0]
    middle_back = side_by_side(middles_back)
    attend_back = middle_back.astype(HALF)
    fetched.need(0, 1)
    mixed_back[...] = dot_right(attend_back, leave[...]).astype(HALF)
    add(3, side_by_side(mixes), attend_back)
    unit, inverse = unit_of(jnp.concatenate(parts, axis=0).astype(FLOAT))
    normed = (unit * gain[...] + offset[...]).astype(HALF)
    for half in range(HALVES):
        span = pl.ds(half * count, count)
        back = triple_back.at[:, span]

        def put(rows, pair, part, value, back=back):
            back[part, rows, columns(pair)] = value

        attend_backward(triples[half], weights[half], mixed_back.at[span], put, count // window, window)
    normed_back = jnp.zeros_like(middle_back)
    for part in range(3):
        back = triple_back[part]
        normed_back = normed_back + dot_right(back, entry[:, part * D : (part + 1) * D])
        add(part, normed, back)
    sums[GAIN] += column_sum(normed_back * unit)
    sums[OFFSET] += column_sum(normed_back)
    rows_back = (middle_back + norm_back(normed_back * gain[...], unit, inverse)).astype(HALF)
    for half in range(HALVES):
        delta[:, half * each : (half + 1) * each] = rows_back[half * count : (half + 1) * count].reshape(
            -1, each, window, D
        )

    @pl.when(step == pl.num_programs(0) - 1)
    def _():
        pick(place[4], away, own, [held[tile].astype(HALF) for tile in range(4)])

    for piece in range(pieces):

        @pl.when(step == piece)
        def _(piece=piece):
            for copy in results(piece):
                copy.wait()


def attention_back(place, frames, params, came, triple, weights, mixed, middles_back, batch, after):
    pieces = len(came[0])
    per_group, windows, window, _ = frames.shape
    block = (per_group, windows // pieces, window, D)
    rows = per_group * block[1] * window // HALVES
    cut = pl.BlockSpec(block, lambda i, place: (0, place[0] ^ i, 0, 0))
    attended = (rows // window, PAIRS, window, 2 * window)
    halves = range(HALVES)
    spread_out = lambda half: lambda i, place: jnp.where(i < 2, 2 * i + half, i + (pieces if half else 2))
    ins = [(frames, cut)] + plain(params[:2]) + anywhere([params[3], params[2]])
    ins += [(array, pl.BlockSpec(memory_space=pl.ANY)) for half in came for array in half]
    ins += [(triple, row_spec(rows, 3 * D, lambda i, place, h=h: h * pieces + i)) for h in halves]
    ins += [
        (weights, pl.BlockSpec(attended, lambda i, place, h=h: (h * pieces + i, 0, 0, 0))) for h in halves
    ]
    ins += [(mixed, row_spec(rows, D, lambda i, place, h=h: h * pieces + i)) for h in halves]
    ins += [(middles_back, row_spec(rows, D, spread_out(h))) for h in halves]
    tiles = (2, batch, D // batch, CHUNK)
    count = rows * pieces * HALVES
    return run(
        functools.partial(attention_back_body, window=window, pieces=pieces),
        "attention_back",
        (pieces,),
        [place],
        ins,
        [
            (frames.shape, HALF, cut),
            (frames.shape, HALF, cut),
            *[(tiles, HALF, whole(tiles))] * 2,
            ((SUMS, 1, D), FLOAT, whole((SUMS, 1, D))),
        ],
        scratch=[
            pltpu.VMEM((rows * HALVES, D), HALF),
            pltpu.VMEM((3, rows * HALVES, D), HALF),
            pltpu.VMEM((4, CHUNK, CHUNK), FLOAT),
            pltpu.SemaphoreType.DMA((HALVES,)),
            *buffers_of([params[3], params[2]]),
        ],
        after=after,
        flops=16 * count * D * D,
        moved=count * D * 2 * (3 + 1 + 1 + 2 + 2 + 4),
    )


def swap(value, axis, mask):
    size = lax.axis_size(axis)
    if mask == 0:
        return value
    return lax.ppermute(value, axis, [(i, i ^ mask) for i in range(size)])


def move(value, batch_mask, win_mask):
    if batch_mask == 0:
        return swap(value, "win", win_mask)
    if win_mask == 0:
        return swap(value, "batch", batch_mask)
    batch, win = lax.axis_size("batch"), lax.axis_size("win")
    pairs = [
        (b * win + w, (b ^ batch_mask) * win + (w ^ win_mask)) for b in range(batch) for w in range(win)
    ]
    return lax.ppermute(value, ("batch", "win"), pairs)


def exchange(arrays):
    made = {k: swap(arrays[k], "win", k) for k in reversed(range(len(arrays)))}
    return [made[k] for k in range(len(arrays))]


def split_body(place, *refs, groups, alone, across):
    own, got, outs = refs[:groups], refs[groups : 2 * groups - alone], refs[2 * groups - alone :]
    got = [*got, *[None] * alone]
    column, row = place[1], place[2]
    width = CHUNK // across
    at = 0
    for one, two in zip(own, got):
        rows = one.shape[3]
        for tile in range(one.shape[0]):
            for piece, out in enumerate(outs):
                y = row ^ (piece % 2)
                x = pl.ds(pl.multiple_of((column ^ (piece // 2)) * width, width), width)
                total = one[tile, :, y, :, x]
                if two is not None:
                    total = (total.astype(FLOAT) + two[tile, :, y, :, x].astype(FLOAT)).astype(HALF)
                out[:, at : at + rows] = total
            at += rows


def total_of(refs, index):
    total = refs[0][index].astype(FLOAT)
    for ref in refs[1:]:
        total = total + ref[index].astype(FLOAT)
    return total.astype(HALF)


def merge_body(place, *refs, inputs):
    ins, outs = refs[:inputs], refs[inputs:]
    for piece, out in enumerate(outs):
        out[...] = total_of(ins, place[3] ^ piece)


def pair_body(place, *refs, inputs, bit):
    ins, outs = refs[:inputs], refs[inputs:]
    mine = (place[3] >> bit) & 1
    for side, out in zip((mine, 1 - mine), outs):
        out[...] = total_of(ins, (slice(None), side))


def last_body(*refs, sets):
    ins, out = refs[:-1], refs[-1]
    at, start = 0, 0
    for size in sets:
        rows, width = ins[at].shape[-2:]
        made = [ref.reshape(rows, width) for ref in ins[at : at + size]]
        out[start : start + rows] = total_of(made, slice(None))
        at += size
        start += rows


def unpack_body(place, *refs, pieces, across, layout):
    ins, outs, held = refs[:pieces], refs[pieces:-1], refs[-1]
    width = CHUNK // across
    for piece, ref in enumerate(ins):
        x = pl.ds(pl.multiple_of((place[1] ^ (piece // 2)) * width, width), width)
        held[place[4] ^ (piece % 2), :, x] = ref[...].astype(FLOAT)
    for out, places in zip(outs, layout):
        for core, start, rows, left, wide, row, column in places:
            here = (slice(start, start + rows), slice(left, left + wide))
            value = held[(0, *here)] + held[(1, *here)] if core is None else held[(core, *here)]
            out[row : row + rows, column : column + wide] = value


def arrived_body(*refs):
    refs[-1][...] = jnp.zeros_like(refs[-1])


def arrived(arrays):
    shape = (8, 128)
    outs = [(shape, FLOAT, whole(shape))]
    return run(
        arrived_body, "arrived", (1,), [], [], outs, after=arrays, flops=LONG_FLOPS, vmem=SMALL_VMEM
    )


class Reduction:
    def __init__(self, place, away, own, alone=()):
        self.place = place
        self.batch, self.win = lax.axis_size("batch"), lax.axis_size("win")
        self.across, self.depth = self.win // 2, self.batch // 2
        cut = lambda a: a.reshape(-1, self.depth, 2, *a.shape[2:])
        self.own = [cut(a) for a in (*own, *alone)]
        self.alone = len(alone)
        self.got = [swap(cut(a), "win", 1) for a in away]
        self.rows = sum(a.shape[0] * a.shape[3] for a in self.own)
        self.width = CHUNK // self.across
        self.vmem = VMEM

    def cores(self, after=()):
        shape = (self.depth, self.rows, self.width)
        pieces = run(
            functools.partial(split_body, groups=len(self.own), alone=self.alone, across=self.across),
            "sum_cores",
            (1,),
            [self.place],
            plain(self.own + self.got),
            [(shape, HALF, whole(shape))] * (2 * self.across),
            after=after,
            vmem=self.vmem,
            flops=SMALL_FLOPS,
        )
        self.mark = pieces[:1]
        self.pieces = [move(a, number % 2, 2 * (number // 2)) for number, a in enumerate(pieces)]

    def chips(self, after=(), flops=SMALL_FLOPS):
        shape = (self.rows, self.width)
        pieces = run(
            functools.partial(merge_body, inputs=len(self.pieces)),
            "sum_chips",
            (1,),
            [self.place],
            plain(self.pieces),
            [(shape, HALF, whole(shape))] * self.depth,
            after=after,
            vmem=self.vmem,
            flops=flops,
        )
        self.mark = pieces[:1]
        self.pieces = [swap(a, "batch", 2 * number) for number, a in enumerate(pieces)]

    def pair(self, bit, after=(), flops=SMALL_FLOPS):
        depth, rows, width = self.pieces[0].shape
        shape = (depth // 2, rows, width)
        kept, away = run(
            functools.partial(pair_body, inputs=len(self.pieces), bit=bit),
            "sum_pairs",
            (1,),
            [self.place],
            plain([a.reshape(depth // 2, 2, rows, width) for a in self.pieces]),
            [(shape, HALF, whole(shape))] * 2,
            after=after,
            vmem=self.vmem,
            flops=flops,
        )
        self.mark = [kept]
        self.pieces = [kept, swap(away, "batch", 2 << bit)]

    def last(self, after=(), other=None):
        groups = [self] if other is None else [other, self]
        self.rows = sum(group.rows for group in groups)
        shape = (self.rows, self.width)
        (total,) = run(
            functools.partial(last_body, sets=[len(group.pieces) for group in groups]),
            "sum_last",
            (1,),
            [],
            plain([a for group in groups for a in group.pieces]),
            [(shape, HALF, whole(shape))],
            after=after,
            vmem=self.vmem,
            flops=SMALL_FLOPS,
        )
        self.mark = [total]
        across = [swap(total, "win", 2 * number) for number in range(self.across)]
        self.pieces = [a if side == 0 else swap(a, "win", 1) for a in across for side in range(2)]

    def unpack(self, layout, shapes, after=()):
        return run(
            functools.partial(
                unpack_body, pieces=self.win, across=self.across, layout=layout
            ),
            "unpack",
            (1,),
            [self.place],
            plain(self.pieces),
            [(s, FLOAT, whole(s)) for s in shapes],
            scratch=[pltpu.VMEM((2, self.rows, CHUNK), FLOAT)],
            after=after,
            vmem=self.vmem,
            flops=SMALL_FLOPS,
        )


SMALL_ROWS = 16


def small_tiles(sums, batch):
    blocks = len(sums)
    sums = jnp.stack(sums)[:, :, 0]
    vectors = sums[:, :6].reshape(blocks, 6, batch, -1).transpose(2, 0, 1, 3).reshape(batch, blocks, -1)
    lifts = sums[:, LIFT:].reshape(blocks, batch, -1).swapaxes(0, 1)
    wide = lambda a: jnp.pad(a, ((0, 0), (0, 0), (0, CHUNK - a.shape[2])))
    both = jnp.concatenate([wide(vectors), wide(lifts)], axis=1)
    return jnp.pad(both, ((0, 0), (0, SMALL_ROWS - 2 * blocks), (0, 0))).astype(HALF)[None]


def attend_places(rows, start):
    spot = lambda tile: (tile // 2, start + tile % 2 * rows, rows, 0, CHUNK)
    return [
        [(*spot(part), 0, part * CHUNK) for part in range(3)],
        [(*spot(3), 0, 0)],
    ], [(rows, 3 * D), (rows, D)]


def feed_places(rows, start):
    narrows = [(sub // 2, start + sub % 2 * rows, rows, 0, CHUNK, sub * rows, 0) for sub in range(4)]
    start += 2 * rows
    widens = [
        (chunk // 2, start + chunk % 2 * rows, rows, 0, CHUNK, 0, chunk * CHUNK) for chunk in range(CHUNKS)
    ]
    return [widens, narrows], [(rows, FF), (4 * rows, D)]


def small_places(rows, start):
    layout, shapes = [], []
    for block in range(2):
        layout += [[(None, start + block, 1, number * rows, rows, 0, 0)] for number in range(6)]
        layout.append([(None, start + 2 + block, 1, 0, 4 * rows, 0, 0)])
        shapes += [(1, rows)] * 6 + [(1, 4 * rows)]
    return layout, shapes


def local(*args):
    frames, cotangent, video_frames = args[0], args[23], args[24]
    space = [a.reshape(1, -1) if a.ndim == 1 else a for a in args[1:12]]
    time = [a.reshape(1, -1) if a.ndim == 1 else a for a in args[12:23]]
    batch, win = lax.axis_size("batch"), lax.axis_size("win")
    here, group = lax.axis_index("win"), lax.axis_index("batch")
    core = here % 2
    place = jnp.stack([here, here // 2, group % 2, group // 2, core]).astype(jnp.int32)
    _, per_group, _, windows, window, _ = frames.shape
    shape = (per_group, windows, window, D)
    rows_in, cotangent = frames.reshape(shape), cotangent.reshape(shape)
    rows = D // batch

    kept, came = [], []
    for half in range(HALVES):
        sent, kept = space_forward(place, rows_in, cotangent, space, half, win, kept)
        came.append(exchange(sent))
    triple, weights, mixed, middles, hiddens = kept
    backs, time_sums, tiles = [], [], [None]
    for half in range(HALVES):
        sent, tiles, sums = time_block(place, video_frames, came[half], time, batch, *tiles)
        backs.append(exchange(sent))
        time_sums.append(sums)

    bits = (batch // 2).bit_length() - 1
    time_sum = Reduction(place, tiles[:1], tiles[1:])
    time_sum.cores(arrived(backs[0][1:]))
    *fed, first_sums = feed_back(place, space, backs, middles, hiddens, batch, after=time_sum.mark)
    middles_back, away, own, feed_sums = feed_back(place, space, backs, middles, hiddens, batch, fed)
    feed_sum = Reduction(place, [away], [own])
    time_sum.pair(0, [middles_back], LONG_FLOPS)
    feed_sum.cores(time_sum.mark)
    delta, outcome, away, own, attend_sums = attention_back(
        place, rows_in, space, backs, triple, weights, mixed, middles_back, batch, feed_sum.mark
    )
    time_sum.vmem = feed_sum.vmem = SMALL_VMEM
    small = small_tiles([first_sums + feed_sums + attend_sums, sum(time_sums)], batch)
    attend_sum = Reduction(place, [away], [own], [small])
    attend_sum.vmem = SMALL_VMEM
    feed_sum.pair(0, [delta], LONG_FLOPS)
    attend_sum.cores(feed_sum.mark)
    mark = attend_sum.mark
    for bit in range(1, bits):
        time_sum.pair(bit, mark)
        feed_sum.pair(bit, time_sum.mark)
        mark = feed_sum.mark
    attend_sum.chips(mark)
    time_rows = time_sum.rows
    feed_sum.last(attend_sum.mark, time_sum)
    attend_sum.last(feed_sum.mark)
    feed_layout, feed_shapes = feed_places(rows, 0)
    attend_layout, attend_shapes = attend_places(rows, 4 * rows)
    last_layout, last_shapes = feed_places(rows, time_rows)
    made = feed_sum.unpack(
        feed_layout + attend_layout + last_layout,
        feed_shapes + attend_shapes + last_shapes,
        attend_sum.mark,
    )
    time_grads, feed_grads = made[:4], made[4:]
    attend_layout, attend_shapes = attend_places(rows, 0)
    small_layout, small_shapes = small_places(rows, 2 * rows)
    attend_grads = attend_sum.unpack(attend_layout + small_layout, attend_shapes + small_shapes)
    smalls = [a.reshape(-1) for a in attend_grads[2:]]

    def collected(grads, smalls):
        widen, narrow, entry, leave = grads
        gain, offset, bias, weigh, shift, nudge, lift = smalls
        return gain, offset, entry, leave, bias, weigh, shift, widen, lift, narrow, nudge

    return (
        outcome.reshape(frames.shape),
        delta.reshape(frames.shape),
        *collected([*feed_grads, *attend_grads[:2]], smalls[:7]),
        *collected(time_grads, smalls[7:]),
    )


def solution(mesh):
    rows = P("batch", None, "win", None, None, None)
    one, two = P("batch"), P("batch", None)
    grads = (one, one, two, two, one, one, one, two, one, two, one)
    return jax.shard_map(
        local,
        mesh=mesh,
        in_specs=(rows, *([P()] * 22), rows, P("batch", None)),
        out_specs=(rows, rows, *grads, *grads),
        check_vma=False,
    )
```

```python
import functools

import jax
import jax.numpy as jnp
from jax import lax
from jax.experimental import pallas as pl
from jax.experimental.pallas import tpu as pltpu
from jax.sharding import PartitionSpec as P

D = 512
HEADS = 8
HDIM = 64
FF = 2048
PAIR = 2 * HDIM
PAIRS = HEADS // 2
CHUNK = 512
CHUNKS = FF // CHUNK
EPS = 1e-05
NEGATIVE = -1e30
FLOAT = jnp.float32
HALF = jnp.bfloat16
HALVES = 2
UNITS = 16
VMEM = 127 << 19
SMALL_VMEM = 24 << 20
LONG_FLOPS = 10**11
SMALL_FLOPS = 2 * 10**8
SLOWER = 4

NARROW, WIDEN, ENTRY, EXIT = 0, CHUNKS, 2 * CHUNKS, 2 * CHUNKS + 3
TILES = 2 * CHUNKS + 4
SHARED = [WIDEN, WIDEN + 1, ENTRY, ENTRY + 1, WIDEN + 2, WIDEN + 3, ENTRY + 2, EXIT]
INNER, COTANGENT = 0, 1
BACK, RESULT = 0, 1
GAIN, OFFSET, BIAS, WEIGH, SHIFT, NUDGE, LIFT = 0, 1, 2, 3, 4, 5, 6
SUMS = 6 + CHUNKS


def dot(left, right):
    return lax.dot_general(left, right, (((1,), (0,)), ((), ())), preferred_element_type=FLOAT)


def dot_right(left, right):
    return lax.dot_general(left, right, (((1,), (1,)), ((), ())), preferred_element_type=FLOAT)


def dot_left(left, right):
    return lax.dot_general(left, right, (((0,), (0,)), ((), ())), preferred_element_type=FLOAT)


def unit_of(rows):
    centre = rows - jnp.mean(rows, axis=-1, keepdims=True)
    inverse = lax.rsqrt(jnp.mean(centre * centre, axis=-1, keepdims=True) + EPS)
    return centre * inverse, inverse


def norm_back(scaled, unit, inverse):
    return inverse * (
        scaled
        - jnp.mean(scaled, axis=-1, keepdims=True)
        - unit * jnp.mean(scaled * unit, axis=-1, keepdims=True)
    )


def gelu_pair(hidden):
    half = 0.5 * lax.erf(hidden * 0.7071067811865476) + 0.5
    bell = jnp.exp(hidden * hidden * -0.5) * 0.3989422804014327
    return hidden * half, half + hidden * bell


def gelu_of(hidden):
    return hidden * (0.5 * lax.erf(hidden * 0.7071067811865476) + 0.5)


def column_sum(values):
    return jnp.sum(values, axis=0, keepdims=True)


def first_head(rows):
    return lax.broadcasted_iota(jnp.int32, (rows, PAIR), 1) < HDIM


def spread(pair, first):
    zero = jnp.zeros_like(pair)
    return jnp.concatenate([jnp.where(first, pair, zero), jnp.where(first, zero, pair)], axis=0)


def gathered(both, first, rows):
    return jnp.where(first, both[:rows], both[rows:])


def attend_units(blocks):
    units = [(block, pair) for block in range(blocks) for pair in range(PAIRS)]
    return [units[start : start + UNITS] for start in range(0, len(units), UNITS)]


def columns(pair, part=0):
    start = part * D + pair * PAIR
    return slice(start, start + PAIR)


def attend_forward(triple, mixed, weights, blocks, rows, mask):
    first = first_head(rows)
    for units in attend_units(blocks):
        spans = [slice(block * rows, block * rows + rows) for block, _ in units]
        queries = [spread(triple[s, columns(p)], first) for s, (_, p) in zip(spans, units)]
        scores = [dot_right(triple[s, columns(p, 1)], q) for q, s, (_, p) in zip(queries, spans, units)]
        if mask is not None:
            scores = [score + mask for score in scores]
        powers = [
            jnp.exp((score - jnp.max(score, axis=0, keepdims=True)) * HDIM ** (-0.5)) for score in scores
        ]
        probs = [
            (power * (1.0 / jnp.sum(power, axis=0, keepdims=True))).astype(HALF) for power in powers
        ]
        both = [dot_left(prob, triple[s, columns(p, 2)]) for prob, s, (_, p) in zip(probs, spans, units)]
        for value, prob, s, (block, p) in zip(both, probs, spans, units):
            weights[block, p] = prob
            mixed[s, columns(p)] = gathered(value, first, rows).astype(HALF)


def attend_backward(triple, weights, mixed_back, put, blocks, rows):
    first = first_head(rows)
    scale = HDIM ** (-0.5)
    for units in attend_units(blocks):
        spans = [slice(block * rows, block * rows + rows) for block, _ in units]
        mixes = [spread(mixed_back[s, columns(p)], first) for s, (_, p) in zip(spans, units)]
        probs = [weights[block, p] for block, p in units]
        values_back = [dot(prob, mix) for prob, mix in zip(probs, mixes)]
        weights_back = [
            dot_right(triple[s, columns(p, 2)], mix) for mix, s, (_, p) in zip(mixes, spans, units)
        ]
        scores_back = []
        for prob, back in zip(probs, weights_back):
            wide = prob.astype(FLOAT)
            inside = back - jnp.sum(back * wide, axis=0, keepdims=True)
            scores_back.append((wide * inside * scale).astype(HALF))
        queries = [spread(triple[s, columns(p)], first) for s, (_, p) in zip(spans, units)]
        keys_back = [dot(score, query) for score, query in zip(scores_back, queries)]
        both = [
            dot_left(score, triple[s, columns(p, 1)])
            for score, s, (_, p) in zip(scores_back, spans, units)
        ]
        for key, value, pair, s, (_, p) in zip(keys_back, values_back, both, spans, units):
            put(s, p, 0, gathered(pair, first, rows).astype(HALF))
            put(s, p, 1, key.astype(HALF))
            put(s, p, 2, value.astype(HALF))


def whole(shape):
    return pl.BlockSpec(shape, lambda *_: (0,) * len(shape), pipeline_mode=pl.Buffered(1))


def run(body, name, grid, scalars, ins, outs, scratch=(), aliases=None, after=(), flops=0, moved=0, vmem=VMEM):
    aliases = aliases or {}
    unread = pl.BlockSpec(memory_space=pl.ANY)
    first = len(scalars) + len(ins)
    extra = [*aliases.values(), *after]

    def inner(*refs):
        body(*refs[:first], *refs[first + len(extra) :])

    return pl.pallas_call(
        inner,
        out_shape=[jax.ShapeDtypeStruct(shape, kind) for shape, kind, _ in outs],
        grid_spec=pltpu.PrefetchScalarGridSpec(
            num_scalar_prefetch=len(scalars),
            grid=grid,
            in_specs=[spec for _, spec in ins] + [unread] * len(extra),
            out_specs=[spec for _, _, spec in outs],
            scratch_shapes=list(scratch),
        ),
        input_output_aliases={first + at: out for at, out in enumerate(aliases)},
        compiler_params=pltpu.CompilerParams(vmem_limit_bytes=vmem),
        cost_estimate=pl.CostEstimate(flops=flops * SLOWER, bytes_accessed=moved * SLOWER, transcendentals=0),
        name=name,
    )(*scalars, *[array for array, _ in ins], *extra)


class Fetched:
    def __init__(self, sources, buffers, sems):
        self.copies = [
            pltpu.make_async_copy(source, buffer, sems.at[number])
            for number, (source, buffer) in enumerate(zip(sources, buffers))
        ]

    def start(self):
        for copy in self.copies:
            copy.start()

    def need(self, *numbers):
        @pl.when(pl.program_id(0) == 0)
        def _():
            for number in numbers:
                self.copies[number].wait()


def anywhere(arrays):
    return [(array, pl.BlockSpec(memory_space=pl.ANY)) for array in arrays]


def buffers_of(arrays):
    return [pltpu.VMEM(a.shape, a.dtype) for a in arrays] + [pltpu.SemaphoreType.DMA((len(arrays),))]


def plain(arrays):
    return [(array, whole(array.shape)) for array in arrays]


def slab_spec(slabs, rows, at):
    return pl.BlockSpec((slabs, rows, D), lambda *i: (0, at(*i), 0))


def row_spec(rows, width, at):
    return pl.BlockSpec((rows, width), lambda *i: (at(*i), 0))


def vectors_of(params):
    return [param for param in params if param.shape[0] == 1]


def weights_of(params):
    return [param for param in params if param.shape[0] > 1]


def space_forward_body(place, *refs, window, pieces):
    ins, cotangents, refs = refs[:2], refs[2:4], refs[4:]
    gain, offset, bias, weigh, shift, lift, nudge = refs[:7]
    sent = refs[11 : 11 + pieces]
    triple, weights, mixed, middles, hiddens, *buffers, sems = refs[11 + pieces :]
    entry, leave, widen, narrow = buffers
    fetched = Fetched(refs[7:11], buffers, sems)
    step = pl.program_id(0)

    @pl.when(step == 0)
    def _():
        fetched.start()

    shape = ins[0].shape
    rows = jnp.concatenate([ref[...].reshape(-1, D) for ref in ins], axis=0).astype(FLOAT)
    count = rows.shape[0]
    unit, _ = unit_of(rows)
    normed = (unit * gain[...] + offset[...]).astype(HALF)
    fetched.need(0)
    triple[...] = dot(normed, entry[...]).astype(HALF)
    attend_forward(triple, mixed, weights, count // window, window, None)
    fetched.need(1, 2, 3)
    middle = rows + dot(mixed[...], leave[...]) + bias[...]
    middles[...] = middle.astype(HALF)
    unit_two, _ = unit_of(middle)
    second = (unit_two * weigh[...] + shift[...]).astype(HALF)
    total = middle + nudge[...]
    for chunk in range(CHUNKS):
        at = slice(chunk * CHUNK, (chunk + 1) * CHUNK)
        hidden = dot(second, widen[:, at]) + lift[:, at]
        hiddens[:, at] = hidden.astype(HALF)
        total = total + dot(gelu_of(hidden).astype(HALF), narrow[at, :])
    inner = total.astype(HALF).reshape(2, *shape)
    for piece in range(pieces):

        @pl.when(step == piece // 2)
        def _(piece=piece):
            sent[piece][INNER] = inner[piece % 2]
            sent[piece][COTANGENT] = cotangents[piece % 2][...]


def space_forward(place, frames, cotangent, params, half, pieces, before):
    per_group, windows, window, _ = frames.shape
    each = windows // pieces // HALVES
    block = (per_group, each, window, D)
    rows = per_group * each * window
    count = rows * pieces * HALVES
    cuts = [
        pl.BlockSpec(block, lambda i, place, side=side: (0, (place[0] ^ (2 * i + side)) * HALVES + half, 0, 0))
        for side in range(2)
    ]
    rows *= 2
    at = lambda i, place: half * pieces // 2 + i
    attended = (rows // window, PAIRS, window, 2 * window)
    both = (2, *block)
    outs = [(both, HALF, pl.BlockSpec(both, lambda i, place: (0,) * 5))] * pieces
    outs += [
        ((count, 3 * D), HALF, row_spec(rows, 3 * D, at)),
        (
            (count // window, *attended[1:]),
            HALF,
            pl.BlockSpec(attended, lambda i, place: (at(i, place), 0, 0, 0)),
        ),
        ((count, D), HALF, row_spec(rows, D, at)),
        ((count, D), HALF, row_spec(rows, D, at)),
        ((count, FF), HALF, row_spec(rows, FF, at)),
    ]
    made = run(
        functools.partial(space_forward_body, window=window, pieces=pieces),
        "space_forward",
        (pieces // 2,),
        [place],
        [(a, cut) for a in (frames, cotangent) for cut in cuts] + plain(vectors_of(params)) + anywhere(weights_of(params)),
        outs,
        scratch=buffers_of(weights_of(params)),
        aliases={pieces + number: array for number, array in enumerate(before)},
        flops=rows * pieces * D * (4 * D + 2 * FF),
        moved=rows * pieces * (4 * D + 6 * D + FF),
    )
    return made[:pieces], made[pieces:]


def by_position(refs, which, frames_of, positions):
    parts = [ref[which, frame].astype(FLOAT) for ref in refs for frame in range(frames_of)]
    return jnp.concatenate(
        [part[start : start + 8] for start in range(0, positions, 8) for part in parts], axis=0
    )


def by_frame(values, refs, which, frames_of, positions):
    total = len(refs) * frames_of
    for at, ref in enumerate(refs):
        for frame in range(frames_of):
            number = at * frames_of + frame
            ref[which, frame] = jnp.concatenate(
                [
                    values[(group * total + number) * 8 : (group * total + number) * 8 + 8]
                    for group in range(positions // 8)
                ],
                axis=0,
            ).astype(HALF)


def fill_mask(mask, place, lengths, per_group, pieces):
    window = mask.shape[0]
    key = lax.broadcasted_iota(jnp.int32, mask.shape, 0)
    query = lax.broadcasted_iota(jnp.int32, mask.shape, 1) % window
    frames = []
    for row in (query, key):
        number = row // 8
        frames.append((number % per_group) * pieces + ((number // per_group) ^ place[0]))
    videos = [jnp.zeros_like(frame) for frame in frames]
    entries = lengths.shape[1]
    end = 0
    for entry in range(entries):
        end = end + lengths[0, entry]
        videos = [v + (f >= end).astype(jnp.int32) for v, f in zip(videos, frames)]
    videos = [jnp.where(f < end, v, entries + f) for v, f in zip(videos, frames)]
    allowed = (videos[0] == videos[1]) & (frames[1] <= frames[0]) & (query % 8 == key % 8)
    mask[...] = jnp.where(allowed, 0.0, NEGATIVE)


def shared_copies(tile, core, stage, away, own, sems):
    _, batch, rows, _ = own.shape
    made = []
    if tile < WIDEN:
        shards = batch // CHUNKS
        source = stage.at[tile].reshape(shards, 4, rows, CHUNK)
        at = pl.ds(tile * shards, shards)
        for sub in range(4):
            target = own if sub // 2 == core else away
            made.append((source.at[:, sub], target.at[sub % 2, at]))
    else:
        place = SHARED.index(tile)
        target = own if place // 4 == core else away
        made.append((stage.at[tile].reshape(batch, rows, CHUNK), target.at[2 + place % 4]))
    return [
        pltpu.make_async_copy(source, target, sems.at[tile, number])
        for number, (source, target) in enumerate(made)
    ]


def time_body(place, lengths, *refs, pieces, last):
    came = refs[:pieces]
    gain, offset, bias, weigh, shift, lift, nudge = refs[pieces : pieces + 7]
    entry, leave, widen, narrow, fetch_sems = refs[-5:]
    fetched = Fetched(refs[pieces + 7 : pieces + 11], [entry, leave, widen, narrow], fetch_sems)
    refs = refs[pieces + 11 : -5]
    if last:
        partial, refs = refs[0], refs[1:]
    sent, refs = refs[:pieces], refs[pieces:]
    grads, refs = refs[: 1 + last], refs[1 + last :]
    sums, triple, weights, mixed, mixed_back, triple_back, mask, held, stage, sems, came_sem = refs
    _, frames_of, positions, _ = came[0].shape
    window = 8 * pieces * frames_of
    rows = by_position(came, INNER, frames_of, positions)
    blocks = rows.shape[0] // window
    step = pl.program_id(0)

    @pl.when(step == 0)
    def _():
        fetched.start()
        sums[...] = jnp.zeros_like(sums)
        fill_mask(mask, place, lengths, frames_of, pieces)
        if last:
            pltpu.make_async_copy(partial, stage, came_sem).start()

    def each_copy(tile, act):
        if not last:
            act(pltpu.make_async_copy(stage.at[tile], grads[0].at[tile], sems.at[tile, 0]))
            return
        for core in range(2):

            @pl.when(place[4] == core)
            def _(core=core):
                for copy in shared_copies(tile, core, stage, *grads, sems):
                    act(copy)

    def done(tiles):
        @pl.when(step == pl.num_programs(0) - 1)
        def _():
            if last and tiles[0] == 0:
                pltpu.make_async_copy(partial, stage, came_sem).wait()
            for tile in tiles:
                value = held[tile]
                if last:
                    value = value + stage[tile].astype(FLOAT)
                stage[tile] = value.astype(HALF)
                each_copy(tile, lambda copy: copy.start())

    def add(tile, left, right):
        before = jnp.where(step == 0, 0.0, held[tile])
        held[tile] = before + dot_left(left, right)

    unit, inverse = unit_of(rows)
    normed = (unit * gain[...] + offset[...]).astype(HALF)
    fetched.need(0)
    triple[...] = dot(normed, entry[...]).astype(HALF)
    attend_forward(triple, mixed, weights, blocks, window, mask[...])
    fetched.need(1, 2, 3)
    middle = rows + dot(mixed[...], leave[...]) + bias[...]
    unit_two, inverse_two = unit_of(middle)
    second = (unit_two * weigh[...] + shift[...]).astype(HALF)
    upstream = by_position(came, COTANGENT, frames_of, positions)
    branch_back = upstream.astype(HALF)
    sums[NUDGE] += column_sum(upstream)
    total = middle + nudge[...]
    second_back = jnp.zeros_like(middle)
    for chunk in range(CHUNKS):
        at = slice(chunk * CHUNK, (chunk + 1) * CHUNK)
        active, slope = gelu_pair(dot(second, widen[:, at]) + lift[:, at])
        active = active.astype(HALF)
        hidden_back = dot_right(branch_back, narrow[at, :]) * slope
        hidden_low = hidden_back.astype(HALF)
        sums[LIFT + chunk] += column_sum(hidden_back)
        total = total + dot(active, narrow[at, :])
        second_back = second_back + dot_right(hidden_low, widen[:, at])
        add(NARROW + chunk, active, branch_back)
        add(WIDEN + chunk, second, hidden_low)
    done(range(ENTRY))
    by_frame(total, sent, RESULT, frames_of, positions)
    sums[WEIGH] += column_sum(second_back * unit_two)
    sums[SHIFT] += column_sum(second_back)
    middle_back = upstream + norm_back(second_back * weigh[...], unit_two, inverse_two)
    attend_back = middle_back.astype(HALF)
    sums[BIAS] += column_sum(middle_back)
    mixed_back[...] = dot_right(attend_back, leave[...]).astype(HALF)
    add(EXIT, mixed[...], attend_back)

    def put(span, pair, part, value):
        triple_back[part, span, columns(pair)] = value

    attend_backward(triple, weights, mixed_back, put, blocks, window)
    normed_back = jnp.zeros_like(middle)
    for part in range(3):
        back = triple_back[part]
        normed_back = normed_back + dot_right(back, entry[:, part * D : (part + 1) * D])
        add(ENTRY + part, normed, back)
    sums[GAIN] += column_sum(normed_back * unit)
    sums[OFFSET] += column_sum(normed_back)
    rows_back = middle_back + norm_back(normed_back * gain[...], unit, inverse)
    by_frame(rows_back, sent, BACK, frames_of, positions)

    done(range(ENTRY, TILES))

    @pl.when(step == pl.num_programs(0) - 1)
    def _():
        for tile in range(TILES):
            each_copy(tile, lambda copy: copy.wait())


def time_block(place, lengths, came, params, batch, partial=None, step_rows=512):
    pieces = len(came)
    _, per_group, each, window, _ = came[0].shape
    positions = each * window
    flat = (2, per_group, positions, D)
    frames = per_group * pieces
    together = min(max(step_rows // frames, 16), positions)
    rows = together * frames
    steps = positions // together
    count = positions * frames
    attended = 8 * frames
    last = partial is not None
    spec = pl.BlockSpec((2, per_group, together, D), lambda i, *_: (0, 0, i, 0))
    grads = (TILES // 2, batch, D // batch, CHUNK) if last else (TILES, CHUNK, CHUNK)
    outs = [(flat, HALF, spec)] * pieces
    outs += [(grads, HALF, pl.BlockSpec(memory_space=pl.ANY))] * (1 + last)
    outs += [((SUMS, 1, D), FLOAT, whole((SUMS, 1, D)))]
    ins = [(array.reshape(flat), spec) for array in came] + plain(vectors_of(params))
    ins += anywhere(weights_of(params))
    if last:
        ins += anywhere([partial])
    made = run(
        functools.partial(time_body, pieces=pieces, last=last),
        "time_block",
        (steps,),
        [place, lengths],
        ins,
        outs,
        scratch=[
            pltpu.VMEM((rows, 3 * D), HALF),
            pltpu.VMEM((rows // attended, PAIRS, attended, 2 * attended), HALF),
            pltpu.VMEM((rows, D), HALF),
            pltpu.VMEM((rows, D), HALF),
            pltpu.VMEM((3, rows, D), HALF),
            pltpu.VMEM((attended, 2 * attended), FLOAT),
            pltpu.VMEM((TILES, CHUNK, CHUNK), FLOAT),
            pltpu.VMEM((TILES, CHUNK, CHUNK), HALF),
            pltpu.SemaphoreType.DMA((TILES, 8)),
            pltpu.SemaphoreType.DMA,
            *buffers_of(weights_of(params)),
        ],
        flops=6 * count * D * (4 * D + 2 * FF),
        moved=count * 2 * D * 4 + 2 * D * (4 * D + 2 * FF),
    )
    shape = (2, per_group, each, window, D)
    sent = [array.reshape(shape) for array in made[:pieces]]
    return sent, made[pieces:-1], made[-1]


def side_by_side(refs, index=slice(None)):
    return jnp.concatenate([ref[index] for ref in refs], axis=0)


def pick(core, away, own, tiles):
    size = len(tiles) // 2
    for number in range(size):
        one, two = tiles[number], tiles[size + number]
        own[number] = jnp.where(core == 0, one, two).reshape(own.shape[1:])
        away[number] = jnp.where(core == 0, two, one).reshape(away.shape[1:])


def feed_back_body(place, weigh, shift, narrow_in, widen_in, *refs, arrays, steps, last):
    narrow, widen, fetch_sems = refs[-3:]
    fetched = Fetched([narrow_in, widen_in], [narrow, widen], fetch_sems)
    came, refs = refs[:arrays], refs[arrays:-3]
    middles, hiddens, refs = refs[:2], refs[2:4], refs[4:]
    if last:
        partial, refs = refs[0], refs[1:]
    middles_back, refs = refs[0], refs[1:]
    if last:
        away, own, sums, arrived, held, sems, stage, stage_sem = refs
    else:
        tiles, sums, arrived, held, sems = refs
    step = pl.program_id(0)

    def coming(number):
        return [
            pltpu.make_async_copy(
                came[number * 2 + side].at[BACK], arrived.at[number % 2, side], sems.at[number % 2, side]
            )
            for side in range(2)
        ]

    @pl.when(step == 0)
    def _():
        for copy in coming(0):
            copy.start()
        fetched.start()
        if last:
            pltpu.make_async_copy(partial, stage, stage_sem).start()
        sums[...] = jnp.zeros_like(sums)
        held[...] = jnp.zeros_like(held)

    for number in range(steps):

        @pl.when(step == number)
        def _(number=number):
            for copy in coming(number):
                copy.wait()
            if number + 1 < steps:
                for copy in coming(number + 1):
                    copy.start()

    branch_back = arrived[step % 2].reshape(-1, D)
    upstream = branch_back.astype(FLOAT)
    unit_two, inverse_two = unit_of(side_by_side(middles).astype(FLOAT))
    second = (unit_two * weigh[...] + shift[...]).astype(HALF)
    sums[NUDGE] += column_sum(upstream)
    second_back = jnp.zeros_like(upstream)
    fetched.need(0, 1)
    for chunk in range(CHUNKS):
        at = slice(chunk * CHUNK, (chunk + 1) * CHUNK)
        active, slope = gelu_pair(side_by_side(hiddens, (slice(None), at)).astype(FLOAT))
        hidden_back = dot_right(branch_back, narrow[at, :]) * slope
        hidden_low = hidden_back.astype(HALF)
        sums[LIFT + chunk] += column_sum(hidden_back)
        second_back = second_back + dot_right(hidden_low, widen[:, at])
        held[NARROW + chunk] += dot_left(active.astype(HALF), branch_back)
        held[WIDEN + chunk] += dot_left(second, hidden_low)
    sums[WEIGH] += column_sum(second_back * unit_two)
    sums[SHIFT] += column_sum(second_back)
    middle_back = upstream + norm_back(second_back * weigh[...], unit_two, inverse_two)
    middles_back[...] = middle_back.astype(HALF)
    sums[BIAS] += column_sum(middle_back)

    @pl.when(step == steps - 1)
    def _():
        if not last:
            tiles[...] = held[...].astype(HALF)
            return
        pltpu.make_async_copy(partial, stage, stage_sem).wait()
        value = lambda tile: (held[tile] + stage[tile].astype(FLOAT)).astype(HALF)
        tail = pl.ds(2, 2)
        pick(place[4], away.at[tail], own.at[tail], [value(WIDEN + chunk) for chunk in range(CHUNKS)])
        _, batch, rows, _ = own.shape
        shards = batch // CHUNKS
        for chunk in range(CHUNKS):
            parts = value(NARROW + chunk).reshape(shards, 4, rows, CHUNK)
            at = pl.ds(chunk * shards, shards)
            pick(place[4], away.at[:, at], own.at[:, at], [parts[:, sub] for sub in range(4)])


def feed_back(place, params, came, middles, hiddens, batch, before=None, after=()):
    pieces = len(came[0])
    part = came[0][0].shape[1:]
    count = middles.shape[0]
    rows = count // (pieces * HALVES)
    last = before is not None
    pairs = [((0, 0), (1, 0)), ((0, 1), (1, 1))] + [((0, k), (0, k + 1)) for k in range(2, pieces, 2)]
    start = len(pairs) if last else 0
    if last:
        pairs = [((1, k), (1, k + 1)) for k in range(2, pieces, 2)]
    steps = len(pairs)
    numbers = [[half * pieces + piece for half, piece in side] for side in zip(*pairs)]
    tables = [jnp.array(side, jnp.int32) for side in numbers]
    block_of = lambda width, side: pl.BlockSpec((rows, width), lambda i, place, *tables: (tables[side][i], 0))
    ins = plain([params[5], params[6]]) + anywhere([params[9], params[7]])
    ins += [(came[half][piece], pl.BlockSpec(memory_space=pl.ANY)) for pair in pairs for half, piece in pair]
    ins += [(middles, block_of(D, side)) for side in range(2)]
    ins += [(hiddens, block_of(FF, side)) for side in range(2)]
    scratch = [
        pltpu.VMEM((2, 2, *part), HALF),
        pltpu.VMEM((2 * CHUNKS, CHUNK, CHUNK), FLOAT),
        pltpu.SemaphoreType.DMA((2, 2)),
    ]
    outs = [((count, D), HALF, row_spec(2 * rows, D, lambda i, *_: start + i))]
    aliases = {}
    if last:
        aliases = {0: before[0]}
        ins.append((before[1], pl.BlockSpec(memory_space=pl.ANY)))
        tiles = (4, batch, D // batch, CHUNK)
        outs += [(tiles, HALF, whole(tiles))] * 2
        scratch += [pltpu.VMEM((2 * CHUNKS, CHUNK, CHUNK), HALF), pltpu.SemaphoreType.DMA]
    else:
        tiles = (2 * CHUNKS, CHUNK, CHUNK)
        outs.append((tiles, HALF, whole(tiles)))
    outs.append(((SUMS, 1, D), FLOAT, whole((SUMS, 1, D))))
    scratch += buffers_of([params[9], params[7]])
    body = functools.partial(feed_back_body, arrays=2 * steps, steps=steps, last=last)
    return run(
        lambda place, one, two, *refs: body(place, *refs),
        "feed_back",
        (steps,),
        [place, *tables],
        ins,
        outs,
        scratch=scratch,
        aliases=aliases,
        after=after,
        flops=SMALL_FLOPS if last else 32 * rows * steps * D * FF,
        moved=0 if last else 2 * rows * steps * (10 * D + 2 * FF) + 8 * D * FF,
    )


def attention_back_body(place, rows_in, gain, offset, leave_in, entry_in, *refs, window, pieces):
    leave, entry, fetch_sems = refs[-3:]
    fetched = Fetched([leave_in, entry_in], [leave, entry], fetch_sems)
    refs = refs[:-3]
    came, refs = refs[: HALVES * pieces], refs[HALVES * pieces :]
    triples, weights, mixes, middles_back = [refs[HALVES * k : HALVES * (k + 1)] for k in range(4)]
    delta, outcome, away, own, sums, mixed_back, triple_back, held, sems = refs[4 * HALVES :]
    step = pl.program_id(0)
    each = rows_in.shape[1] // HALVES

    def results(piece):
        return [
            pltpu.make_async_copy(
                came[half * pieces + piece].at[RESULT],
                outcome.at[:, pl.ds(half * each, each)],
                sems.at[half],
            )
            for half in range(HALVES)
        ]

    @pl.when(step == 0)
    def _():
        fetched.start()
        sums[...] = jnp.zeros_like(sums)

    def add(tile, left, right):
        before = jnp.where(step == 0, 0.0, held[tile])
        held[tile] = before + dot_left(left, right)

    for piece in range(pieces):

        @pl.when(step == piece)
        def _(piece=piece):
            for copy in results(piece):
                copy.start()

    parts = [rows_in[:, half * each : (half + 1) * each].reshape(-1, D) for half in range(HALVES)]
    count = parts[0].shape[0]
    attend_back = side_by_side(middles_back)
    middle_back = attend_back.astype(FLOAT)
    fetched.need(0, 1)
    mixed_back[...] = dot_right(attend_back, leave[...]).astype(HALF)
    add(3, side_by_side(mixes), attend_back)
    unit, inverse = unit_of(jnp.concatenate(parts, axis=0).astype(FLOAT))
    normed = (unit * gain[...] + offset[...]).astype(HALF)
    for half in range(HALVES):
        span = pl.ds(half * count, count)
        back = triple_back.at[:, span]

        def put(rows, pair, part, value, back=back):
            back[part, rows, columns(pair)] = value

        attend_backward(triples[half], weights[half], mixed_back.at[span], put, count // window, window)
    normed_back = jnp.zeros_like(middle_back)
    for part in range(3):
        back = triple_back[part]
        normed_back = normed_back + dot_right(back, entry[:, part * D : (part + 1) * D])
        add(part, normed, back)
    sums[GAIN] += column_sum(normed_back * unit)
    sums[OFFSET] += column_sum(normed_back)
    rows_back = (middle_back + norm_back(normed_back * gain[...], unit, inverse)).astype(HALF)
    for half in range(HALVES):
        delta[:, half * each : (half + 1) * each] = rows_back[half * count : (half + 1) * count].reshape(
            -1, each, window, D
        )

    @pl.when(step == pl.num_programs(0) - 1)
    def _():
        pick(place[4], away, own, [held[tile].astype(HALF) for tile in range(4)])

    for piece in range(pieces):

        @pl.when(step == piece)
        def _(piece=piece):
            for copy in results(piece):
                copy.wait()


def attention_back(place, frames, params, came, triple, weights, mixed, middles_back, batch, after):
    pieces = len(came[0])
    per_group, windows, window, _ = frames.shape
    block = (per_group, windows // pieces, window, D)
    rows = per_group * block[1] * window // HALVES
    cut = pl.BlockSpec(block, lambda i, place: (0, place[0] ^ i, 0, 0))
    attended = (rows // window, PAIRS, window, 2 * window)
    halves = range(HALVES)
    spread_out = lambda half: lambda i, place: jnp.where(i < 2, 2 * i + half, i + (pieces if half else 2))
    ins = [(frames, cut)] + plain(params[:2]) + anywhere([params[3], params[2]])
    ins += [(array, pl.BlockSpec(memory_space=pl.ANY)) for half in came for array in half]
    ins += [(triple, row_spec(rows, 3 * D, lambda i, place, h=h: h * pieces + i)) for h in halves]
    ins += [
        (weights, pl.BlockSpec(attended, lambda i, place, h=h: (h * pieces + i, 0, 0, 0))) for h in halves
    ]
    ins += [(mixed, row_spec(rows, D, lambda i, place, h=h: h * pieces + i)) for h in halves]
    ins += [(middles_back, row_spec(rows, D, spread_out(h))) for h in halves]
    tiles = (2, batch, D // batch, CHUNK)
    count = rows * pieces * HALVES
    return run(
        functools.partial(attention_back_body, window=window, pieces=pieces),
        "attention_back",
        (pieces,),
        [place],
        ins,
        [
            (frames.shape, HALF, cut),
            (frames.shape, HALF, cut),
            *[(tiles, HALF, whole(tiles))] * 2,
            ((SUMS, 1, D), FLOAT, whole((SUMS, 1, D))),
        ],
        scratch=[
            pltpu.VMEM((rows * HALVES, D), HALF),
            pltpu.VMEM((3, rows * HALVES, D), HALF),
            pltpu.VMEM((4, CHUNK, CHUNK), FLOAT),
            pltpu.SemaphoreType.DMA((HALVES,)),
            *buffers_of([params[3], params[2]]),
        ],
        after=after,
        flops=16 * count * D * D,
        moved=count * D * 2 * (3 + 1 + 1 + 2 + 2 + 4),
    )


def swap(value, axis, mask):
    size = lax.axis_size(axis)
    if mask == 0:
        return value
    return lax.ppermute(value, axis, [(i, i ^ mask) for i in range(size)])


def move(value, batch_mask, win_mask):
    if batch_mask == 0:
        return swap(value, "win", win_mask)
    if win_mask == 0:
        return swap(value, "batch", batch_mask)
    batch, win = lax.axis_size("batch"), lax.axis_size("win")
    pairs = [
        (b * win + w, (b ^ batch_mask) * win + (w ^ win_mask)) for b in range(batch) for w in range(win)
    ]
    return lax.ppermute(value, ("batch", "win"), pairs)


def exchange(arrays):
    made = {k: swap(arrays[k], "win", k) for k in reversed(range(len(arrays)))}
    return [made[k] for k in range(len(arrays))]


def split_body(place, *refs, groups, alone, across):
    own, got, outs = refs[:groups], refs[groups : 2 * groups - alone], refs[2 * groups - alone :]
    got = [*got, *[None] * alone]
    column, row = place[1], place[2]
    width = CHUNK // across
    at = 0
    for one, two in zip(own, got):
        rows = one.shape[3]
        for tile in range(one.shape[0]):
            for piece, out in enumerate(outs):
                y = row ^ (piece % 2)
                x = pl.ds(pl.multiple_of((column ^ (piece // 2)) * width, width), width)
                total = one[tile, :, y, :, x]
                if two is not None:
                    total = (total.astype(FLOAT) + two[tile, :, y, :, x].astype(FLOAT)).astype(HALF)
                out[:, at : at + rows] = total
            at += rows


def total_of(refs, index):
    total = refs[0][index].astype(FLOAT)
    for ref in refs[1:]:
        total = total + ref[index].astype(FLOAT)
    return total.astype(HALF)


def merge_body(place, *refs, inputs):
    ins, outs = refs[:inputs], refs[inputs:]
    for piece, out in enumerate(outs):
        out[...] = total_of(ins, place[3] ^ piece)


def pair_body(place, *refs, inputs, bit):
    ins, outs = refs[:inputs], refs[inputs:]
    mine = (place[3] >> bit) & 1
    for side, out in zip((mine, 1 - mine), outs):
        out[...] = total_of(ins, (slice(None), side))


def last_body(*refs, sets):
    ins, out = refs[:-1], refs[-1]
    at, start = 0, 0
    for size in sets:
        rows, width = ins[at].shape[-2:]
        made = [ref.reshape(rows, width) for ref in ins[at : at + size]]
        out[start : start + rows] = total_of(made, slice(None))
        at += size
        start += rows


def unpack_body(place, *refs, pieces, across, layout):
    ins, outs, held = refs[:pieces], refs[pieces:-1], refs[-1]
    width = CHUNK // across
    for piece, ref in enumerate(ins):
        x = pl.ds(pl.multiple_of((place[1] ^ (piece // 2)) * width, width), width)
        held[place[4] ^ (piece % 2), :, x] = ref[...].astype(FLOAT)
    for out, places in zip(outs, layout):
        for core, start, rows, left, wide, row, column in places:
            here = (slice(start, start + rows), slice(left, left + wide))
            value = held[(0, *here)] + held[(1, *here)] if core is None else held[(core, *here)]
            out[row : row + rows, column : column + wide] = value


def arrived_body(*refs):
    refs[-1][...] = jnp.zeros_like(refs[-1])


def arrived(arrays):
    shape = (8, 128)
    outs = [(shape, FLOAT, whole(shape))]
    return run(
        arrived_body, "arrived", (1,), [], [], outs, after=arrays, flops=LONG_FLOPS, vmem=SMALL_VMEM
    )


class Reduction:
    def __init__(self, place, away, own, alone=()):
        self.place = place
        self.batch, self.win = lax.axis_size("batch"), lax.axis_size("win")
        self.across, self.depth = self.win // 2, self.batch // 2
        cut = lambda a: a.reshape(-1, self.depth, 2, *a.shape[2:])
        self.own = [cut(a) for a in (*own, *alone)]
        self.alone = len(alone)
        self.got = [swap(cut(a), "win", 1) for a in away]
        self.rows = sum(a.shape[0] * a.shape[3] for a in self.own)
        self.width = CHUNK // self.across
        self.vmem = VMEM

    def cores(self, after=()):
        shape = (self.depth, self.rows, self.width)
        pieces = run(
            functools.partial(split_body, groups=len(self.own), alone=self.alone, across=self.across),
            "sum_cores",
            (1,),
            [self.place],
            plain(self.own + self.got),
            [(shape, HALF, whole(shape))] * (2 * self.across),
            after=after,
            vmem=self.vmem,
            flops=SMALL_FLOPS,
        )
        self.mark = pieces[:1]
        self.pieces = [move(a, number % 2, 2 * (number // 2)) for number, a in enumerate(pieces)]

    def chips(self, after=(), flops=SMALL_FLOPS):
        shape = (self.rows, self.width)
        pieces = run(
            functools.partial(merge_body, inputs=len(self.pieces)),
            "sum_chips",
            (1,),
            [self.place],
            plain(self.pieces),
            [(shape, HALF, whole(shape))] * self.depth,
            after=after,
            vmem=self.vmem,
            flops=flops,
        )
        self.mark = pieces[:1]
        self.pieces = [swap(a, "batch", 2 * number) for number, a in enumerate(pieces)]

    def pair(self, bit, after=(), flops=SMALL_FLOPS):
        depth, rows, width = self.pieces[0].shape
        shape = (depth // 2, rows, width)
        kept, away = run(
            functools.partial(pair_body, inputs=len(self.pieces), bit=bit),
            "sum_pairs",
            (1,),
            [self.place],
            plain([a.reshape(depth // 2, 2, rows, width) for a in self.pieces]),
            [(shape, HALF, whole(shape))] * 2,
            after=after,
            vmem=self.vmem,
            flops=flops,
        )
        self.mark = [kept]
        self.pieces = [kept, swap(away, "batch", 2 << bit)]

    def last(self, after=(), other=None, flops=SMALL_FLOPS):
        groups = [self] if other is None else [other, self]
        self.rows = sum(group.rows for group in groups)
        shape = (self.rows, self.width)
        (total,) = run(
            functools.partial(last_body, sets=[len(group.pieces) for group in groups]),
            "sum_last",
            (1,),
            [],
            plain([a for group in groups for a in group.pieces]),
            [(shape, HALF, whole(shape))],
            after=after,
            vmem=self.vmem,
            flops=flops,
        )
        self.mark = [total]
        across = [swap(total, "win", 2 * number) for number in range(self.across)]
        self.pieces = [a if side == 0 else swap(a, "win", 1) for a in across for side in range(2)]

    def unpack(self, layout, shapes, after=()):
        return run(
            functools.partial(
                unpack_body, pieces=self.win, across=self.across, layout=layout
            ),
            "unpack",
            (1,),
            [self.place],
            plain(self.pieces),
            [(s, FLOAT, whole(s)) for s in shapes],
            scratch=[pltpu.VMEM((2, self.rows, CHUNK), FLOAT)],
            after=after,
            vmem=self.vmem,
            flops=SMALL_FLOPS,
        )


SMALL_ROWS = 16


def small_body(*refs, blocks):
    out = refs[-1]
    sums, at = [], 0
    for size in blocks:
        sums.append(total_in(refs[at : at + size]))
        at += size
    _, batch, _, width = out.shape
    rows = D // batch
    wide = lambda parts: jnp.concatenate(
        [*parts, jnp.zeros((1, width - sum(p.shape[1] for p in parts)), FLOAT)], axis=1
    )
    for shard in range(batch):
        made = []
        for total in sums:
            made.append(wide([total[n][:, shard * rows : (shard + 1) * rows] for n in range(6)]))
        for total in sums:
            chunk, start = divmod(shard * 4 * rows, CHUNK)
            made.append(wide([total[LIFT + chunk][:, start : start + 4 * rows]]))
        made.append(jnp.zeros((SMALL_ROWS - len(made), width), FLOAT))
        out[0, shard] = jnp.concatenate(made, axis=0).astype(HALF)


def total_in(refs):
    total = refs[0][...]
    for ref in refs[1:]:
        total = total + ref[...]
    return total


def small_tiles(blocks, batch):
    shape = (1, batch, SMALL_ROWS, CHUNK)
    (out,) = run(
        functools.partial(small_body, blocks=[len(sums) for sums in blocks]),
        "small_tiles",
        (1,),
        [],
        plain([a for sums in blocks for a in sums]),
        [(shape, HALF, whole(shape))],
        vmem=SMALL_VMEM,
    )
    return out


def attend_places(rows, start):
    spot = lambda tile: (tile // 2, start + tile % 2 * rows, rows, 0, CHUNK)
    return [
        [(*spot(part), 0, part * CHUNK) for part in range(3)],
        [(*spot(3), 0, 0)],
    ], [(rows, 3 * D), (rows, D)]


def feed_places(rows, start):
    narrows = [(sub // 2, start + sub % 2 * rows, rows, 0, CHUNK, sub * rows, 0) for sub in range(4)]
    start += 2 * rows
    widens = [
        (chunk // 2, start + chunk % 2 * rows, rows, 0, CHUNK, 0, chunk * CHUNK) for chunk in range(CHUNKS)
    ]
    return [widens, narrows], [(rows, FF), (4 * rows, D)]


def small_places(rows, start):
    layout, shapes = [], []
    for block in range(2):
        layout += [[(None, start + block, 1, number * rows, rows, 0, 0)] for number in range(6)]
        layout.append([(None, start + 2 + block, 1, 0, 4 * rows, 0, 0)])
        shapes += [(1, rows)] * 6 + [(1, 4 * rows)]
    return layout, shapes


def local(*args):
    frames, cotangent, video_frames = args[0], args[23], args[24]
    space = [a.reshape(1, -1) if a.ndim == 1 else a for a in args[1:12]]
    time = [a.reshape(1, -1) if a.ndim == 1 else a for a in args[12:23]]
    batch, win = lax.axis_size("batch"), lax.axis_size("win")
    here, group = lax.axis_index("win"), lax.axis_index("batch")
    core = here % 2
    place = jnp.stack([here, here // 2, group % 2, group // 2, core]).astype(jnp.int32)
    _, per_group, _, windows, window, _ = frames.shape
    shape = (per_group, windows, window, D)
    rows_in, cotangent = frames.reshape(shape), cotangent.reshape(shape)
    rows = D // batch

    kept, came = [], []
    for half in range(HALVES):
        sent, kept = space_forward(place, rows_in, cotangent, space, half, win, kept)
        came.append(exchange(sent))
    triple, weights, mixed, middles, hiddens = kept
    backs, time_sums, tiles = [], [], [None]
    for half in range(HALVES):
        sent, tiles, sums = time_block(place, video_frames, came[half], time, batch, *tiles)
        backs.append(exchange(sent))
        time_sums.append(sums)

    bits = (batch // 2).bit_length() - 1
    time_sum = Reduction(place, tiles[:1], tiles[1:])
    time_sum.cores(arrived(backs[0][1:]))
    *fed, first_sums = feed_back(place, space, backs, middles, hiddens, batch, after=time_sum.mark)
    middles_back, away, own, feed_sums = feed_back(place, space, backs, middles, hiddens, batch, fed)
    feed_sum = Reduction(place, [away], [own])
    time_sum.pair(0, [feed_sums], LONG_FLOPS)
    feed_sum.cores(time_sum.mark)
    delta, outcome, away, own, attend_sums = attention_back(
        place, rows_in, space, backs, triple, weights, mixed, middles_back, batch, feed_sum.mark
    )
    time_sum.vmem = feed_sum.vmem = SMALL_VMEM
    small = small_tiles([[first_sums, feed_sums, attend_sums], time_sums], batch)
    attend_sum = Reduction(place, [away], [own], [small])
    attend_sum.vmem = SMALL_VMEM
    feed_sum.pair(0, [attend_sums], LONG_FLOPS)
    attend_sum.cores(feed_sum.mark)
    mark = attend_sum.mark
    for bit in range(1, bits):
        time_sum.pair(bit, mark)
        feed_sum.pair(bit, time_sum.mark)
        mark = feed_sum.mark
    attend_sum.chips(mark)
    time_rows = time_sum.rows
    feed_sum.last(attend_sum.mark, time_sum, 0)
    attend_sum.last(feed_sum.mark)
    feed_layout, feed_shapes = feed_places(rows, 0)
    attend_layout, attend_shapes = attend_places(rows, 4 * rows)
    last_layout, last_shapes = feed_places(rows, time_rows)
    made = feed_sum.unpack(
        feed_layout + attend_layout + last_layout,
        feed_shapes + attend_shapes + last_shapes,
        attend_sum.mark,
    )
    time_grads, feed_grads = made[:4], made[4:]
    attend_layout, attend_shapes = attend_places(rows, 0)
    small_layout, small_shapes = small_places(rows, 2 * rows)
    attend_grads = attend_sum.unpack(attend_layout + small_layout, attend_shapes + small_shapes)
    smalls = [a.reshape(-1) for a in attend_grads[2:]]

    def collected(grads, smalls):
        widen, narrow, entry, leave = grads
        gain, offset, bias, weigh, shift, nudge, lift = smalls
        return gain, offset, entry, leave, bias, weigh, shift, widen, lift, narrow, nudge

    return (
        outcome.reshape(frames.shape),
        delta.reshape(frames.shape),
        *collected([*feed_grads, *attend_grads[:2]], smalls[:7]),
        *collected(time_grads, smalls[7:]),
    )


def solution(mesh):
    rows = P("batch", None, "win", None, None, None)
    one, two = P("batch"), P("batch", None)
    grads = (one, one, two, two, one, one, one, two, one, two, one)
    return jax.shard_map(
        local,
        mesh=mesh,
        in_specs=(rows, *([P()] * 22), rows, P("batch", None)),
        out_specs=(rows, rows, *grads, *grads),
        check_vma=False,
    )
```

```python
import functools

import jax
import jax.numpy as jnp
from jax import lax
from jax.experimental import pallas as pl
from jax.experimental.pallas import tpu as pltpu
from jax.sharding import PartitionSpec as P

D = 512
HEADS = 8
HDIM = 64
FF = 2048
PAIR = 2 * HDIM
PAIRS = HEADS // 2
CHUNK = 512
CHUNKS = FF // CHUNK
EPS = 1e-05
NEGATIVE = -1e30
FLOAT = jnp.float32
HALF = jnp.bfloat16
HALVES = 2
UNITS = 16
VMEM = 127 << 19
SMALL_VMEM = 24 << 20
LONG_FLOPS = 10**11
SMALL_FLOPS = 2 * 10**8
SLOWER = 4

NARROW, WIDEN, ENTRY, EXIT = 0, CHUNKS, 2 * CHUNKS, 2 * CHUNKS + 3
TILES = 2 * CHUNKS + 4
SHARED = [WIDEN, WIDEN + 1, ENTRY, ENTRY + 1, WIDEN + 2, WIDEN + 3, ENTRY + 2, EXIT]
INNER, COTANGENT = 0, 1
BACK, RESULT = 0, 1
GAIN, OFFSET, BIAS, WEIGH, SHIFT, NUDGE, LIFT = 0, 1, 2, 3, 4, 5, 6
SUMS = 6 + CHUNKS


def dot(left, right):
    return lax.dot_general(left, right, (((1,), (0,)), ((), ())), preferred_element_type=FLOAT)


def dot_right(left, right):
    return lax.dot_general(left, right, (((1,), (1,)), ((), ())), preferred_element_type=FLOAT)


def dot_left(left, right):
    return lax.dot_general(left, right, (((0,), (0,)), ((), ())), preferred_element_type=FLOAT)


def unit_of(rows):
    centre = rows - jnp.mean(rows, axis=-1, keepdims=True)
    inverse = lax.rsqrt(jnp.mean(centre * centre, axis=-1, keepdims=True) + EPS)
    return centre * inverse, inverse


def norm_back(scaled, unit, inverse):
    return inverse * (
        scaled
        - jnp.mean(scaled, axis=-1, keepdims=True)
        - unit * jnp.mean(scaled * unit, axis=-1, keepdims=True)
    )


def gelu_pair(hidden):
    half = 0.5 * lax.erf(hidden * 0.7071067811865476) + 0.5
    bell = jnp.exp(hidden * hidden * -0.5) * 0.3989422804014327
    return hidden * half, half + hidden * bell


def gelu_of(hidden):
    return hidden * (0.5 * lax.erf(hidden * 0.7071067811865476) + 0.5)


def column_sum(values):
    return jnp.sum(values, axis=0, keepdims=True)


def first_head(rows):
    return lax.broadcasted_iota(jnp.int32, (rows, PAIR), 1) < HDIM


def spread(pair, first):
    zero = jnp.zeros_like(pair)
    return jnp.concatenate([jnp.where(first, pair, zero), jnp.where(first, zero, pair)], axis=0)


def gathered(both, first, rows):
    return jnp.where(first, both[:rows], both[rows:])


def attend_units(blocks):
    units = [(block, pair) for block in range(blocks) for pair in range(PAIRS)]
    return [units[start : start + UNITS] for start in range(0, len(units), UNITS)]


def columns(pair, part=0):
    start = part * D + pair * PAIR
    return slice(start, start + PAIR)


def attend_forward(triple, mixed, weights, blocks, rows, mask):
    first = first_head(rows)
    for units in attend_units(blocks):
        spans = [slice(block * rows, block * rows + rows) for block, _ in units]
        queries = [spread(triple[s, columns(p)], first) for s, (_, p) in zip(spans, units)]
        scores = [dot_right(triple[s, columns(p, 1)], q) for q, s, (_, p) in zip(queries, spans, units)]
        if mask is not None:
            scores = [score + mask for score in scores]
        powers = [
            jnp.exp((score - jnp.max(score, axis=0, keepdims=True)) * HDIM ** (-0.5)) for score in scores
        ]
        probs = [
            (power * (1.0 / jnp.sum(power, axis=0, keepdims=True))).astype(HALF) for power in powers
        ]
        both = [dot_left(prob, triple[s, columns(p, 2)]) for prob, s, (_, p) in zip(probs, spans, units)]
        for value, prob, s, (block, p) in zip(both, probs, spans, units):
            weights[block, p] = prob
            mixed[s, columns(p)] = gathered(value, first, rows).astype(HALF)


def attend_backward(triple, weights, mixed_back, put, blocks, rows):
    first = first_head(rows)
    scale = HDIM ** (-0.5)
    for units in attend_units(blocks):
        spans = [slice(block * rows, block * rows + rows) for block, _ in units]
        mixes = [spread(mixed_back[s, columns(p)], first) for s, (_, p) in zip(spans, units)]
        probs = [weights[block, p] for block, p in units]
        values_back = [dot(prob, mix) for prob, mix in zip(probs, mixes)]
        weights_back = [
            dot_right(triple[s, columns(p, 2)], mix) for mix, s, (_, p) in zip(mixes, spans, units)
        ]
        scores_back = []
        for prob, back in zip(probs, weights_back):
            wide = prob.astype(FLOAT)
            inside = back - jnp.sum(back * wide, axis=0, keepdims=True)
            scores_back.append((wide * inside * scale).astype(HALF))
        queries = [spread(triple[s, columns(p)], first) for s, (_, p) in zip(spans, units)]
        keys_back = [dot(score, query) for score, query in zip(scores_back, queries)]
        both = [
            dot_left(score, triple[s, columns(p, 1)])
            for score, s, (_, p) in zip(scores_back, spans, units)
        ]
        for key, value, pair, s, (_, p) in zip(keys_back, values_back, both, spans, units):
            put(s, p, 0, gathered(pair, first, rows).astype(HALF))
            put(s, p, 1, key.astype(HALF))
            put(s, p, 2, value.astype(HALF))


def whole(shape):
    return pl.BlockSpec(shape, lambda *_: (0,) * len(shape), pipeline_mode=pl.Buffered(1))


def run(body, name, grid, scalars, ins, outs, scratch=(), aliases=None, after=(), flops=0, moved=0, vmem=VMEM):
    aliases = aliases or {}
    unread = pl.BlockSpec(memory_space=pl.ANY)
    first = len(scalars) + len(ins)
    extra = [*aliases.values(), *after]

    def inner(*refs):
        body(*refs[:first], *refs[first + len(extra) :])

    return pl.pallas_call(
        inner,
        out_shape=[jax.ShapeDtypeStruct(shape, kind) for shape, kind, _ in outs],
        grid_spec=pltpu.PrefetchScalarGridSpec(
            num_scalar_prefetch=len(scalars),
            grid=grid,
            in_specs=[spec for _, spec in ins] + [unread] * len(extra),
            out_specs=[spec for _, _, spec in outs],
            scratch_shapes=list(scratch),
        ),
        input_output_aliases={first + at: out for at, out in enumerate(aliases)},
        compiler_params=pltpu.CompilerParams(vmem_limit_bytes=vmem),
        cost_estimate=pl.CostEstimate(flops=flops * SLOWER, bytes_accessed=moved * SLOWER, transcendentals=0),
        name=name,
    )(*scalars, *[array for array, _ in ins], *extra)


class Fetched:
    def __init__(self, sources, buffers, sems):
        self.copies = [
            pltpu.make_async_copy(source, buffer, sems.at[number])
            for number, (source, buffer) in enumerate(zip(sources, buffers))
        ]

    def start(self):
        for copy in self.copies:
            copy.start()

    def need(self, *numbers):
        @pl.when(pl.program_id(0) == 0)
        def _():
            for number in numbers:
                self.copies[number].wait()


def anywhere(arrays):
    return [(array, pl.BlockSpec(memory_space=pl.ANY)) for array in arrays]


def buffers_of(arrays):
    return [pltpu.VMEM(a.shape, a.dtype) for a in arrays] + [pltpu.SemaphoreType.DMA((len(arrays),))]


def plain(arrays):
    return [(array, whole(array.shape)) for array in arrays]


def slab_spec(slabs, rows, at):
    return pl.BlockSpec((slabs, rows, D), lambda *i: (0, at(*i), 0))


def row_spec(rows, width, at):
    return pl.BlockSpec((rows, width), lambda *i: (at(*i), 0))


def vectors_of(params):
    return [param for param in params if param.shape[0] == 1]


def weights_of(params):
    return [param for param in params if param.shape[0] > 1]


def space_forward_body(place, *refs, window, pieces):
    ins, cotangents, refs = refs[:2], refs[2:4], refs[4:]
    gain, offset, bias, weigh, shift, lift, nudge = refs[:7]
    sent = refs[11 : 11 + pieces]
    triple, weights, mixed, middles, hiddens, *buffers, sems = refs[11 + pieces :]
    entry, leave, widen, narrow = buffers
    fetched = Fetched(refs[7:11], buffers, sems)
    step = pl.program_id(0)

    @pl.when(step == 0)
    def _():
        fetched.start()

    shape = ins[0].shape
    rows = jnp.concatenate([ref[...].reshape(-1, D) for ref in ins], axis=0).astype(FLOAT)
    count = rows.shape[0]
    unit, _ = unit_of(rows)
    normed = (unit * gain[...] + offset[...]).astype(HALF)
    fetched.need(0)
    triple[...] = dot(normed, entry[...]).astype(HALF)
    attend_forward(triple, mixed, weights, count // window, window, None)
    fetched.need(1, 2, 3)
    middle = rows + dot(mixed[...], leave[...]) + bias[...]
    middles[...] = middle.astype(HALF)
    unit_two, _ = unit_of(middle)
    second = (unit_two * weigh[...] + shift[...]).astype(HALF)
    total = middle + nudge[...]
    for chunk in range(CHUNKS):
        at = slice(chunk * CHUNK, (chunk + 1) * CHUNK)
        hidden = dot(second, widen[:, at]) + lift[:, at]
        hiddens[:, at] = hidden.astype(HALF)
        total = total + dot(gelu_of(hidden).astype(HALF), narrow[at, :])
    inner = total.astype(HALF).reshape(2, *shape)
    for piece in range(pieces):

        @pl.when(step == piece // 2)
        def _(piece=piece):
            sent[piece][INNER] = inner[piece % 2]
            sent[piece][COTANGENT] = cotangents[piece % 2][...]


def space_forward(place, frames, cotangent, params, half, pieces, before):
    per_group, windows, window, _ = frames.shape
    each = windows // pieces // HALVES
    block = (per_group, each, window, D)
    rows = per_group * each * window
    count = rows * pieces * HALVES
    cuts = [
        pl.BlockSpec(block, lambda i, place, side=side: (0, (place[0] ^ (2 * i + side)) * HALVES + half, 0, 0))
        for side in range(2)
    ]
    rows *= 2
    at = lambda i, place: half * pieces // 2 + i
    attended = (rows // window, PAIRS, window, 2 * window)
    both = (2, *block)
    outs = [(both, HALF, pl.BlockSpec(both, lambda i, place: (0,) * 5))] * pieces
    outs += [
        ((count, 3 * D), HALF, row_spec(rows, 3 * D, at)),
        (
            (count // window, *attended[1:]),
            HALF,
            pl.BlockSpec(attended, lambda i, place: (at(i, place), 0, 0, 0)),
        ),
        ((count, D), HALF, row_spec(rows, D, at)),
        ((count, D), HALF, row_spec(rows, D, at)),
        ((count, FF), HALF, row_spec(rows, FF, at)),
    ]
    made = run(
        functools.partial(space_forward_body, window=window, pieces=pieces),
        "space_forward",
        (pieces // 2,),
        [place],
        [(a, cut) for a in (frames, cotangent) for cut in cuts] + plain(vectors_of(params)) + anywhere(weights_of(params)),
        outs,
        scratch=buffers_of(weights_of(params)),
        aliases={pieces + number: array for number, array in enumerate(before)},
        flops=rows * pieces * D * (4 * D + 2 * FF),
        moved=rows * pieces * (4 * D + 6 * D + FF),
    )
    return made[:pieces], made[pieces:]


def by_position(refs, which, frames_of, positions):
    parts = [ref[which, frame].astype(FLOAT) for ref in refs for frame in range(frames_of)]
    return jnp.concatenate(
        [part[start : start + 8] for start in range(0, positions, 8) for part in parts], axis=0
    )


def by_frame(values, refs, which, frames_of, positions):
    total = len(refs) * frames_of
    for at, ref in enumerate(refs):
        for frame in range(frames_of):
            number = at * frames_of + frame
            ref[which, frame] = jnp.concatenate(
                [
                    values[(group * total + number) * 8 : (group * total + number) * 8 + 8]
                    for group in range(positions // 8)
                ],
                axis=0,
            ).astype(HALF)


def fill_mask(mask, place, lengths, per_group, pieces):
    window = mask.shape[0]
    key = lax.broadcasted_iota(jnp.int32, mask.shape, 0)
    query = lax.broadcasted_iota(jnp.int32, mask.shape, 1) % window
    frames = []
    for row in (query, key):
        number = row // 8
        frames.append((number % per_group) * pieces + ((number // per_group) ^ place[0]))
    videos = [jnp.zeros_like(frame) for frame in frames]
    entries = lengths.shape[1]
    end = 0
    for entry in range(entries):
        end = end + lengths[0, entry]
        videos = [v + (f >= end).astype(jnp.int32) for v, f in zip(videos, frames)]
    videos = [jnp.where(f < end, v, entries + f) for v, f in zip(videos, frames)]
    allowed = (videos[0] == videos[1]) & (frames[1] <= frames[0]) & (query % 8 == key % 8)
    mask[...] = jnp.where(allowed, 0.0, NEGATIVE)


def shared_copies(tile, core, stage, away, own, sems):
    _, batch, rows, _ = own.shape
    made = []
    if tile < WIDEN:
        shards = batch // CHUNKS
        source = stage.at[tile].reshape(shards, 4, rows, CHUNK)
        at = pl.ds(tile * shards, shards)
        for sub in range(4):
            target = own if sub // 2 == core else away
            made.append((source.at[:, sub], target.at[sub % 2, at]))
    else:
        place = SHARED.index(tile)
        target = own if place // 4 == core else away
        made.append((stage.at[tile].reshape(batch, rows, CHUNK), target.at[2 + place % 4]))
    return [
        pltpu.make_async_copy(source, target, sems.at[tile, number])
        for number, (source, target) in enumerate(made)
    ]


def time_body(place, lengths, *refs, pieces, last, steps):
    came = refs[:pieces]
    gain, offset, bias, weigh, shift, lift, nudge = refs[pieces : pieces + 7]
    entry, leave, widen, narrow, fetch_sems = refs[-5:]
    fetched = Fetched(refs[pieces + 7 : pieces + 11], [entry, leave, widen, narrow], fetch_sems)
    refs = refs[pieces + 11 : -5]
    if last:
        partial, refs = refs[0], refs[1:]
    sent, refs = refs[:pieces], refs[pieces:]
    grads, refs = refs[: 1 + last], refs[1 + last :]
    sums, triple, weights, mixed, mixed_back, triple_back, mask, stage, sems, came_sem, *held = refs
    held = held[0] if held else None
    _, frames_of, positions, _ = came[0].shape
    window = 8 * pieces * frames_of
    rows = by_position(came, INNER, frames_of, positions)
    blocks = rows.shape[0] // window
    step = pl.program_id(0)

    @pl.when(step == 0)
    def _():
        fetched.start()
        sums[...] = jnp.zeros_like(sums)
        fill_mask(mask, place, lengths, frames_of, pieces)
        if last:
            pltpu.make_async_copy(partial, stage, came_sem).start()

    def each_copy(tile, act):
        if not last:
            act(pltpu.make_async_copy(stage.at[tile], grads[0].at[tile], sems.at[tile, 0]))
            return
        for core in range(2):

            @pl.when(place[4] == core)
            def _(core=core):
                for copy in shared_copies(tile, core, stage, *grads, sems):
                    act(copy)

    def done(tiles):
        @pl.when(step == pl.num_programs(0) - 1)
        def _():
            if last and steps > 1 and tiles[0] == 0:
                pltpu.make_async_copy(partial, stage, came_sem).wait()
            for tile in tiles:
                if steps > 1:
                    finish(tile, held[tile])
                each_copy(tile, lambda copy: copy.start())

    def finish(tile, value):
        if last:
            value = value + stage[tile].astype(FLOAT)
        stage[tile] = value.astype(HALF)

    def add(tile, left, right):
        if steps == 1:
            finish(tile, dot_left(left, right))
            return
        before = jnp.where(step == 0, 0.0, held[tile])
        held[tile] = before + dot_left(left, right)

    unit, inverse = unit_of(rows)
    normed = (unit * gain[...] + offset[...]).astype(HALF)
    fetched.need(0)
    triple[...] = dot(normed, entry[...]).astype(HALF)
    attend_forward(triple, mixed, weights, blocks, window, mask[...])
    fetched.need(1, 2, 3)
    middle = rows + dot(mixed[...], leave[...]) + bias[...]
    unit_two, inverse_two = unit_of(middle)
    second = (unit_two * weigh[...] + shift[...]).astype(HALF)
    upstream = by_position(came, COTANGENT, frames_of, positions)
    branch_back = upstream.astype(HALF)
    sums[NUDGE] += column_sum(upstream)
    total = middle + nudge[...]
    second_back = jnp.zeros_like(middle)
    if last and steps == 1:
        pltpu.make_async_copy(partial, stage, came_sem).wait()
    for chunk in range(CHUNKS):
        at = slice(chunk * CHUNK, (chunk + 1) * CHUNK)
        active, slope = gelu_pair(dot(second, widen[:, at]) + lift[:, at])
        active = active.astype(HALF)
        hidden_back = dot_right(branch_back, narrow[at, :]) * slope
        hidden_low = hidden_back.astype(HALF)
        sums[LIFT + chunk] += column_sum(hidden_back)
        total = total + dot(active, narrow[at, :])
        second_back = second_back + dot_right(hidden_low, widen[:, at])
        add(NARROW + chunk, active, branch_back)
        add(WIDEN + chunk, second, hidden_low)
    done(range(ENTRY))
    by_frame(total, sent, RESULT, frames_of, positions)
    sums[WEIGH] += column_sum(second_back * unit_two)
    sums[SHIFT] += column_sum(second_back)
    middle_back = upstream + norm_back(second_back * weigh[...], unit_two, inverse_two)
    attend_back = middle_back.astype(HALF)
    sums[BIAS] += column_sum(middle_back)
    mixed_back[...] = dot_right(attend_back, leave[...]).astype(HALF)
    add(EXIT, mixed[...], attend_back)

    def put(span, pair, part, value):
        triple_back[part, span, columns(pair)] = value

    attend_backward(triple, weights, mixed_back, put, blocks, window)
    normed_back = jnp.zeros_like(middle)
    for part in range(3):
        back = triple_back[part]
        normed_back = normed_back + dot_right(back, entry[:, part * D : (part + 1) * D])
        add(ENTRY + part, normed, back)
    sums[GAIN] += column_sum(normed_back * unit)
    sums[OFFSET] += column_sum(normed_back)
    rows_back = middle_back + norm_back(normed_back * gain[...], unit, inverse)
    by_frame(rows_back, sent, BACK, frames_of, positions)

    done(range(ENTRY, TILES))

    @pl.when(step == pl.num_programs(0) - 1)
    def _():
        for tile in range(TILES):
            each_copy(tile, lambda copy: copy.wait())


def time_block(place, lengths, came, params, batch, partial=None, step_rows=1024):
    pieces = len(came)
    _, per_group, each, window, _ = came[0].shape
    positions = each * window
    flat = (2, per_group, positions, D)
    frames = per_group * pieces
    together = min(max(step_rows // frames, 16), positions)
    rows = together * frames
    steps = positions // together
    count = positions * frames
    attended = 8 * frames
    last = partial is not None
    spec = pl.BlockSpec((2, per_group, together, D), lambda i, *_: (0, 0, i, 0))
    grads = (TILES // 2, batch, D // batch, CHUNK) if last else (TILES, CHUNK, CHUNK)
    outs = [(flat, HALF, spec)] * pieces
    outs += [(grads, HALF, pl.BlockSpec(memory_space=pl.ANY))] * (1 + last)
    outs += [((SUMS, 1, D), FLOAT, whole((SUMS, 1, D)))]
    ins = [(array.reshape(flat), spec) for array in came] + plain(vectors_of(params))
    ins += anywhere(weights_of(params))
    if last:
        ins += anywhere([partial])
    made = run(
        functools.partial(time_body, pieces=pieces, last=last, steps=steps),
        "time_block",
        (steps,),
        [place, lengths],
        ins,
        outs,
        scratch=[
            pltpu.VMEM((rows, 3 * D), HALF),
            pltpu.VMEM((rows // attended, PAIRS, attended, 2 * attended), HALF),
            pltpu.VMEM((rows, D), HALF),
            pltpu.VMEM((rows, D), HALF),
            pltpu.VMEM((3, rows, D), HALF),
            pltpu.VMEM((attended, 2 * attended), FLOAT),
            pltpu.VMEM((TILES, CHUNK, CHUNK), HALF),
            pltpu.SemaphoreType.DMA((TILES, 8)),
            pltpu.SemaphoreType.DMA,
            *[pltpu.VMEM((TILES, CHUNK, CHUNK), FLOAT)] * (steps > 1),
            *buffers_of(weights_of(params)),
        ],
        flops=6 * count * D * (4 * D + 2 * FF),
        moved=count * 2 * D * 4 + 2 * D * (4 * D + 2 * FF),
    )
    shape = (2, per_group, each, window, D)
    sent = [array.reshape(shape) for array in made[:pieces]]
    return sent, made[pieces:-1], made[-1]


def side_by_side(refs, index=slice(None)):
    return jnp.concatenate([ref[index] for ref in refs], axis=0)


def pick(core, away, own, tiles):
    size = len(tiles) // 2
    for number in range(size):
        one, two = tiles[number], tiles[size + number]
        own[number] = jnp.where(core == 0, one, two).reshape(own.shape[1:])
        away[number] = jnp.where(core == 0, two, one).reshape(away.shape[1:])


def feed_back_body(place, weigh, shift, narrow_in, widen_in, *refs, arrays, steps, last):
    narrow, widen, fetch_sems = refs[-3:]
    fetched = Fetched([narrow_in, widen_in], [narrow, widen], fetch_sems)
    came, refs = refs[:arrays], refs[arrays:-3]
    middles, hiddens, refs = refs[:2], refs[2:4], refs[4:]
    if last:
        partial, refs = refs[0], refs[1:]
    middles_back, refs = refs[0], refs[1:]
    if last:
        away, own, sums, arrived, held, sems, stage, stage_sem = refs
    else:
        tiles, sums, arrived, held, sems = refs
    step = pl.program_id(0)

    def coming(number):
        return [
            pltpu.make_async_copy(
                came[number * 2 + side].at[BACK], arrived.at[number % 2, side], sems.at[number % 2, side]
            )
            for side in range(2)
        ]

    @pl.when(step == 0)
    def _():
        for copy in coming(0):
            copy.start()
        fetched.start()
        if last:
            pltpu.make_async_copy(partial, stage, stage_sem).start()
        sums[...] = jnp.zeros_like(sums)
        held[...] = jnp.zeros_like(held)

    for number in range(steps):

        @pl.when(step == number)
        def _(number=number):
            for copy in coming(number):
                copy.wait()
            if number + 1 < steps:
                for copy in coming(number + 1):
                    copy.start()

    branch_back = arrived[step % 2].reshape(-1, D)
    upstream = branch_back.astype(FLOAT)
    unit_two, inverse_two = unit_of(side_by_side(middles).astype(FLOAT))
    second = (unit_two * weigh[...] + shift[...]).astype(HALF)
    sums[NUDGE] += column_sum(upstream)
    second_back = jnp.zeros_like(upstream)
    fetched.need(0, 1)
    for chunk in range(CHUNKS):
        at = slice(chunk * CHUNK, (chunk + 1) * CHUNK)
        active, slope = gelu_pair(side_by_side(hiddens, (slice(None), at)).astype(FLOAT))
        hidden_back = dot_right(branch_back, narrow[at, :]) * slope
        hidden_low = hidden_back.astype(HALF)
        sums[LIFT + chunk] += column_sum(hidden_back)
        second_back = second_back + dot_right(hidden_low, widen[:, at])
        held[NARROW + chunk] += dot_left(active.astype(HALF), branch_back)
        held[WIDEN + chunk] += dot_left(second, hidden_low)
    sums[WEIGH] += column_sum(second_back * unit_two)
    sums[SHIFT] += column_sum(second_back)
    middle_back = upstream + norm_back(second_back * weigh[...], unit_two, inverse_two)
    middles_back[...] = middle_back.astype(HALF)
    sums[BIAS] += column_sum(middle_back)

    @pl.when(step == steps - 1)
    def _():
        if not last:
            tiles[...] = held[...].astype(HALF)
            return
        pltpu.make_async_copy(partial, stage, stage_sem).wait()
        value = lambda tile: (held[tile] + stage[tile].astype(FLOAT)).astype(HALF)
        tail = pl.ds(2, 2)
        pick(place[4], away.at[tail], own.at[tail], [value(WIDEN + chunk) for chunk in range(CHUNKS)])
        _, batch, rows, _ = own.shape
        shards = batch // CHUNKS
        for chunk in range(CHUNKS):
            parts = value(NARROW + chunk).reshape(shards, 4, rows, CHUNK)
            at = pl.ds(chunk * shards, shards)
            pick(place[4], away.at[:, at], own.at[:, at], [parts[:, sub] for sub in range(4)])


def feed_back(place, params, came, middles, hiddens, batch, before=None, after=()):
    pieces = len(came[0])
    part = came[0][0].shape[1:]
    count = middles.shape[0]
    rows = count // (pieces * HALVES)
    last = before is not None
    pairs = [((0, 0), (1, 0)), ((0, 1), (1, 1))] + [((0, k), (0, k + 1)) for k in range(2, pieces, 2)]
    start = len(pairs) if last else 0
    if last:
        pairs = [((1, k), (1, k + 1)) for k in range(2, pieces, 2)]
    steps = len(pairs)
    numbers = [[half * pieces + piece for half, piece in side] for side in zip(*pairs)]
    tables = [jnp.array(side, jnp.int32) for side in numbers]
    block_of = lambda width, side: pl.BlockSpec((rows, width), lambda i, place, *tables: (tables[side][i], 0))
    ins = plain([params[5], params[6]]) + anywhere([params[9], params[7]])
    ins += [(came[half][piece], pl.BlockSpec(memory_space=pl.ANY)) for pair in pairs for half, piece in pair]
    ins += [(middles, block_of(D, side)) for side in range(2)]
    ins += [(hiddens, block_of(FF, side)) for side in range(2)]
    scratch = [
        pltpu.VMEM((2, 2, *part), HALF),
        pltpu.VMEM((2 * CHUNKS, CHUNK, CHUNK), FLOAT),
        pltpu.SemaphoreType.DMA((2, 2)),
    ]
    outs = [((count, D), HALF, row_spec(2 * rows, D, lambda i, *_: start + i))]
    aliases = {}
    if last:
        aliases = {0: before[0]}
        ins.append((before[1], pl.BlockSpec(memory_space=pl.ANY)))
        tiles = (4, batch, D // batch, CHUNK)
        outs += [(tiles, HALF, whole(tiles))] * 2
        scratch += [pltpu.VMEM((2 * CHUNKS, CHUNK, CHUNK), HALF), pltpu.SemaphoreType.DMA]
    else:
        tiles = (2 * CHUNKS, CHUNK, CHUNK)
        outs.append((tiles, HALF, whole(tiles)))
    outs.append(((SUMS, 1, D), FLOAT, whole((SUMS, 1, D))))
    scratch += buffers_of([params[9], params[7]])
    body = functools.partial(feed_back_body, arrays=2 * steps, steps=steps, last=last)
    return run(
        lambda place, one, two, *refs: body(place, *refs),
        "feed_back",
        (steps,),
        [place, *tables],
        ins,
        outs,
        scratch=scratch,
        aliases=aliases,
        after=after,
        flops=SMALL_FLOPS if last else 32 * rows * steps * D * FF,
        moved=0 if last else 2 * rows * steps * (10 * D + 2 * FF) + 8 * D * FF,
    )


def attention_back_body(place, rows_in, gain, offset, leave_in, entry_in, *refs, window, pieces):
    leave, entry, fetch_sems = refs[-3:]
    fetched = Fetched([leave_in, entry_in], [leave, entry], fetch_sems)
    refs = refs[:-3]
    came, refs = refs[: HALVES * pieces], refs[HALVES * pieces :]
    triples, weights, mixes, middles_back = [refs[HALVES * k : HALVES * (k + 1)] for k in range(4)]
    delta, outcome, away, own, sums, mixed_back, triple_back, held, sems = refs[4 * HALVES :]
    step = pl.program_id(0)
    each = rows_in.shape[1] // HALVES

    def results(piece):
        return [
            pltpu.make_async_copy(
                came[half * pieces + piece].at[RESULT],
                outcome.at[:, pl.ds(half * each, each)],
                sems.at[half],
            )
            for half in range(HALVES)
        ]

    @pl.when(step == 0)
    def _():
        fetched.start()
        sums[...] = jnp.zeros_like(sums)

    def add(tile, left, right):
        before = jnp.where(step == 0, 0.0, held[tile])
        held[tile] = before + dot_left(left, right)

    for piece in range(pieces):

        @pl.when(step == piece)
        def _(piece=piece):
            for copy in results(piece):
                copy.start()

    parts = [rows_in[:, half * each : (half + 1) * each].reshape(-1, D) for half in range(HALVES)]
    count = parts[0].shape[0]
    attend_back = side_by_side(middles_back)
    middle_back = attend_back.astype(FLOAT)
    fetched.need(0, 1)
    mixed_back[...] = dot_right(attend_back, leave[...]).astype(HALF)
    add(3, side_by_side(mixes), attend_back)
    unit, inverse = unit_of(jnp.concatenate(parts, axis=0).astype(FLOAT))
    normed = (unit * gain[...] + offset[...]).astype(HALF)
    for half in range(HALVES):
        span = pl.ds(half * count, count)
        back = triple_back.at[:, span]

        def put(rows, pair, part, value, back=back):
            back[part, rows, columns(pair)] = value

        attend_backward(triples[half], weights[half], mixed_back.at[span], put, count // window, window)
    normed_back = jnp.zeros_like(middle_back)
    for part in range(3):
        back = triple_back[part]
        normed_back = normed_back + dot_right(back, entry[:, part * D : (part + 1) * D])
        add(part, normed, back)
    sums[GAIN] += column_sum(normed_back * unit)
    sums[OFFSET] += column_sum(normed_back)
    rows_back = (middle_back + norm_back(normed_back * gain[...], unit, inverse)).astype(HALF)
    for half in range(HALVES):
        delta[:, half * each : (half + 1) * each] = rows_back[half * count : (half + 1) * count].reshape(
            -1, each, window, D
        )

    @pl.when(step == pl.num_programs(0) - 1)
    def _():
        pick(place[4], away, own, [held[tile].astype(HALF) for tile in range(4)])

    for piece in range(pieces):

        @pl.when(step == piece)
        def _(piece=piece):
            for copy in results(piece):
                copy.wait()


def attention_back(place, frames, params, came, triple, weights, mixed, middles_back, batch, after):
    pieces = len(came[0])
    per_group, windows, window, _ = frames.shape
    block = (per_group, windows // pieces, window, D)
    rows = per_group * block[1] * window // HALVES
    cut = pl.BlockSpec(block, lambda i, place: (0, place[0] ^ i, 0, 0))
    attended = (rows // window, PAIRS, window, 2 * window)
    halves = range(HALVES)
    spread_out = lambda half: lambda i, place: jnp.where(i < 2, 2 * i + half, i + (pieces if half else 2))
    ins = [(frames, cut)] + plain(params[:2]) + anywhere([params[3], params[2]])
    ins += [(array, pl.BlockSpec(memory_space=pl.ANY)) for half in came for array in half]
    ins += [(triple, row_spec(rows, 3 * D, lambda i, place, h=h: h * pieces + i)) for h in halves]
    ins += [
        (weights, pl.BlockSpec(attended, lambda i, place, h=h: (h * pieces + i, 0, 0, 0))) for h in halves
    ]
    ins += [(mixed, row_spec(rows, D, lambda i, place, h=h: h * pieces + i)) for h in halves]
    ins += [(middles_back, row_spec(rows, D, spread_out(h))) for h in halves]
    tiles = (2, batch, D // batch, CHUNK)
    count = rows * pieces * HALVES
    return run(
        functools.partial(attention_back_body, window=window, pieces=pieces),
        "attention_back",
        (pieces,),
        [place],
        ins,
        [
            (frames.shape, HALF, cut),
            (frames.shape, HALF, cut),
            *[(tiles, HALF, whole(tiles))] * 2,
            ((SUMS, 1, D), FLOAT, whole((SUMS, 1, D))),
        ],
        scratch=[
            pltpu.VMEM((rows * HALVES, D), HALF),
            pltpu.VMEM((3, rows * HALVES, D), HALF),
            pltpu.VMEM((4, CHUNK, CHUNK), FLOAT),
            pltpu.SemaphoreType.DMA((HALVES,)),
            *buffers_of([params[3], params[2]]),
        ],
        after=after,
        flops=16 * count * D * D,
        moved=count * D * 2 * (3 + 1 + 1 + 2 + 2 + 4),
    )


def swap(value, axis, mask):
    size = lax.axis_size(axis)
    if mask == 0:
        return value
    return lax.ppermute(value, axis, [(i, i ^ mask) for i in range(size)])


def move(value, batch_mask, win_mask):
    if batch_mask == 0:
        return swap(value, "win", win_mask)
    if win_mask == 0:
        return swap(value, "batch", batch_mask)
    batch, win = lax.axis_size("batch"), lax.axis_size("win")
    pairs = [
        (b * win + w, (b ^ batch_mask) * win + (w ^ win_mask)) for b in range(batch) for w in range(win)
    ]
    return lax.ppermute(value, ("batch", "win"), pairs)


def exchange(arrays):
    made = {k: swap(arrays[k], "win", k) for k in reversed(range(len(arrays)))}
    return [made[k] for k in range(len(arrays))]


def split_body(place, *refs, groups, alone, across):
    own, got, outs = refs[:groups], refs[groups : 2 * groups - alone], refs[2 * groups - alone :]
    got = [*got, *[None] * alone]
    column, row = place[1], place[2]
    width = CHUNK // across
    at = 0
    for one, two in zip(own, got):
        rows = one.shape[3]
        for tile in range(one.shape[0]):
            for piece, out in enumerate(outs):
                y = row ^ (piece % 2)
                x = pl.ds(pl.multiple_of((column ^ (piece // 2)) * width, width), width)
                total = one[tile, :, y, :, x]
                if two is not None:
                    total = (total.astype(FLOAT) + two[tile, :, y, :, x].astype(FLOAT)).astype(HALF)
                out[:, at : at + rows] = total
            at += rows


def total_of(refs, index):
    total = refs[0][index].astype(FLOAT)
    for ref in refs[1:]:
        total = total + ref[index].astype(FLOAT)
    return total.astype(HALF)


def merge_body(place, *refs, inputs):
    ins, outs = refs[:inputs], refs[inputs:]
    for piece, out in enumerate(outs):
        out[...] = total_of(ins, place[3] ^ piece)


def pair_body(place, *refs, inputs, bit):
    ins, outs = refs[:inputs], refs[inputs:]
    mine = (place[3] >> bit) & 1
    for side, out in zip((mine, 1 - mine), outs):
        out[...] = total_of(ins, (slice(None), side))


def last_body(*refs, sets):
    ins, out = refs[:-1], refs[-1]
    at, start = 0, 0
    for size in sets:
        rows, width = ins[at].shape[-2:]
        made = [ref.reshape(rows, width) for ref in ins[at : at + size]]
        out[start : start + rows] = total_of(made, slice(None))
        at += size
        start += rows


def unpack_body(place, *refs, pieces, across, layout):
    ins, outs, held = refs[:pieces], refs[pieces:-1], refs[-1]
    width = CHUNK // across
    for piece, ref in enumerate(ins):
        x = pl.ds(pl.multiple_of((place[1] ^ (piece // 2)) * width, width), width)
        held[place[4] ^ (piece % 2), :, x] = ref[...].astype(FLOAT)
    for out, places in zip(outs, layout):
        for core, start, rows, left, wide, row, column in places:
            here = (slice(start, start + rows), slice(left, left + wide))
            value = held[(0, *here)] + held[(1, *here)] if core is None else held[(core, *here)]
            out[row : row + rows, column : column + wide] = value


def arrived_body(*refs):
    refs[-1][...] = jnp.zeros_like(refs[-1])


def arrived(arrays):
    shape = (8, 128)
    outs = [(shape, FLOAT, whole(shape))]
    return run(
        arrived_body, "arrived", (1,), [], [], outs, after=arrays, flops=8 * 10**9, vmem=SMALL_VMEM
    )


class Reduction:
    def __init__(self, place, away, own, alone=()):
        self.place = place
        self.batch, self.win = lax.axis_size("batch"), lax.axis_size("win")
        self.across, self.depth = self.win // 2, self.batch // 2
        cut = lambda a: a.reshape(-1, self.depth, 2, *a.shape[2:])
        self.own = [cut(a) for a in (*own, *alone)]
        self.alone = len(alone)
        self.got = [swap(cut(a), "win", 1) for a in away]
        self.rows = sum(a.shape[0] * a.shape[3] for a in self.own)
        self.width = CHUNK // self.across
        self.vmem = VMEM

    def cores(self, after=()):
        shape = (self.depth, self.rows, self.width)
        pieces = run(
            functools.partial(split_body, groups=len(self.own), alone=self.alone, across=self.across),
            "sum_cores",
            (1,),
            [self.place],
            plain(self.own + self.got),
            [(shape, HALF, whole(shape))] * (2 * self.across),
            after=after,
            vmem=self.vmem,
            flops=SMALL_FLOPS,
        )
        self.mark = pieces[:1]
        self.pieces = [move(a, number % 2, 2 * (number // 2)) for number, a in enumerate(pieces)]

    def chips(self, after=(), flops=SMALL_FLOPS):
        shape = (self.rows, self.width)
        pieces = run(
            functools.partial(merge_body, inputs=len(self.pieces)),
            "sum_chips",
            (1,),
            [self.place],
            plain(self.pieces),
            [(shape, HALF, whole(shape))] * self.depth,
            after=after,
            vmem=self.vmem,
            flops=flops,
        )
        self.mark = pieces[:1]
        self.pieces = [swap(a, "batch", 2 * number) for number, a in enumerate(pieces)]

    def pair(self, bit, after=(), flops=SMALL_FLOPS):
        depth, rows, width = self.pieces[0].shape
        shape = (depth // 2, rows, width)
        kept, away = run(
            functools.partial(pair_body, inputs=len(self.pieces), bit=bit),
            "sum_pairs",
            (1,),
            [self.place],
            plain([a.reshape(depth // 2, 2, rows, width) for a in self.pieces]),
            [(shape, HALF, whole(shape))] * 2,
            after=after,
            vmem=self.vmem,
            flops=flops,
        )
        self.mark = [kept]
        self.pieces = [kept, swap(away, "batch", 2 << bit)]

    def last(self, after=(), other=None, flops=SMALL_FLOPS):
        groups = [self] if other is None else [other, self]
        self.rows = sum(group.rows for group in groups)
        shape = (self.rows, self.width)
        (total,) = run(
            functools.partial(last_body, sets=[len(group.pieces) for group in groups]),
            "sum_last",
            (1,),
            [],
            plain([a for group in groups for a in group.pieces]),
            [(shape, HALF, whole(shape))],
            after=after,
            vmem=self.vmem,
            flops=flops,
        )
        self.mark = [total]
        across = [swap(total, "win", 2 * number) for number in range(self.across)]
        self.pieces = [a if side == 0 else swap(a, "win", 1) for a in across for side in range(2)]

    def unpack(self, layout, shapes, after=()):
        return run(
            functools.partial(
                unpack_body, pieces=self.win, across=self.across, layout=layout
            ),
            "unpack",
            (1,),
            [self.place],
            plain(self.pieces),
            [(s, FLOAT, whole(s)) for s in shapes],
            scratch=[pltpu.VMEM((2, self.rows, CHUNK), FLOAT)],
            after=after,
            vmem=self.vmem,
            flops=SMALL_FLOPS,
        )


SMALL_ROWS = 16


def small_body(*refs, blocks):
    out = refs[-1]
    sums, at = [], 0
    for size in blocks:
        sums.append(total_in(refs[at : at + size]))
        at += size
    _, batch, _, width = out.shape
    rows = D // batch
    wide = lambda parts: jnp.concatenate(
        [*parts, jnp.zeros((1, width - sum(p.shape[1] for p in parts)), FLOAT)], axis=1
    )
    for shard in range(batch):
        made = []
        for total in sums:
            made.append(wide([total[n][:, shard * rows : (shard + 1) * rows] for n in range(6)]))
        for total in sums:
            chunk, start = divmod(shard * 4 * rows, CHUNK)
            made.append(wide([total[LIFT + chunk][:, start : start + 4 * rows]]))
        made.append(jnp.zeros((SMALL_ROWS - len(made), width), FLOAT))
        out[0, shard] = jnp.concatenate(made, axis=0).astype(HALF)


def total_in(refs):
    total = refs[0][...]
    for ref in refs[1:]:
        total = total + ref[...]
    return total


def small_tiles(blocks, batch):
    shape = (1, batch, SMALL_ROWS, CHUNK)
    (out,) = run(
        functools.partial(small_body, blocks=[len(sums) for sums in blocks]),
        "small_tiles",
        (1,),
        [],
        plain([a for sums in blocks for a in sums]),
        [(shape, HALF, whole(shape))],
        vmem=SMALL_VMEM,
    )
    return out


def attend_places(rows, start):
    spot = lambda tile: (tile // 2, start + tile % 2 * rows, rows, 0, CHUNK)
    return [
        [(*spot(part), 0, part * CHUNK) for part in range(3)],
        [(*spot(3), 0, 0)],
    ], [(rows, 3 * D), (rows, D)]


def feed_places(rows, start):
    narrows = [(sub // 2, start + sub % 2 * rows, rows, 0, CHUNK, sub * rows, 0) for sub in range(4)]
    start += 2 * rows
    widens = [
        (chunk // 2, start + chunk % 2 * rows, rows, 0, CHUNK, 0, chunk * CHUNK) for chunk in range(CHUNKS)
    ]
    return [widens, narrows], [(rows, FF), (4 * rows, D)]


def small_places(rows, start):
    layout, shapes = [], []
    for block in range(2):
        layout += [[(None, start + block, 1, number * rows, rows, 0, 0)] for number in range(6)]
        layout.append([(None, start + 2 + block, 1, 0, 4 * rows, 0, 0)])
        shapes += [(1, rows)] * 6 + [(1, 4 * rows)]
    return layout, shapes


def local(*args):
    frames, cotangent, video_frames = args[0], args[23], args[24]
    space = [a.reshape(1, -1) if a.ndim == 1 else a for a in args[1:12]]
    time = [a.reshape(1, -1) if a.ndim == 1 else a for a in args[12:23]]
    batch, win = lax.axis_size("batch"), lax.axis_size("win")
    here, group = lax.axis_index("win"), lax.axis_index("batch")
    core = here % 2
    place = jnp.stack([here, here // 2, group % 2, group // 2, core]).astype(jnp.int32)
    _, per_group, _, windows, window, _ = frames.shape
    shape = (per_group, windows, window, D)
    rows_in, cotangent = frames.reshape(shape), cotangent.reshape(shape)
    rows = D // batch

    kept, came = [], []
    for half in range(HALVES):
        sent, kept = space_forward(place, rows_in, cotangent, space, half, win, kept)
        came.append(exchange(sent))
    triple, weights, mixed, middles, hiddens = kept
    backs, time_sums, tiles = [], [], [None]
    for half in range(HALVES):
        sent, tiles, sums = time_block(place, video_frames, came[half], time, batch, *tiles)
        backs.append(exchange(sent))
        time_sums.append(sums)

    bits = (batch // 2).bit_length() - 1
    time_sum = Reduction(place, tiles[:1], tiles[1:])
    time_sum.cores(arrived(backs[0][1:]))
    *fed, first_sums = feed_back(place, space, backs, middles, hiddens, batch, after=time_sum.mark)
    middles_back, away, own, feed_sums = feed_back(place, space, backs, middles, hiddens, batch, fed)
    feed_sum = Reduction(place, [away], [own])
    time_sum.pair(0, [feed_sums], LONG_FLOPS)
    feed_sum.cores(time_sum.mark)
    delta, outcome, away, own, attend_sums = attention_back(
        place, rows_in, space, backs, triple, weights, mixed, middles_back, batch, feed_sum.mark
    )
    time_sum.vmem = feed_sum.vmem = SMALL_VMEM
    small = small_tiles([[first_sums, feed_sums, attend_sums], time_sums], batch)
    attend_sum = Reduction(place, [away], [own], [small])
    attend_sum.vmem = SMALL_VMEM
    mark = [attend_sums]
    for bit in range(1, bits):
        time_sum.pair(bit, mark, 0)
        mark = time_sum.mark
    feed_sum.pair(0, mark, LONG_FLOPS)
    attend_sum.cores(feed_sum.mark)
    mark = attend_sum.mark
    for bit in range(1, bits):
        feed_sum.pair(bit, mark)
        mark = feed_sum.mark
    time_rows = time_sum.rows
    attend_sum.chips(mark)
    feed_sum.last(attend_sum.mark, time_sum, 0)
    attend_sum.last(feed_sum.mark)
    feed_layout, feed_shapes = feed_places(rows, 0)
    attend_layout, attend_shapes = attend_places(rows, 4 * rows)
    last_layout, last_shapes = feed_places(rows, time_rows)
    made = feed_sum.unpack(
        feed_layout + attend_layout + last_layout,
        feed_shapes + attend_shapes + last_shapes,
        attend_sum.mark,
    )
    time_grads, feed_grads = made[:4], made[4:]
    attend_layout, attend_shapes = attend_places(rows, 0)
    small_layout, small_shapes = small_places(rows, 2 * rows)
    attend_grads = attend_sum.unpack(attend_layout + small_layout, attend_shapes + small_shapes)
    smalls = [a.reshape(-1) for a in attend_grads[2:]]

    def collected(grads, smalls):
        widen, narrow, entry, leave = grads
        gain, offset, bias, weigh, shift, nudge, lift = smalls
        return gain, offset, entry, leave, bias, weigh, shift, widen, lift, narrow, nudge

    return (
        outcome.reshape(frames.shape),
        delta.reshape(frames.shape),
        *collected([*feed_grads, *attend_grads[:2]], smalls[:7]),
        *collected(time_grads, smalls[7:]),
    )


def solution(mesh):
    rows = P("batch", None, "win", None, None, None)
    one, two = P("batch"), P("batch", None)
    grads = (one, one, two, two, one, one, one, two, one, two, one)
    return jax.shard_map(
        local,
        mesh=mesh,
        in_specs=(rows, *([P()] * 22), rows, P("batch", None)),
        out_specs=(rows, rows, *grads, *grads),
        check_vma=False,
    )
```

```python
import functools

import jax
import jax.numpy as jnp
from jax import lax
from jax.experimental import pallas as pl
from jax.experimental.pallas import tpu as pltpu
from jax.sharding import PartitionSpec as P

D = 512
HEADS = 8
HDIM = 64
FF = 2048
PAIR = 2 * HDIM
PAIRS = HEADS // 2
CHUNK = 512
CHUNKS = FF // CHUNK
EPS = 1e-05
NEGATIVE = -1e30
FLOAT = jnp.float32
HALF = jnp.bfloat16
HALVES = 2
UNITS = 16
VMEM = 127 << 19
SMALL_VMEM = 24 << 20
LONG_FLOPS = 10**11
SMALL_FLOPS = 2 * 10**8
SLOWER = 4

NARROW, WIDEN, ENTRY, EXIT = 0, CHUNKS, 2 * CHUNKS, 2 * CHUNKS + 3
TILES = 2 * CHUNKS + 4
SHARED = [WIDEN, WIDEN + 1, ENTRY, ENTRY + 1, WIDEN + 2, WIDEN + 3, ENTRY + 2, EXIT]
INNER, COTANGENT = 0, 1
BACK, RESULT = 0, 1
GAIN, OFFSET, BIAS, WEIGH, SHIFT, NUDGE, LIFT = 0, 1, 2, 3, 4, 5, 6
SUMS = 6 + CHUNKS


def dot(left, right):
    return lax.dot_general(left, right, (((1,), (0,)), ((), ())), preferred_element_type=FLOAT)


def dot_right(left, right):
    return lax.dot_general(left, right, (((1,), (1,)), ((), ())), preferred_element_type=FLOAT)


def dot_left(left, right):
    return lax.dot_general(left, right, (((0,), (0,)), ((), ())), preferred_element_type=FLOAT)


def unit_of(rows):
    centre = rows - jnp.mean(rows, axis=-1, keepdims=True)
    inverse = lax.rsqrt(jnp.mean(centre * centre, axis=-1, keepdims=True) + EPS)
    return centre * inverse, inverse


def norm_back(scaled, unit, inverse):
    return inverse * (
        scaled
        - jnp.mean(scaled, axis=-1, keepdims=True)
        - unit * jnp.mean(scaled * unit, axis=-1, keepdims=True)
    )


def gelu_pair(hidden):
    half = 0.5 * lax.erf(hidden * 0.7071067811865476) + 0.5
    bell = jnp.exp(hidden * hidden * -0.5) * 0.3989422804014327
    return hidden * half, half + hidden * bell


def gelu_of(hidden):
    return hidden * (0.5 * lax.erf(hidden * 0.7071067811865476) + 0.5)


def column_sum(values):
    return jnp.sum(values, axis=0, keepdims=True)


def first_head(rows):
    return lax.broadcasted_iota(jnp.int32, (rows, PAIR), 1) < HDIM


def spread(pair, first):
    zero = jnp.zeros_like(pair)
    return jnp.concatenate([jnp.where(first, pair, zero), jnp.where(first, zero, pair)], axis=0)


def gathered(both, first, rows):
    return jnp.where(first, both[:rows], both[rows:])


def attend_units(blocks):
    units = [(block, pair) for block in range(blocks) for pair in range(PAIRS)]
    return [units[start : start + UNITS] for start in range(0, len(units), UNITS)]


def columns(pair, part=0):
    start = part * D + pair * PAIR
    return slice(start, start + PAIR)


def attend_forward(triple, mixed, weights, blocks, rows, mask):
    first = first_head(rows)
    for units in attend_units(blocks):
        spans = [slice(block * rows, block * rows + rows) for block, _ in units]
        queries = [spread(triple[s, columns(p)], first) for s, (_, p) in zip(spans, units)]
        scores = [dot_right(triple[s, columns(p, 1)], q) for q, s, (_, p) in zip(queries, spans, units)]
        if mask is not None:
            scores = [score + mask for score in scores]
        powers = [
            jnp.exp((score - jnp.max(score, axis=0, keepdims=True)) * HDIM ** (-0.5)) for score in scores
        ]
        probs = [
            (power * (1.0 / jnp.sum(power, axis=0, keepdims=True))).astype(HALF) for power in powers
        ]
        both = [dot_left(prob, triple[s, columns(p, 2)]) for prob, s, (_, p) in zip(probs, spans, units)]
        for value, prob, s, (block, p) in zip(both, probs, spans, units):
            weights[block, p] = prob
            mixed[s, columns(p)] = gathered(value, first, rows).astype(HALF)


def attend_backward(triple, weights, mixed_back, put, blocks, rows):
    first = first_head(rows)
    scale = HDIM ** (-0.5)
    for units in attend_units(blocks):
        spans = [slice(block * rows, block * rows + rows) for block, _ in units]
        mixes = [spread(mixed_back[s, columns(p)], first) for s, (_, p) in zip(spans, units)]
        probs = [weights[block, p] for block, p in units]
        values_back = [dot(prob, mix) for prob, mix in zip(probs, mixes)]
        weights_back = [
            dot_right(triple[s, columns(p, 2)], mix) for mix, s, (_, p) in zip(mixes, spans, units)
        ]
        scores_back = []
        for prob, back in zip(probs, weights_back):
            wide = prob.astype(FLOAT)
            inside = back - jnp.sum(back * wide, axis=0, keepdims=True)
            scores_back.append((wide * inside * scale).astype(HALF))
        queries = [spread(triple[s, columns(p)], first) for s, (_, p) in zip(spans, units)]
        keys_back = [dot(score, query) for score, query in zip(scores_back, queries)]
        both = [
            dot_left(score, triple[s, columns(p, 1)])
            for score, s, (_, p) in zip(scores_back, spans, units)
        ]
        for key, value, pair, s, (_, p) in zip(keys_back, values_back, both, spans, units):
            put(s, p, 0, gathered(pair, first, rows).astype(HALF))
            put(s, p, 1, key.astype(HALF))
            put(s, p, 2, value.astype(HALF))


def whole(shape):
    return pl.BlockSpec(shape, lambda *_: (0,) * len(shape), pipeline_mode=pl.Buffered(1))


def run(body, name, grid, scalars, ins, outs, scratch=(), aliases=None, after=(), flops=0, moved=0, vmem=VMEM):
    aliases = aliases or {}
    unread = pl.BlockSpec(memory_space=pl.ANY)
    first = len(scalars) + len(ins)
    extra = [*aliases.values(), *after]

    def inner(*refs):
        body(*refs[:first], *refs[first + len(extra) :])

    return pl.pallas_call(
        inner,
        out_shape=[jax.ShapeDtypeStruct(shape, kind) for shape, kind, _ in outs],
        grid_spec=pltpu.PrefetchScalarGridSpec(
            num_scalar_prefetch=len(scalars),
            grid=grid,
            in_specs=[spec for _, spec in ins] + [unread] * len(extra),
            out_specs=[spec for _, _, spec in outs],
            scratch_shapes=list(scratch),
        ),
        input_output_aliases={first + at: out for at, out in enumerate(aliases)},
        compiler_params=pltpu.CompilerParams(vmem_limit_bytes=vmem),
        cost_estimate=pl.CostEstimate(flops=flops * SLOWER, bytes_accessed=moved * SLOWER, transcendentals=0),
        name=name,
    )(*scalars, *[array for array, _ in ins], *extra)


class Fetched:
    def __init__(self, sources, buffers, sems):
        self.copies = [
            pltpu.make_async_copy(source, buffer, sems.at[number])
            for number, (source, buffer) in enumerate(zip(sources, buffers))
        ]

    def start(self):
        for copy in self.copies:
            copy.start()

    def need(self, *numbers):
        @pl.when(pl.program_id(0) == 0)
        def _():
            for number in numbers:
                self.copies[number].wait()


def anywhere(arrays):
    return [(array, pl.BlockSpec(memory_space=pl.ANY)) for array in arrays]


def buffers_of(arrays):
    return [pltpu.VMEM(a.shape, a.dtype) for a in arrays] + [pltpu.SemaphoreType.DMA((len(arrays),))]


def plain(arrays):
    return [(array, whole(array.shape)) for array in arrays]


def slab_spec(slabs, rows, at):
    return pl.BlockSpec((slabs, rows, D), lambda *i: (0, at(*i), 0))


def row_spec(rows, width, at):
    return pl.BlockSpec((rows, width), lambda *i: (at(*i), 0))


def vectors_of(params):
    return [param for param in params if param.shape[0] == 1]


def weights_of(params):
    return [param for param in params if param.shape[0] > 1]


def space_forward_body(place, *refs, window, pieces):
    ins, cotangents, refs = refs[:pieces], refs[pieces : 2 * pieces], refs[2 * pieces :]
    gain, offset, bias, weigh, shift, lift, nudge = refs[:7]
    sent = refs[11 : 11 + pieces]
    triple, weights, mixed, middles, hiddens, *buffers, sems = refs[11 + pieces :]
    entry, leave, widen, narrow = buffers
    fetched = Fetched(refs[7:11], buffers, sems)
    step = pl.program_id(0)

    @pl.when(step == 0)
    def _():
        fetched.start()

    shape = ins[0].shape
    rows = jnp.concatenate([ref[...].reshape(-1, D) for ref in ins], axis=0).astype(FLOAT)
    count = rows.shape[0]
    unit, _ = unit_of(rows)
    normed = (unit * gain[...] + offset[...]).astype(HALF)
    fetched.need(0)
    triple[...] = dot(normed, entry[...]).astype(HALF)
    attend_forward(triple, mixed, weights, count // window, window, None)
    fetched.need(1, 2, 3)
    middle = rows + dot(mixed[...], leave[...]) + bias[...]
    middles[...] = middle.astype(HALF)
    unit_two, _ = unit_of(middle)
    second = (unit_two * weigh[...] + shift[...]).astype(HALF)
    total = middle + nudge[...]
    for chunk in range(CHUNKS):
        at = slice(chunk * CHUNK, (chunk + 1) * CHUNK)
        hidden = dot(second, widen[:, at]) + lift[:, at]
        hiddens[:, at] = hidden.astype(HALF)
        total = total + dot(gelu_of(hidden).astype(HALF), narrow[at, :])
    inner = total.astype(HALF).reshape(pieces, *shape)
    for piece in range(pieces):
        sent[piece][INNER] = inner[piece]
        sent[piece][COTANGENT] = cotangents[piece][...]


def space_forward(place, frames, cotangent, params, half, pieces, before):
    per_group, windows, window, _ = frames.shape
    each = windows // pieces // HALVES
    block = (per_group, each, window, D)
    rows = per_group * each * window
    count = rows * pieces * HALVES
    cuts = [
        pl.BlockSpec(block, lambda i, place, side=side: (0, (place[0] ^ side) * HALVES + half, 0, 0))
        for side in range(pieces)
    ]
    rows *= pieces
    at = lambda i, place: half
    attended = (rows // window, PAIRS, window, 2 * window)
    both = (2, *block)
    outs = [(both, HALF, pl.BlockSpec(both, lambda i, place: (0,) * 5))] * pieces
    outs += [
        ((count, 3 * D), HALF, row_spec(rows, 3 * D, at)),
        (
            (count // window, *attended[1:]),
            HALF,
            pl.BlockSpec(attended, lambda i, place: (at(i, place), 0, 0, 0)),
        ),
        ((count, D), HALF, row_spec(rows, D, at)),
        ((count, D), HALF, row_spec(rows, D, at)),
        ((count, FF), HALF, row_spec(rows, FF, at)),
    ]
    made = run(
        functools.partial(space_forward_body, window=window, pieces=pieces),
        "space_forward",
        (1,),
        [place],
        [(a, cut) for a in (frames, cotangent) for cut in cuts] + plain(vectors_of(params)) + anywhere(weights_of(params)),
        outs,
        scratch=buffers_of(weights_of(params)),
        aliases={pieces + number: array for number, array in enumerate(before)},
        flops=2 * rows * D * (4 * D + 2 * FF),
        moved=rows * (8 * D + 12 * D + 2 * FF),
    )
    return made[:pieces], made[pieces:]


def by_position(refs, which, frames_of, positions):
    parts = [ref[which, frame].astype(FLOAT) for ref in refs for frame in range(frames_of)]
    return jnp.concatenate(
        [part[start : start + 8] for start in range(0, positions, 8) for part in parts], axis=0
    )


def by_frame(values, refs, which, frames_of, positions):
    total = len(refs) * frames_of
    for at, ref in enumerate(refs):
        for frame in range(frames_of):
            number = at * frames_of + frame
            ref[which, frame] = jnp.concatenate(
                [
                    values[(group * total + number) * 8 : (group * total + number) * 8 + 8]
                    for group in range(positions // 8)
                ],
                axis=0,
            ).astype(HALF)


def fill_mask(mask, place, lengths, per_group, pieces):
    window = mask.shape[0]
    key = lax.broadcasted_iota(jnp.int32, mask.shape, 0)
    query = lax.broadcasted_iota(jnp.int32, mask.shape, 1) % window
    frames = []
    for row in (query, key):
        number = row // 8
        frames.append((number % per_group) * pieces + ((number // per_group) ^ place[0]))
    videos = [jnp.zeros_like(frame) for frame in frames]
    entries = lengths.shape[1]
    end = 0
    for entry in range(entries):
        end = end + lengths[0, entry]
        videos = [v + (f >= end).astype(jnp.int32) for v, f in zip(videos, frames)]
    videos = [jnp.where(f < end, v, entries + f) for v, f in zip(videos, frames)]
    allowed = (videos[0] == videos[1]) & (frames[1] <= frames[0]) & (query % 8 == key % 8)
    mask[...] = jnp.where(allowed, 0.0, NEGATIVE)


def shared_copies(tile, core, stage, away, own, sems):
    _, batch, rows, _ = own.shape
    made = []
    if tile < WIDEN:
        shards = batch // CHUNKS
        source = stage.at[tile].reshape(shards, 4, rows, CHUNK)
        at = pl.ds(tile * shards, shards)
        for sub in range(4):
            target = own if sub // 2 == core else away
            made.append((source.at[:, sub], target.at[sub % 2, at]))
    else:
        place = SHARED.index(tile)
        target = own if place // 4 == core else away
        made.append((stage.at[tile].reshape(batch, rows, CHUNK), target.at[2 + place % 4]))
    return [
        pltpu.make_async_copy(source, target, sems.at[tile, number])
        for number, (source, target) in enumerate(made)
    ]


def time_body(place, lengths, *refs, pieces, last, steps):
    came = refs[:pieces]
    gain, offset, bias, weigh, shift, lift, nudge = refs[pieces : pieces + 7]
    entry, leave, widen, narrow, fetch_sems = refs[-5:]
    fetched = Fetched(refs[pieces + 7 : pieces + 11], [entry, leave, widen, narrow], fetch_sems)
    refs = refs[pieces + 11 : -5]
    if last:
        partial, refs = refs[0], refs[1:]
    sent, refs = refs[:pieces], refs[pieces:]
    grads, refs = refs[: 1 + last], refs[1 + last :]
    sums, triple, weights, mixed, mixed_back, triple_back, mask, stage, sems, came_sem, *held = refs
    held = held[0] if held else None
    _, frames_of, positions, _ = came[0].shape
    window = 8 * pieces * frames_of
    rows = by_position(came, INNER, frames_of, positions)
    blocks = rows.shape[0] // window
    step = pl.program_id(0)

    @pl.when(step == 0)
    def _():
        fetched.start()
        sums[...] = jnp.zeros_like(sums)
        fill_mask(mask, place, lengths, frames_of, pieces)
        if last:
            pltpu.make_async_copy(partial, stage, came_sem).start()

    def each_copy(tile, act):
        if not last:
            act(pltpu.make_async_copy(stage.at[tile], grads[0].at[tile], sems.at[tile, 0]))
            return
        for core in range(2):

            @pl.when(place[4] == core)
            def _(core=core):
                for copy in shared_copies(tile, core, stage, *grads, sems):
                    act(copy)

    def done(tiles):
        @pl.when(step == pl.num_programs(0) - 1)
        def _():
            if last and steps > 1 and tiles[0] == 0:
                pltpu.make_async_copy(partial, stage, came_sem).wait()
            for tile in tiles:
                if steps > 1:
                    finish(tile, held[tile])
                each_copy(tile, lambda copy: copy.start())

    def finish(tile, value):
        if last:
            value = value + stage[tile].astype(FLOAT)
        stage[tile] = value.astype(HALF)

    def add(tile, left, right):
        if steps == 1:
            finish(tile, dot_left(left, right))
            return
        before = jnp.where(step == 0, 0.0, held[tile])
        held[tile] = before + dot_left(left, right)

    unit, inverse = unit_of(rows)
    normed = (unit * gain[...] + offset[...]).astype(HALF)
    fetched.need(0)
    triple[...] = dot(normed, entry[...]).astype(HALF)
    attend_forward(triple, mixed, weights, blocks, window, mask[...])
    fetched.need(1, 2, 3)
    middle = rows + dot(mixed[...], leave[...]) + bias[...]
    unit_two, inverse_two = unit_of(middle)
    second = (unit_two * weigh[...] + shift[...]).astype(HALF)
    upstream = by_position(came, COTANGENT, frames_of, positions)
    branch_back = upstream.astype(HALF)
    sums[NUDGE] += column_sum(upstream)
    total = middle + nudge[...]
    second_back = jnp.zeros_like(middle)
    if last and steps == 1:
        pltpu.make_async_copy(partial, stage, came_sem).wait()
    for chunk in range(CHUNKS):
        at = slice(chunk * CHUNK, (chunk + 1) * CHUNK)
        active, slope = gelu_pair(dot(second, widen[:, at]) + lift[:, at])
        active = active.astype(HALF)
        hidden_back = dot_right(branch_back, narrow[at, :]) * slope
        hidden_low = hidden_back.astype(HALF)
        sums[LIFT + chunk] += column_sum(hidden_back)
        total = total + dot(active, narrow[at, :])
        second_back = second_back + dot_right(hidden_low, widen[:, at])
        add(NARROW + chunk, active, branch_back)
        add(WIDEN + chunk, second, hidden_low)
    done(range(ENTRY))
    by_frame(total, sent, RESULT, frames_of, positions)
    sums[WEIGH] += column_sum(second_back * unit_two)
    sums[SHIFT] += column_sum(second_back)
    middle_back = upstream + norm_back(second_back * weigh[...], unit_two, inverse_two)
    attend_back = middle_back.astype(HALF)
    sums[BIAS] += column_sum(middle_back)
    mixed_back[...] = dot_right(attend_back, leave[...]).astype(HALF)
    add(EXIT, mixed[...], attend_back)

    def put(span, pair, part, value):
        triple_back[part, span, columns(pair)] = value

    attend_backward(triple, weights, mixed_back, put, blocks, window)
    normed_back = jnp.zeros_like(middle)
    for part in range(3):
        back = triple_back[part]
        normed_back = normed_back + dot_right(back, entry[:, part * D : (part + 1) * D])
        add(ENTRY + part, normed, back)
    sums[GAIN] += column_sum(normed_back * unit)
    sums[OFFSET] += column_sum(normed_back)
    rows_back = middle_back + norm_back(normed_back * gain[...], unit, inverse)
    by_frame(rows_back, sent, BACK, frames_of, positions)

    done(range(ENTRY, TILES))

    @pl.when(step == pl.num_programs(0) - 1)
    def _():
        for tile in range(TILES):
            each_copy(tile, lambda copy: copy.wait())


def time_block(place, lengths, came, params, batch, partial=None, step_rows=1024):
    pieces = len(came)
    _, per_group, each, window, _ = came[0].shape
    positions = each * window
    flat = (2, per_group, positions, D)
    frames = per_group * pieces
    together = min(max(step_rows // frames, 16), positions)
    rows = together * frames
    steps = positions // together
    count = positions * frames
    attended = 8 * frames
    last = partial is not None
    spec = pl.BlockSpec((2, per_group, together, D), lambda i, *_: (0, 0, i, 0))
    grads = (TILES // 2, batch, D // batch, CHUNK) if last else (TILES, CHUNK, CHUNK)
    outs = [(flat, HALF, spec)] * pieces
    outs += [(grads, HALF, pl.BlockSpec(memory_space=pl.ANY))] * (1 + last)
    outs += [((SUMS, 1, D), FLOAT, whole((SUMS, 1, D)))]
    ins = [(array.reshape(flat), spec) for array in came] + plain(vectors_of(params))
    ins += anywhere(weights_of(params))
    if last:
        ins += anywhere([partial])
    made = run(
        functools.partial(time_body, pieces=pieces, last=last, steps=steps),
        "time_block",
        (steps,),
        [place, lengths],
        ins,
        outs,
        scratch=[
            pltpu.VMEM((rows, 3 * D), HALF),
            pltpu.VMEM((rows // attended, PAIRS, attended, 2 * attended), HALF),
            pltpu.VMEM((rows, D), HALF),
            pltpu.VMEM((rows, D), HALF),
            pltpu.VMEM((3, rows, D), HALF),
            pltpu.VMEM((attended, 2 * attended), FLOAT),
            pltpu.VMEM((TILES, CHUNK, CHUNK), HALF),
            pltpu.SemaphoreType.DMA((TILES, 8)),
            pltpu.SemaphoreType.DMA,
            *[pltpu.VMEM((TILES, CHUNK, CHUNK), FLOAT)] * (steps > 1),
            *buffers_of(weights_of(params)),
        ],
        flops=6 * count * D * (4 * D + 2 * FF),
        moved=count * 2 * D * 4 + 2 * D * (4 * D + 2 * FF),
    )
    shape = (2, per_group, each, window, D)
    sent = [array.reshape(shape) for array in made[:pieces]]
    return sent, made[pieces:-1], made[-1]


def side_by_side(refs, index=slice(None)):
    return jnp.concatenate([ref[index] for ref in refs], axis=0)


def pick(core, away, own, tiles):
    size = len(tiles) // 2
    for number in range(size):
        one, two = tiles[number], tiles[size + number]
        own[number] = jnp.where(core == 0, one, two).reshape(own.shape[1:])
        away[number] = jnp.where(core == 0, two, one).reshape(away.shape[1:])


def feed_back_body(place, weigh, shift, narrow_in, widen_in, *refs, arrays, steps, last):
    narrow, widen, fetch_sems = refs[-3:]
    fetched = Fetched([narrow_in, widen_in], [narrow, widen], fetch_sems)
    came, refs = refs[:arrays], refs[arrays:-3]
    middles, hiddens, refs = refs[:2], refs[2:4], refs[4:]
    if last:
        partial, refs = refs[0], refs[1:]
    middles_back, refs = refs[0], refs[1:]
    if last:
        away, own, sums, arrived, held, sems, stage, stage_sem = refs
    else:
        tiles, sums, arrived, held, sems = refs
    step = pl.program_id(0)

    def coming(number):
        return [
            pltpu.make_async_copy(
                came[number * 2 + side].at[BACK], arrived.at[number % 2, side], sems.at[number % 2, side]
            )
            for side in range(2)
        ]

    @pl.when(step == 0)
    def _():
        for copy in coming(0):
            copy.start()
        fetched.start()
        if last:
            pltpu.make_async_copy(partial, stage, stage_sem).start()
        sums[...] = jnp.zeros_like(sums)
        held[...] = jnp.zeros_like(held)

    for number in range(steps):

        @pl.when(step == number)
        def _(number=number):
            for copy in coming(number):
                copy.wait()
            if number + 1 < steps:
                for copy in coming(number + 1):
                    copy.start()

    branch_back = arrived[step % 2].reshape(-1, D)
    upstream = branch_back.astype(FLOAT)
    unit_two, inverse_two = unit_of(side_by_side(middles).astype(FLOAT))
    second = (unit_two * weigh[...] + shift[...]).astype(HALF)
    sums[NUDGE] += column_sum(upstream)
    second_back = jnp.zeros_like(upstream)
    fetched.need(0, 1)
    for chunk in range(CHUNKS):
        at = slice(chunk * CHUNK, (chunk + 1) * CHUNK)
        active, slope = gelu_pair(side_by_side(hiddens, (slice(None), at)).astype(FLOAT))
        hidden_back = dot_right(branch_back, narrow[at, :]) * slope
        hidden_low = hidden_back.astype(HALF)
        sums[LIFT + chunk] += column_sum(hidden_back)
        second_back = second_back + dot_right(hidden_low, widen[:, at])
        held[NARROW + chunk] += dot_left(active.astype(HALF), branch_back)
        held[WIDEN + chunk] += dot_left(second, hidden_low)
    sums[WEIGH] += column_sum(second_back * unit_two)
    sums[SHIFT] += column_sum(second_back)
    middle_back = upstream + norm_back(second_back * weigh[...], unit_two, inverse_two)
    middles_back[...] = middle_back.astype(HALF)
    sums[BIAS] += column_sum(middle_back)

    @pl.when(step == steps - 1)
    def _():
        if not last:
            tiles[...] = held[...].astype(HALF)
            return
        pltpu.make_async_copy(partial, stage, stage_sem).wait()
        value = lambda tile: (held[tile] + stage[tile].astype(FLOAT)).astype(HALF)
        tail = pl.ds(2, 2)
        pick(place[4], away.at[tail], own.at[tail], [value(WIDEN + chunk) for chunk in range(CHUNKS)])
        _, batch, rows, _ = own.shape
        shards = batch // CHUNKS
        for chunk in range(CHUNKS):
            parts = value(NARROW + chunk).reshape(shards, 4, rows, CHUNK)
            at = pl.ds(chunk * shards, shards)
            pick(place[4], away.at[:, at], own.at[:, at], [parts[:, sub] for sub in range(4)])


def feed_back(place, params, came, middles, hiddens, batch, before=None, after=()):
    pieces = len(came[0])
    part = came[0][0].shape[1:]
    count = middles.shape[0]
    rows = count // (pieces * HALVES)
    last = before is not None
    pairs = [((0, 0), (1, 0)), ((0, 1), (1, 1))] + [((0, k), (0, k + 1)) for k in range(2, pieces, 2)]
    start = len(pairs) if last else 0
    if last:
        pairs = [((1, k), (1, k + 1)) for k in range(2, pieces, 2)]
    steps = len(pairs)
    numbers = [[half * pieces + piece for half, piece in side] for side in zip(*pairs)]
    tables = [jnp.array(side, jnp.int32) for side in numbers]
    block_of = lambda width, side: pl.BlockSpec((rows, width), lambda i, place, *tables: (tables[side][i], 0))
    ins = plain([params[5], params[6]]) + anywhere([params[9], params[7]])
    ins += [(came[half][piece], pl.BlockSpec(memory_space=pl.ANY)) for pair in pairs for half, piece in pair]
    ins += [(middles, block_of(D, side)) for side in range(2)]
    ins += [(hiddens, block_of(FF, side)) for side in range(2)]
    scratch = [
        pltpu.VMEM((2, 2, *part), HALF),
        pltpu.VMEM((2 * CHUNKS, CHUNK, CHUNK), FLOAT),
        pltpu.SemaphoreType.DMA((2, 2)),
    ]
    outs = [((count, D), HALF, row_spec(2 * rows, D, lambda i, *_: start + i))]
    aliases = {}
    if last:
        aliases = {0: before[0]}
        ins.append((before[1], pl.BlockSpec(memory_space=pl.ANY)))
        tiles = (4, batch, D // batch, CHUNK)
        outs += [(tiles, HALF, whole(tiles))] * 2
        scratch += [pltpu.VMEM((2 * CHUNKS, CHUNK, CHUNK), HALF), pltpu.SemaphoreType.DMA]
    else:
        tiles = (2 * CHUNKS, CHUNK, CHUNK)
        outs.append((tiles, HALF, whole(tiles)))
    outs.append(((SUMS, 1, D), FLOAT, whole((SUMS, 1, D))))
    scratch += buffers_of([params[9], params[7]])
    body = functools.partial(feed_back_body, arrays=2 * steps, steps=steps, last=last)
    return run(
        lambda place, one, two, *refs: body(place, *refs),
        "feed_back",
        (steps,),
        [place, *tables],
        ins,
        outs,
        scratch=scratch,
        aliases=aliases,
        after=after,
        flops=SMALL_FLOPS if last else 32 * rows * steps * D * FF,
        moved=0 if last else 2 * rows * steps * (10 * D + 2 * FF) + 8 * D * FF,
    )


def attention_back_body(place, rows_in, gain, offset, leave_in, entry_in, *refs, window, pieces):
    leave, entry, fetch_sems = refs[-3:]
    fetched = Fetched([leave_in, entry_in], [leave, entry], fetch_sems)
    refs = refs[:-3]
    came, refs = refs[: HALVES * pieces], refs[HALVES * pieces :]
    triples, weights, mixes, middles_back = [refs[HALVES * k : HALVES * (k + 1)] for k in range(4)]
    delta, outcome, away, own, sums, mixed_back, triple_back, held, sems = refs[4 * HALVES :]
    step = pl.program_id(0)
    each = rows_in.shape[1] // HALVES

    def results(piece):
        return [
            pltpu.make_async_copy(
                came[half * pieces + piece].at[RESULT],
                outcome.at[:, pl.ds(half * each, each)],
                sems.at[half],
            )
            for half in range(HALVES)
        ]

    @pl.when(step == 0)
    def _():
        fetched.start()
        sums[...] = jnp.zeros_like(sums)

    def add(tile, left, right):
        before = jnp.where(step == 0, 0.0, held[tile])
        held[tile] = before + dot_left(left, right)

    for piece in range(pieces):

        @pl.when(step == piece)
        def _(piece=piece):
            for copy in results(piece):
                copy.start()

    parts = [rows_in[:, half * each : (half + 1) * each].reshape(-1, D) for half in range(HALVES)]
    count = parts[0].shape[0]
    attend_back = side_by_side(middles_back)
    middle_back = attend_back.astype(FLOAT)
    fetched.need(0, 1)
    mixed_back[...] = dot_right(attend_back, leave[...]).astype(HALF)
    add(3, side_by_side(mixes), attend_back)
    unit, inverse = unit_of(jnp.concatenate(parts, axis=0).astype(FLOAT))
    normed = (unit * gain[...] + offset[...]).astype(HALF)
    for half in range(HALVES):
        span = pl.ds(half * count, count)
        back = triple_back.at[:, span]

        def put(rows, pair, part, value, back=back):
            back[part, rows, columns(pair)] = value

        attend_backward(triples[half], weights[half], mixed_back.at[span], put, count // window, window)
    normed_back = jnp.zeros_like(middle_back)
    for part in range(3):
        back = triple_back[part]
        normed_back = normed_back + dot_right(back, entry[:, part * D : (part + 1) * D])
        add(part, normed, back)
    sums[GAIN] += column_sum(normed_back * unit)
    sums[OFFSET] += column_sum(normed_back)
    rows_back = (middle_back + norm_back(normed_back * gain[...], unit, inverse)).astype(HALF)
    for half in range(HALVES):
        delta[:, half * each : (half + 1) * each] = rows_back[half * count : (half + 1) * count].reshape(
            -1, each, window, D
        )

    @pl.when(step == pl.num_programs(0) - 1)
    def _():
        pick(place[4], away, own, [held[tile].astype(HALF) for tile in range(4)])

    for piece in range(pieces):

        @pl.when(step == piece)
        def _(piece=piece):
            for copy in results(piece):
                copy.wait()


def attention_back(place, frames, params, came, triple, weights, mixed, middles_back, batch, after):
    pieces = len(came[0])
    per_group, windows, window, _ = frames.shape
    block = (per_group, windows // pieces, window, D)
    rows = per_group * block[1] * window // HALVES
    cut = pl.BlockSpec(block, lambda i, place: (0, place[0] ^ i, 0, 0))
    attended = (rows // window, PAIRS, window, 2 * window)
    halves = range(HALVES)
    spread_out = lambda half: lambda i, place: jnp.where(i < 2, 2 * i + half, i + (pieces if half else 2))
    ins = [(frames, cut)] + plain(params[:2]) + anywhere([params[3], params[2]])
    ins += [(array, pl.BlockSpec(memory_space=pl.ANY)) for half in came for array in half]
    ins += [(triple, row_spec(rows, 3 * D, lambda i, place, h=h: h * pieces + i)) for h in halves]
    ins += [
        (weights, pl.BlockSpec(attended, lambda i, place, h=h: (h * pieces + i, 0, 0, 0))) for h in halves
    ]
    ins += [(mixed, row_spec(rows, D, lambda i, place, h=h: h * pieces + i)) for h in halves]
    ins += [(middles_back, row_spec(rows, D, spread_out(h))) for h in halves]
    tiles = (2, batch, D // batch, CHUNK)
    count = rows * pieces * HALVES
    return run(
        functools.partial(attention_back_body, window=window, pieces=pieces),
        "attention_back",
        (pieces,),
        [place],
        ins,
        [
            (frames.shape, HALF, cut),
            (frames.shape, HALF, cut),
            *[(tiles, HALF, whole(tiles))] * 2,
            ((SUMS, 1, D), FLOAT, whole((SUMS, 1, D))),
        ],
        scratch=[
            pltpu.VMEM((rows * HALVES, D), HALF),
            pltpu.VMEM((3, rows * HALVES, D), HALF),
            pltpu.VMEM((4, CHUNK, CHUNK), FLOAT),
            pltpu.SemaphoreType.DMA((HALVES,)),
            *buffers_of([params[3], params[2]]),
        ],
        after=after,
        flops=16 * count * D * D,
        moved=count * D * 2 * (3 + 1 + 1 + 2 + 2 + 4),
    )


def swap(value, axis, mask):
    size = lax.axis_size(axis)
    if mask == 0:
        return value
    return lax.ppermute(value, axis, [(i, i ^ mask) for i in range(size)])


def move(value, batch_mask, win_mask):
    if batch_mask == 0:
        return swap(value, "win", win_mask)
    if win_mask == 0:
        return swap(value, "batch", batch_mask)
    batch, win = lax.axis_size("batch"), lax.axis_size("win")
    pairs = [
        (b * win + w, (b ^ batch_mask) * win + (w ^ win_mask)) for b in range(batch) for w in range(win)
    ]
    return lax.ppermute(value, ("batch", "win"), pairs)


def exchange(arrays):
    made = {k: swap(arrays[k], "win", k) for k in reversed(range(len(arrays)))}
    return [made[k] for k in range(len(arrays))]


def split_body(place, *refs, groups, alone, across):
    own, got, outs = refs[:groups], refs[groups : 2 * groups - alone], refs[2 * groups - alone :]
    got = [*got, *[None] * alone]
    column, row = place[1], place[2]
    width = CHUNK // across
    at = 0
    for one, two in zip(own, got):
        rows = one.shape[3]
        for tile in range(one.shape[0]):
            for piece, out in enumerate(outs):
                y = row ^ (piece % 2)
                x = pl.ds(pl.multiple_of((column ^ (piece // 2)) * width, width), width)
                total = one[tile, :, y, :, x]
                if two is not None:
                    total = (total.astype(FLOAT) + two[tile, :, y, :, x].astype(FLOAT)).astype(HALF)
                out[:, at : at + rows] = total
            at += rows


def total_of(refs, index):
    total = refs[0][index].astype(FLOAT)
    for ref in refs[1:]:
        total = total + ref[index].astype(FLOAT)
    return total.astype(HALF)


def merge_body(place, *refs, inputs):
    ins, outs = refs[:inputs], refs[inputs:]
    for piece, out in enumerate(outs):
        out[...] = total_of(ins, place[3] ^ piece)


def pair_body(place, *refs, inputs, bit):
    ins, outs = refs[:inputs], refs[inputs:]
    mine = (place[3] >> bit) & 1
    for side, out in zip((mine, 1 - mine), outs):
        out[...] = total_of(ins, (slice(None), side))


def last_body(*refs, sets):
    ins, out = refs[:-1], refs[-1]
    at, start = 0, 0
    for size in sets:
        rows, width = ins[at].shape[-2:]
        made = [ref.reshape(rows, width) for ref in ins[at : at + size]]
        out[start : start + rows] = total_of(made, slice(None))
        at += size
        start += rows


def unpack_body(place, *refs, pieces, across, layout):
    ins, outs, held = refs[:pieces], refs[pieces:-1], refs[-1]
    width = CHUNK // across
    for piece, ref in enumerate(ins):
        x = pl.ds(pl.multiple_of((place[1] ^ (piece // 2)) * width, width), width)
        held[place[4] ^ (piece % 2), :, x] = ref[...].astype(FLOAT)
    for out, places in zip(outs, layout):
        for core, start, rows, left, wide, row, column in places:
            here = (slice(start, start + rows), slice(left, left + wide))
            value = held[(0, *here)] + held[(1, *here)] if core is None else held[(core, *here)]
            out[row : row + rows, column : column + wide] = value


def arrived_body(*refs):
    refs[-1][...] = jnp.zeros_like(refs[-1])


def arrived(arrays):
    shape = (8, 128)
    outs = [(shape, FLOAT, whole(shape))]
    return run(
        arrived_body, "arrived", (1,), [], [], outs, after=arrays, flops=8 * 10**9, vmem=SMALL_VMEM
    )


class Reduction:
    def __init__(self, place, away, own, alone=()):
        self.place = place
        self.batch, self.win = lax.axis_size("batch"), lax.axis_size("win")
        self.across, self.depth = self.win // 2, self.batch // 2
        cut = lambda a: a.reshape(-1, self.depth, 2, *a.shape[2:])
        self.own = [cut(a) for a in (*own, *alone)]
        self.alone = len(alone)
        self.got = [swap(cut(a), "win", 1) for a in away]
        self.rows = sum(a.shape[0] * a.shape[3] for a in self.own)
        self.width = CHUNK // self.across
        self.vmem = VMEM

    def cores(self, after=()):
        shape = (self.depth, self.rows, self.width)
        pieces = run(
            functools.partial(split_body, groups=len(self.own), alone=self.alone, across=self.across),
            "sum_cores",
            (1,),
            [self.place],
            plain(self.own + self.got),
            [(shape, HALF, whole(shape))] * (2 * self.across),
            after=after,
            vmem=self.vmem,
            flops=SMALL_FLOPS,
        )
        self.mark = pieces[:1]
        self.pieces = [move(a, number % 2, 2 * (number // 2)) for number, a in enumerate(pieces)]

    def chips(self, after=(), flops=SMALL_FLOPS):
        shape = (self.rows, self.width)
        pieces = run(
            functools.partial(merge_body, inputs=len(self.pieces)),
            "sum_chips",
            (1,),
            [self.place],
            plain(self.pieces),
            [(shape, HALF, whole(shape))] * self.depth,
            after=after,
            vmem=self.vmem,
            flops=flops,
        )
        self.mark = pieces[:1]
        self.pieces = [swap(a, "batch", 2 * number) for number, a in enumerate(pieces)]

    def pair(self, bit, after=(), flops=SMALL_FLOPS):
        depth, rows, width = self.pieces[0].shape
        shape = (depth // 2, rows, width)
        kept, away = run(
            functools.partial(pair_body, inputs=len(self.pieces), bit=bit),
            "sum_pairs",
            (1,),
            [self.place],
            plain([a.reshape(depth // 2, 2, rows, width) for a in self.pieces]),
            [(shape, HALF, whole(shape))] * 2,
            after=after,
            vmem=self.vmem,
            flops=flops,
        )
        self.mark = [kept]
        self.pieces = [kept, swap(away, "batch", 2 << bit)]

    def last(self, after=(), other=None, flops=SMALL_FLOPS):
        groups = [self] if other is None else [other, self]
        self.rows = sum(group.rows for group in groups)
        shape = (self.rows, self.width)
        (total,) = run(
            functools.partial(last_body, sets=[len(group.pieces) for group in groups]),
            "sum_last",
            (1,),
            [],
            plain([a for group in groups for a in group.pieces]),
            [(shape, HALF, whole(shape))],
            after=after,
            vmem=self.vmem,
            flops=flops,
        )
        self.mark = [total]
        across = [swap(total, "win", 2 * number) for number in range(self.across)]
        self.pieces = [a if side == 0 else swap(a, "win", 1) for a in across for side in range(2)]

    def unpack(self, layout, shapes, after=()):
        return run(
            functools.partial(
                unpack_body, pieces=self.win, across=self.across, layout=layout
            ),
            "unpack",
            (1,),
            [self.place],
            plain(self.pieces),
            [(s, FLOAT, whole(s)) for s in shapes],
            scratch=[pltpu.VMEM((2, self.rows, CHUNK), FLOAT)],
            after=after,
            vmem=self.vmem,
            flops=SMALL_FLOPS,
        )


SMALL_ROWS = 16


def small_body(*refs, blocks):
    out = refs[-1]
    sums, at = [], 0
    for size in blocks:
        sums.append(total_in(refs[at : at + size]))
        at += size
    _, batch, _, width = out.shape
    rows = D // batch
    wide = lambda parts: jnp.concatenate(
        [*parts, jnp.zeros((1, width - sum(p.shape[1] for p in parts)), FLOAT)], axis=1
    )
    for shard in range(batch):
        made = []
        for total in sums:
            made.append(wide([total[n][:, shard * rows : (shard + 1) * rows] for n in range(6)]))
        for total in sums:
            chunk, start = divmod(shard * 4 * rows, CHUNK)
            made.append(wide([total[LIFT + chunk][:, start : start + 4 * rows]]))
        made.append(jnp.zeros((SMALL_ROWS - len(made), width), FLOAT))
        out[0, shard] = jnp.concatenate(made, axis=0).astype(HALF)


def total_in(refs):
    total = refs[0][...]
    for ref in refs[1:]:
        total = total + ref[...]
    return total


def small_tiles(blocks, batch):
    shape = (1, batch, SMALL_ROWS, CHUNK)
    (out,) = run(
        functools.partial(small_body, blocks=[len(sums) for sums in blocks]),
        "small_tiles",
        (1,),
        [],
        plain([a for sums in blocks for a in sums]),
        [(shape, HALF, whole(shape))],
        vmem=SMALL_VMEM,
    )
    return out


def attend_places(rows, start):
    spot = lambda tile: (tile // 2, start + tile % 2 * rows, rows, 0, CHUNK)
    return [
        [(*spot(part), 0, part * CHUNK) for part in range(3)],
        [(*spot(3), 0, 0)],
    ], [(rows, 3 * D), (rows, D)]


def feed_places(rows, start):
    narrows = [(sub // 2, start + sub % 2 * rows, rows, 0, CHUNK, sub * rows, 0) for sub in range(4)]
    start += 2 * rows
    widens = [
        (chunk // 2, start + chunk % 2 * rows, rows, 0, CHUNK, 0, chunk * CHUNK) for chunk in range(CHUNKS)
    ]
    return [widens, narrows], [(rows, FF), (4 * rows, D)]


def small_places(rows, start):
    layout, shapes = [], []
    for block in range(2):
        layout += [[(None, start + block, 1, number * rows, rows, 0, 0)] for number in range(6)]
        layout.append([(None, start + 2 + block, 1, 0, 4 * rows, 0, 0)])
        shapes += [(1, rows)] * 6 + [(1, 4 * rows)]
    return layout, shapes


def local(*args):
    frames, cotangent, video_frames = args[0], args[23], args[24]
    space = [a.reshape(1, -1) if a.ndim == 1 else a for a in args[1:12]]
    time = [a.reshape(1, -1) if a.ndim == 1 else a for a in args[12:23]]
    batch, win = lax.axis_size("batch"), lax.axis_size("win")
    here, group = lax.axis_index("win"), lax.axis_index("batch")
    core = here % 2
    place = jnp.stack([here, here // 2, group % 2, group // 2, core]).astype(jnp.int32)
    _, per_group, _, windows, window, _ = frames.shape
    shape = (per_group, windows, window, D)
    rows_in, cotangent = frames.reshape(shape), cotangent.reshape(shape)
    rows = D // batch

    kept, came = [], []
    for half in range(HALVES):
        sent, kept = space_forward(place, rows_in, cotangent, space, half, win, kept)
        came.append(exchange(sent))
    triple, weights, mixed, middles, hiddens = kept
    backs, time_sums, tiles = [], [], [None]
    for half in range(HALVES):
        sent, tiles, sums = time_block(place, video_frames, came[half], time, batch, *tiles)
        backs.append(exchange(sent))
        time_sums.append(sums)

    bits = (batch // 2).bit_length() - 1
    time_sum = Reduction(place, tiles[:1], tiles[1:])
    time_sum.cores(arrived(backs[0][1:]))
    *fed, first_sums = feed_back(place, space, backs, middles, hiddens, batch, after=time_sum.mark)
    middles_back, away, own, feed_sums = feed_back(place, space, backs, middles, hiddens, batch, fed)
    feed_sum = Reduction(place, [away], [own])
    time_sum.pair(0, [feed_sums], LONG_FLOPS)
    feed_sum.cores(time_sum.mark)
    delta, outcome, away, own, attend_sums = attention_back(
        place, rows_in, space, backs, triple, weights, mixed, middles_back, batch, feed_sum.mark
    )
    time_sum.vmem = feed_sum.vmem = SMALL_VMEM
    small = small_tiles([[first_sums, feed_sums, attend_sums], time_sums], batch)
    attend_sum = Reduction(place, [away], [own], [small])
    attend_sum.vmem = SMALL_VMEM
    mark = [attend_sums]
    for bit in range(1, bits):
        time_sum.pair(bit, mark, 0)
        mark = time_sum.mark
    feed_sum.pair(0, mark, LONG_FLOPS)
    attend_sum.cores(feed_sum.mark)
    mark = attend_sum.mark
    for bit in range(1, bits):
        feed_sum.pair(bit, mark)
        mark = feed_sum.mark
    time_rows = time_sum.rows
    attend_sum.chips(mark)
    feed_sum.last(attend_sum.mark, time_sum, 0)
    attend_sum.last(feed_sum.mark)
    feed_layout, feed_shapes = feed_places(rows, 0)
    attend_layout, attend_shapes = attend_places(rows, 4 * rows)
    last_layout, last_shapes = feed_places(rows, time_rows)
    made = feed_sum.unpack(
        feed_layout + attend_layout + last_layout,
        feed_shapes + attend_shapes + last_shapes,
        attend_sum.mark,
    )
    time_grads, feed_grads = made[:4], made[4:]
    attend_layout, attend_shapes = attend_places(rows, 0)
    small_layout, small_shapes = small_places(rows, 2 * rows)
    attend_grads = attend_sum.unpack(attend_layout + small_layout, attend_shapes + small_shapes)
    smalls = [a.reshape(-1) for a in attend_grads[2:]]

    def collected(grads, smalls):
        widen, narrow, entry, leave = grads
        gain, offset, bias, weigh, shift, nudge, lift = smalls
        return gain, offset, entry, leave, bias, weigh, shift, widen, lift, narrow, nudge

    return (
        outcome.reshape(frames.shape),
        delta.reshape(frames.shape),
        *collected([*feed_grads, *attend_grads[:2]], smalls[:7]),
        *collected(time_grads, smalls[7:]),
    )


def solution(mesh):
    rows = P("batch", None, "win", None, None, None)
    one, two = P("batch"), P("batch", None)
    grads = (one, one, two, two, one, one, one, two, one, two, one)
    return jax.shard_map(
        local,
        mesh=mesh,
        in_specs=(rows, *([P()] * 22), rows, P("batch", None)),
        out_specs=(rows, rows, *grads, *grads),
        check_vma=False,
    )
```
